32 devices in a mesh: leaf: 4 (over x, core), dof: 4 (over z), blk: 2 (over y).
Axes of the slice: x: 2, y: 2, z: 4, core: 2. Of those that a mesh axis runs over, the one named last changes fastest.
Arguments:
- modes: bfloat16 [4, 128, 128, 16, 128], P('leaf', 'blk', 'dof'), may hold values from -1.5 to 1.5
- stiffness: float32 [4, 128, 16, 128], P('leaf', 'dof'), may hold values from 0.25 to 2
- density: float32 [4, 128, 16, 128], P('leaf', 'dof'), may hold values from 0.5 to 4
- eigen_blocks: bfloat16 [4, 128, 128], P('leaf', None, 'blk'), may hold values from -0.5 to 0.5
- parent: int32 [4], replicated, may hold values from 0 to 1
Outputs:
- node_stiffness: float32 [2, 128, 128], P(None, 'blk')
- root_stiffness: float32 [128, 128], P('blk')
- leaf_vectors: bfloat16 [4, 128, 128, 16, 128], P('leaf', 'blk', 'dof')
The draws below stay inside these ranges and needn't reach their ends.
All inputs are finite; a program needn't handle non-finite values.
Results may differ from the reference program's by a relative error of at most 0.0035.
Values may be sent and summed in bfloat16 or wider, within the bound.
No kernel may reach another device: no remote copies, remote signals or barrier semaphores. Data moves between devices by JAX's collectives and lax.ppermute only.
A program may use at most 128 MiB of HBM per device.

```python
import math
import jax
import jax.numpy as jnp
from jax import lax

MODES = 128
EIGS = 128
CY = 16
CZ = 128
LEAVES = 4
NODES = 2
NXL = 128


def draw_parent(key, part):
    base = jax.random.fold_in(key, 9173)
    first, second = jax.random.split(base)
    covered = jnp.arange(NODES, dtype=jnp.int32)
    others = jax.random.randint(first, (LEAVES - NODES,), 0, NODES, dtype=jnp.int32)
    labels = jnp.concatenate([covered, others])
    return jax.random.permutation(second, labels).astype(jnp.int32)


def draw_modes(key, part):
    base = jax.random.fold_in(key, 4411)
    keys = jax.random.split(base, 4)
    waves = jax.random.uniform(keys[0], (3, LEAVES, MODES), jnp.float32, 0.02, 0.25)
    phases = jax.random.uniform(keys[1], (3, LEAVES, MODES), jnp.float32, -math.pi, math.pi)
    x_cells = jnp.arange(NXL, dtype=jnp.float32)
    y_cells = jnp.arange(CY, dtype=jnp.float32)
    z_cells = jnp.arange(CZ, dtype=jnp.float32)
    along_x = jnp.cos(waves[0][:, :, None] * x_cells[None, None, :] + phases[0][:, :, None])
    along_y = jnp.cos(waves[1][:, :, None] * y_cells[None, None, :] + phases[1][:, :, None])
    along_z = jnp.cos(waves[2][:, :, None] * z_cells[None, None, :] + phases[2][:, :, None])
    smooth = along_x[:, :, :, None, None] * along_y[:, :, None, :, None] * along_z[:, :, None, None, :]
    shape = (LEAVES, MODES, NXL, CY, CZ)
    noise = 0.1 * jnp.clip(jax.random.normal(keys[3], shape, jnp.float32), -5.0, 5.0)
    field = smooth + noise
    return field.astype(jnp.bfloat16)


def level_of(stream_key, extent, pieces, least, high):
    def one(dim, parts):
        draws = jax.random.uniform(jax.random.fold_in(jax.random.fold_in(stream_key, 6), dim), (parts,), jnp.float32, least / len(pieces), high / len(pieces))
        return jnp.repeat(jnp.exp(draws), extent[dim] // parts).reshape((-1,) + (1,) * (len(extent) - dim - 1))

    level = one(*pieces[0])
    for cut in pieces[1:]:
        level = level * one(*cut)
    return level


def scatter_about(key, dims, spread, limit, cuts=(), kind=jnp.bfloat16):
    array = jax.random.normal(key, dims, jnp.float32) * spread
    if len(cuts) > 0:
        array = level_of(key, dims, cuts, -0.22, 0.18) * array
    return jnp.clip(array, min=-limit, max=limit).astype(kind)


def setup_inputs(seed: int = 0) -> dict:
    key_of = jax.random.split(jax.random.key(seed), 6)
    modes = draw_modes(jax.random.fold_in(key_of[5], 71), 0)
    stiffness = jnp.clip(0.25 + 1.75 * jax.random.uniform(key_of[1], (LEAVES, NXL, CY, CZ), jnp.float32) ** level_of(key_of[1], (LEAVES, NXL, CY, CZ), ((0, 4), (1, 4)), -0.2, 0.2), 0.25, 2.0)
    density = jnp.clip(jnp.exp(math.log(4.0) - 2.0794415 * jax.random.uniform(key_of[2], (LEAVES, NXL, CY, CZ), jnp.float32) ** level_of(key_of[2], (LEAVES, NXL, CY, CZ), ((0, 4), (1, 4)), -0.2, 0.2)), 0.5, 4.0)
    eigen_blocks = scatter_about(key_of[3], (LEAVES, MODES, EIGS), MODES ** -0.5, 0.5, ((0, 4), (2, 2)))
    parent = draw_parent(jax.random.fold_in(key_of[5], 71), 0)
    return {"modes": modes, "stiffness": stiffness, "density": density, "eigen_blocks": eigen_blocks, "parent": parent}


def neighbours(padded):
    inner = padded[:, 1:-1]
    sides = jnp.pad(inner, ((0, 0), (0, 0), (1, 1), (1, 1)))
    total = padded[:, 2:] + padded[:, :-2]
    total = total + sides[:, :, 2:, 1:-1] + sides[:, :, :-2, 1:-1]
    total = total + sides[:, :, 1:-1, 2:] + sides[:, :, 1:-1, :-2]
    return total

def leaf_terms(items):
    phi, coefs, masses, blocks = items
    field = phi.astype(jnp.float32)
    padded = jnp.pad(field, ((0, 0), (1, 1), (0, 0), (0, 0)))
    stiff = ((6.0 + coefs) * field - neighbours(padded)).astype(jnp.bfloat16)
    flat = phi.reshape(MODES, -1)
    reduced = lax.dot_general(stiff.reshape(MODES, -1), flat, (((1,), (1,)), ((), ())), preferred_element_type=jnp.float32)
    weighed = lax.optimization_barrier((masses * field).astype(jnp.bfloat16))
    diagonal = lax.optimization_barrier(jnp.sum(weighed.reshape(MODES, -1).astype(jnp.float32) * flat.astype(jnp.float32), axis=1))
    vectors = lax.dot_general(blocks, flat, (((0,), (0,)), ((), ())), preferred_element_type=jnp.float32)
    vectors = vectors.astype(jnp.bfloat16).reshape(EIGS, NXL, CY, CZ)
    return (reduced, diagonal, vectors)

def reference(modes, stiffness, density, eigen_blocks, parent):
    reduced, diagonal, vectors = lax.map(leaf_terms, (modes, stiffness, density, eigen_blocks))
    onehot = (parent[:, None] == jnp.arange(NODES, dtype=jnp.int32)[None, :]).astype(jnp.float32)
    node_stiffness = jnp.einsum('lp,lij->pij', onehot, reduced, precision=lax.Precision.HIGHEST)
    node_mass = jnp.einsum('lp,li->pi', onehot, diagonal, precision=lax.Precision.HIGHEST)
    scale = 1.0 / jnp.sqrt(node_mass)
    root_stiffness = lax.optimization_barrier(jnp.sum(scale[:, :, None] * node_stiffness * scale[:, None, :], axis=0))
    return (node_stiffness, root_stiffness, vectors)
```

```python
import functools
import jax
import jax.numpy as jnp
from jax import lax
from jax.experimental import pallas as pl
from jax.experimental.pallas import tpu as pltpu
from jax.sharding import PartitionSpec as P

SUB = 8
VMEM_BYTES = 32 * 1024 * 1024


def params(steps):
    return pltpu.CompilerParams(
        dimension_semantics=("arbitrary",), vmem_limit_bytes=VMEM_BYTES
    )


def split_rows(x):
    wide = x.astype(jnp.float32)
    rows, cells_y, cells_z = wide.shape
    parts = [
        wide[:, i * SUB : (i + 1) * SUB].reshape(rows * SUB, cells_z).astype(jnp.bfloat16)
        for i in range(cells_y // SUB)
    ]
    return jnp.concatenate(parts, axis=1)


def accumulate(total, left, right):
    total[...] += lax.dot_general(
        left, right, (((1,), (1,)), ((), ())), preferred_element_type=jnp.float32
    )


def same_row_sum(total):
    tall, wide = total.shape
    row = lax.broadcasted_iota(jnp.int32, (tall, wide), 0) % SUB
    col = lax.broadcasted_iota(jnp.int32, (tall, wide), 1) % SUB
    kept = jnp.where(row == col, total, 0.0).reshape(tall // SUB, SUB, wide)
    folded = jnp.sum(kept, axis=1)
    group = lax.broadcasted_iota(jnp.int32, (wide, wide // SUB), 0) // SUB
    pick = (group == lax.broadcasted_iota(jnp.int32, (wide, wide // SUB), 1)).astype(jnp.float32)
    return jnp.dot(folded, pick, precision=lax.Precision.HIGHEST, preferred_element_type=jnp.float32)


def stiff_kernel(own, prev, after, low, high, coefs, masses, stiff, gram, mass, total, flat, acc):
    layer, last = pl.program_id(0), pl.num_programs(0) - 1
    rows, _, cells_y, cells_z = own.shape

    @pl.when(layer == 0)
    def _():
        total[...] = jnp.zeros_like(total)
        acc[...] = jnp.zeros_like(acc)

    y = lax.broadcasted_iota(jnp.int32, (SUB, cells_y, cells_z), 1)
    z = lax.broadcasted_iota(jnp.int32, (SUB, cells_y, cells_z), 2)
    diagonal = 6.0 + coefs[0]
    density = masses[0]

    def group(g, carry):
        modes = pl.ds(g * SUB, SUB)
        field = own[modes, 0].astype(jnp.float32)
        before = jnp.where(layer == 0, low[modes, 0], prev[modes, 0]).astype(jnp.float32)
        behind = jnp.where(layer == last, high[modes, 0], after[modes, 0]).astype(jnp.float32)
        around = before + behind
        around += jnp.where(y == 0, 0.0, pltpu.roll(field, 1, 1))
        around += jnp.where(y == cells_y - 1, 0.0, pltpu.roll(field, cells_y - 1, 1))
        around += jnp.where(z == 0, 0.0, pltpu.roll(field, 1, 2))
        around += jnp.where(z == cells_z - 1, 0.0, pltpu.roll(field, cells_z - 1, 2))
        force = diagonal[None] * field - around
        weighed = (density[None] * field).astype(jnp.bfloat16).astype(jnp.float32) * field
        out = pl.ds(g * SUB * SUB, SUB * SUB)
        part = None
        for i in range(cells_y // SUB):
            rows_y, lanes = slice(i * SUB, (i + 1) * SUB), slice(i * cells_z, (i + 1) * cells_z)
            stiff[0, out, lanes] = force[:, rows_y].reshape(SUB * SUB, cells_z).astype(jnp.bfloat16)
            flat[out, lanes] = field[:, rows_y].reshape(SUB * SUB, cells_z).astype(jnp.bfloat16)
            part = weighed[:, rows_y] if part is None else part + weighed[:, rows_y]
        acc[modes] += part
        return carry

    lax.fori_loop(0, rows // SUB, group, 0)
    accumulate(total, stiff[0], flat[...])

    @pl.when(layer == last)
    def _():
        gram[...] = same_row_sum(total[...])
        mass[...] = jnp.broadcast_to(
            jnp.sum(jnp.sum(acc[...], axis=1), axis=1, keepdims=True), mass.shape
        )


def stiff_terms(own, low, high, coefs, masses):
    rows, layers, cells_y, cells_z = own.shape
    tall, wide = rows * SUB, cells_y // SUB * cells_z
    block = (rows, 1, cells_y, cells_z)
    cells = (1, cells_y, cells_z)
    return pl.pallas_call(
        stiff_kernel,
        grid=(layers,),
        in_specs=[
            pl.BlockSpec(block, lambda g: (0, g, 0, 0)),
            pl.BlockSpec(block, lambda g: (0, jnp.maximum(g - 1, 0), 0, 0)),
            pl.BlockSpec(block, lambda g: (0, jnp.minimum(g + 1, layers - 1), 0, 0)),
            pl.BlockSpec(block, lambda g: (0, 0, 0, 0)),
            pl.BlockSpec(block, lambda g: (0, 0, 0, 0)),
            pl.BlockSpec(cells, lambda g: (g, 0, 0)),
            pl.BlockSpec(cells, lambda g: (g, 0, 0)),
        ],
        out_specs=[
            pl.BlockSpec((1, tall, wide), lambda g: (g, 0, 0)),
            pl.BlockSpec((rows, rows), lambda g: (0, 0)),
            pl.BlockSpec((rows, rows), lambda g: (0, 0)),
        ],
        out_shape=[
            jax.ShapeDtypeStruct((layers, tall, wide), jnp.bfloat16),
            jax.ShapeDtypeStruct((rows, rows), jnp.float32),
            jax.ShapeDtypeStruct((rows, rows), jnp.float32),
        ],
        scratch_shapes=[
            pltpu.VMEM((tall, tall), jnp.float32),
            pltpu.VMEM((tall, wide), jnp.bfloat16),
            pltpu.VMEM((rows, SUB, cells_z), jnp.float32),
        ],
        compiler_params=params(layers),
        cost_estimate=pl.CostEstimate(
            flops=2 * layers * tall * tall * wide, bytes_accessed=8 * own.size, transcendentals=0
        ),
        name="stiff_terms",
    )(own, own, own, low, high, coefs, masses)


def cross_kernel(at, stiff, other, gram, total):
    step = pl.program_id(0)

    @pl.when(step == 0)
    def _():
        total[...] = jnp.zeros_like(total)

    accumulate(total, stiff[0], split_rows(other[:, 0]))

    @pl.when(step == pl.num_programs(0) - 1)
    def _():
        gram[...] = same_row_sum(total[...])


def cross_terms(stiff, other, at):
    rows, layers, cells_y, cells_z = other.shape
    _, tall, wide = stiff.shape
    return pl.pallas_call(
        cross_kernel,
        grid_spec=pltpu.PrefetchScalarGridSpec(
            num_scalar_prefetch=1,
            grid=(layers,),
            in_specs=[
                pl.BlockSpec((1, tall, wide), lambda g, at: (at[0] + g, 0, 0)),
                pl.BlockSpec((rows, 1, cells_y, cells_z), lambda g, at: (0, g, 0, 0)),
            ],
            out_specs=pl.BlockSpec((rows, rows), lambda g, at: (0, 0)),
            scratch_shapes=[pltpu.VMEM((tall, tall), jnp.float32)],
        ),
        out_shape=jax.ShapeDtypeStruct((rows, rows), jnp.float32),
        compiler_params=params(layers),
        cost_estimate=pl.CostEstimate(
            flops=2 * layers * tall * tall * wide, bytes_accessed=4 * other.size, transcendentals=0
        ),
        name="cross_terms",
    )(at.reshape(1), stiff, other)


def vector_kernel(at, spread, own, other, *rest):
    out = rest[-1]
    rows, _, cells_y, cells_z = own.shape
    both = jnp.concatenate([split_rows(own[:, 0]), split_rows(other[:, 0])], axis=0)
    made = jnp.dot(spread[...], both, preferred_element_type=jnp.float32)
    eigs = out.shape[0]
    parts = [
        made[:, i * cells_z : (i + 1) * cells_z].reshape(eigs, SUB, cells_z)
        for i in range(cells_y // SUB)
    ]
    out[:, 0] = jnp.concatenate(parts, axis=1).astype(out.dtype)


def expand(spread, own, other, at, held):
    rows, layers, cells_y, cells_z = other.shape
    eigs = spread.shape[0] // SUB
    inputs = [at.reshape(1), spread, own, other]
    specs = [
        pl.BlockSpec(spread.shape, lambda g, at: (0, 0)),
        pl.BlockSpec((rows, 1, cells_y, cells_z), lambda g, at: (0, at[0] + g, 0, 0)),
        pl.BlockSpec((rows, 1, cells_y, cells_z), lambda g, at: (0, g, 0, 0)),
    ]
    aliases = {}
    if held is not None:
        aliases = {len(inputs): 0}
        inputs.append(held)
        specs.append(pl.BlockSpec(memory_space=pl.ANY))
    return pl.pallas_call(
        vector_kernel,
        grid_spec=pltpu.PrefetchScalarGridSpec(
            num_scalar_prefetch=1,
            grid=(layers,),
            in_specs=specs,
            out_specs=pl.BlockSpec((eigs, 1, cells_y, cells_z), lambda g, at: (0, at[0] + g, 0, 0)),
        ),
        out_shape=jax.ShapeDtypeStruct((eigs,) + own.shape[1:], jnp.bfloat16),
        input_output_aliases=aliases,
        compiler_params=params(layers),
        cost_estimate=pl.CostEstimate(
            flops=2 * layers * spread.shape[0] * spread.shape[1] * cells_y // SUB * cells_z,
            bytes_accessed=6 * other.size,
            transcendentals=0,
        ),
        name="expand",
    )(*inputs)


def tied(x, y):
    return lax.optimization_barrier((x, y))[0]


def swap(x):
    return lax.ppermute(x, "blk", [(0, 1), (1, 0)])


def paired_sum(x, axis):
    size, step = lax.axis_size(axis), 1
    while step < size:
        x = x + lax.ppermute(x, axis, [(i, i ^ step) for i in range(size)])
        step *= 2
    return x


def line_sum(x, axis):
    x = x + lax.ppermute(x, axis, [(0, 1), (1, 0), (2, 3), (3, 2)])
    x = x + lax.ppermute(x, axis, [(1, 2), (2, 1)])
    outer = lax.ppermute(x, axis, [(1, 0), (2, 3)])
    place = lax.axis_index(axis)
    return jnp.where((place == 0) | (place == 3), outer, x)


def halved(modes, stiffness, density, eigen_blocks, parent):
    own = modes[0]
    rows, layers = own.shape[:2]
    half = layers // 2
    blk, dof, leaf = lax.axis_index("blk"), lax.axis_index("dof"), lax.axis_index("leaf")
    upper = (blk + dof) % 2

    def start(mine, offset, count, top):
        forward = top == 1 if mine else top == 0
        return jnp.where(forward, half + offset, half - offset - count).astype(jnp.int32)

    def send(mine, offset, count, after=None):
        source = own if after is None else tied(own, after)
        at = start(mine, offset, count, 1 - upper)
        return swap(lax.dynamic_slice_in_dim(source, at, count, axis=1))

    def place(mine, offset, count):
        return start(mine, offset, count, upper)

    near, far = half * 3 // 16, half - half * 3 // 16
    rest = [half * 5 // 16, half * 5 // 16, half * 3 // 16]
    rest.append(half - 1 - sum(rest))
    spots = [1, 1 + rest[0], 1 + rest[0] + rest[1], 1 + sum(rest[:3])]

    edge = send(False, 0, 1)
    first = send(True, 0, near)
    size = lax.axis_size("dof")
    low = lax.ppermute(own[:, -1:], "dof", [(i, i + 1) for i in range(size - 1)])
    high = lax.ppermute(own[:, :1], "dof", [(i + 1, i) for i in range(size - 1)])
    second = send(True, near, far, edge)
    stiff, gram, mass = stiff_terms(own, low, high, stiffness[0], density[0])

    blocks = tied(eigen_blocks[0], mass)
    mine = lax.dynamic_slice_in_dim(blocks, blk * rows, rows, 0)
    other = lax.dynamic_slice_in_dim(blocks, (1 - blk) * rows, rows, 0)
    ordered = jnp.concatenate([mine, other], axis=0).T
    eye = jnp.eye(SUB, dtype=ordered.dtype)
    spread = (ordered[:, None, :, None] * eye[None, :, None, :]).reshape(
        ordered.shape[0] * SUB, ordered.shape[1] * SUB
    )

    third = send(False, spots[0], rest[0], first)
    inner, outer = place(True, 0, 1), place(False, 0, 1)
    own_in = lax.dynamic_slice_in_dim(own, inner, 1, axis=1)
    own_out = lax.dynamic_slice_in_dim(own, outer, 1, axis=1)
    first_in = lax.dynamic_slice_in_dim(first, inner - place(True, 0, near), 1, axis=1)
    across = functools.partial(
        lax.dot_general,
        dimension_numbers=(((1, 2, 3), (1, 2, 3)), ((), ())),
        preferred_element_type=jnp.float32,
    )
    border = 0.5 * (across(own_out, first_in) - across(own_in, edge))
    cross = cross_terms(stiff, first, place(True, 0, near))
    vectors = expand(spread, own, edge, outer, None)
    vectors = expand(spread, own, first, place(True, 0, near), vectors)
    cross = cross + border + cross_terms(stiff, second, place(True, near, far))

    fourth = send(False, spots[1], rest[1], cross)
    theirs = swap(jnp.concatenate([cross, mass], axis=1))
    vectors = expand(spread, own, second, place(True, near, far), vectors)
    fifth = send(False, spots[2], rest[2], third)
    vectors = expand(spread, own, third, place(False, spots[0], rest[0]), vectors)
    sixth = send(False, spots[3], rest[3], fourth)

    whole = jnp.concatenate([gram, cross + theirs[:, :rows].T, mass, theirs[:, rows:]], axis=1)
    whole = line_sum(whole, "dof")
    nodes = lax.axis_size("leaf") // 2
    belongs = (parent[leaf] == jnp.arange(nodes, dtype=jnp.int32)).astype(jnp.float32)
    whole = paired_sum(belongs[:, None, None] * whole[None], "leaf")
    gram, cross = whole[:, :, :rows], whole[:, :, rows : 2 * rows]
    scale_own = 1.0 / jnp.sqrt(whole[:, :, 2 * rows])
    scale_other = 1.0 / jnp.sqrt(whole[:, :, 3 * rows])

    def in_order(a, b):
        return jnp.where(blk == 0, jnp.concatenate([a, b], -1), jnp.concatenate([b, a], -1))

    node_stiffness = in_order(gram, cross)
    scale = in_order(scale_own, scale_other)
    root_stiffness = jnp.sum(scale_own[:, :, None] * node_stiffness * scale[:, None, :], axis=0)

    vectors = expand(spread, own, fourth, place(False, spots[1], rest[1]), vectors)
    vectors = expand(spread, own, fifth, place(False, spots[2], rest[2]), vectors)
    vectors = expand(spread, own, sixth, place(False, spots[3], rest[3]), vectors)
    return (node_stiffness, root_stiffness, vectors[None])


def extended(x, sides, width):
    for axis, dim in sides:
        size, length = (lax.axis_size(axis), x.shape[dim])
        up = [(i, (i + 1) % size) for i in range(size - 1)]
        down = [(j, i) for i, j in up]
        last = lax.slice_in_dim(x, length - width, length, axis=dim)
        leading = lax.slice_in_dim(x, 0, width, axis=dim)
        before = lax.ppermute(last, axis, up)
        after = lax.ppermute(leading, axis, down)
        x = jnp.concatenate([before, x, after], axis=dim)
    return x


def neighbours(padded):
    inner = padded[:, 1:-1]
    sides = jnp.pad(inner, ((0, 0), (0, 0), (1, 1), (1, 1)))
    total = padded[:, 2:] + padded[:, :-2]
    total = total + sides[:, :, 2:, 1:-1] + sides[:, :, :-2, 1:-1]
    total = total + sides[:, :, 1:-1, 2:] + sides[:, :, 1:-1, :-2]
    return total


def gathered(modes, stiffness, density, eigen_blocks, parent):
    own = modes[0]
    rows, cells_x, cells_y, cells_z = own.shape
    cells = cells_x * cells_y * cells_z
    total_modes = rows * lax.axis_size("blk")
    padded = extended(own, (("dof", 1),), 1).astype(jnp.float32)
    field = padded[:, 1:-1]
    stiff = ((6.0 + stiffness[0]) * field - neighbours(padded)).astype(jnp.bfloat16)
    stiff_flat = stiff.reshape(rows, cells)
    own_flat = own.reshape(rows, cells)
    mass_flat = density[0].reshape(cells)
    weighed_own = (mass_flat[None, :] * own_flat.astype(jnp.float32)).astype(jnp.bfloat16)
    diag_own = jnp.einsum("rc,rc->r", weighed_own, own_flat, preferred_element_type=jnp.float32)
    diagonal = lax.all_gather(diag_own, "blk", axis=0, tiled=True)
    blocks = eigen_blocks[0]
    eig_rows = blocks.shape[1]
    piece = lax.all_gather(own_flat, "blk", axis=0, tiled=True)
    columns = lax.dot_general(
        stiff_flat, piece, (((1,), (1,)), ((), ())), preferred_element_type=jnp.float32
    )
    reduced = columns
    vectors = lax.dot_general(
        blocks, piece, (((0,), (0,)), ((), ())), preferred_element_type=jnp.float32
    )
    reduced, vectors = (reduced, vectors)
    vector_flat = vectors.astype(jnp.bfloat16)
    leaf_vectors = vector_flat.reshape(1, eig_rows, cells_x, cells_y, cells_z)
    leaves = lax.axis_size("leaf")
    nodes = leaves // 2
    node_ids = jnp.arange(nodes, dtype=jnp.int32)
    halves = lax.axis_size("dof")
    gathered_rows, gathered_diag = (
        lax.all_gather(reduced[None], ("leaf", "dof"), axis=0, tiled=True),
        lax.all_gather(diagonal[None], ("leaf", "dof"), axis=0, tiled=True),
    )
    leaf_rows = jnp.sum(gathered_rows.reshape(leaves, halves, rows, total_modes), axis=1)
    leaf_diag = jnp.sum(gathered_diag.reshape(leaves, halves, total_modes), axis=1)
    onehot = (parent[:, None] == node_ids[None, :]).astype(jnp.float32)
    node_stiffness = jnp.einsum("lp,lij->pij", onehot, leaf_rows, precision=lax.Precision.HIGHEST)
    node_mass = jnp.einsum("lp,li->pi", onehot, leaf_diag, precision=lax.Precision.HIGHEST)
    scale = 1.0 / jnp.sqrt(node_mass)
    scale_own = lax.dynamic_slice_in_dim(scale, lax.axis_index("blk") * rows, rows, 1)
    root_stiffness = jnp.sum(scale_own[:, :, None] * node_stiffness * scale[:, None, :], axis=0)
    return (node_stiffness, root_stiffness, leaf_vectors)


def solution(mesh):
    body = gathered
    if mesh.shape["blk"] == 2 and mesh.shape["dof"] == 4:
        body = halved
    in_specs = (
        P("leaf", "blk", "dof", None, None),
        P("leaf", "dof", None, None),
        P("leaf", "dof", None, None),
        P("leaf", None, "blk"),
        P(),
    )
    out_specs = (P(None, "blk", None), P("blk", None), P("leaf", "blk", "dof", None, None))
    return jax.shard_map(body, mesh=mesh, in_specs=in_specs, out_specs=out_specs, check_vma=False)
```

```python
import functools
import jax
import jax.numpy as jnp
from jax import lax
from jax.experimental import pallas as pl
from jax.experimental.pallas import tpu as pltpu
from jax.sharding import PartitionSpec as P

SUB = 8
VMEM_BYTES = 32 * 1024 * 1024
SMALL = pl.CostEstimate(flops=1024, bytes_accessed=1024, transcendentals=0)


def params():
    return pltpu.CompilerParams(
        dimension_semantics=("arbitrary",), vmem_limit_bytes=VMEM_BYTES
    )


def split_rows(x):
    wide = x.astype(jnp.float32)
    rows, cells_y, cells_z = wide.shape
    parts = [
        wide[:, i * SUB : (i + 1) * SUB].reshape(rows * SUB, cells_z).astype(jnp.bfloat16)
        for i in range(cells_y // SUB)
    ]
    return jnp.concatenate(parts, axis=1)


def accumulate(total, left, right):
    total[...] += lax.dot_general(
        left, right, (((1,), (1,)), ((), ())), preferred_element_type=jnp.float32
    )


def same_row_sum(total):
    tall, wide = total.shape
    row = lax.broadcasted_iota(jnp.int32, (tall, wide), 0) % SUB
    col = lax.broadcasted_iota(jnp.int32, (tall, wide), 1) % SUB
    kept = jnp.where(row == col, total, 0.0).reshape(tall // SUB, SUB, wide)
    folded = jnp.sum(kept, axis=1)
    group = lax.broadcasted_iota(jnp.int32, (wide, wide // SUB), 0) // SUB
    pick = (group == lax.broadcasted_iota(jnp.int32, (wide, wide // SUB), 1)).astype(jnp.float32)
    return jnp.dot(folded, pick, precision=lax.Precision.HIGHEST, preferred_element_type=jnp.float32)


def stiff_kernel(own, prev, after, low, high, coefs, masses, stiff, gram, mass, total, flat, acc):
    layer, last = pl.program_id(0), pl.num_programs(0) - 1
    rows, _, cells_y, cells_z = own.shape

    @pl.when(layer == 0)
    def _():
        total[...] = jnp.zeros_like(total)
        acc[...] = jnp.zeros_like(acc)

    y = lax.broadcasted_iota(jnp.int32, (SUB, cells_y, cells_z), 1)
    z = lax.broadcasted_iota(jnp.int32, (SUB, cells_y, cells_z), 2)
    diagonal = 6.0 + coefs[0]
    density = masses[0]

    def group(g, carry):
        modes = pl.ds(g * SUB, SUB)
        field = own[modes, 0].astype(jnp.float32)
        before = jnp.where(layer == 0, low[modes, 0], prev[modes, 0]).astype(jnp.float32)
        behind = jnp.where(layer == last, high[modes, 0], after[modes, 0]).astype(jnp.float32)
        around = before + behind
        around += jnp.where(y == 0, 0.0, pltpu.roll(field, 1, 1))
        around += jnp.where(y == cells_y - 1, 0.0, pltpu.roll(field, cells_y - 1, 1))
        around += jnp.where(z == 0, 0.0, pltpu.roll(field, 1, 2))
        around += jnp.where(z == cells_z - 1, 0.0, pltpu.roll(field, cells_z - 1, 2))
        force = diagonal[None] * field - around
        weighed = (density[None] * field).astype(jnp.bfloat16).astype(jnp.float32) * field
        out = pl.ds(g * SUB * SUB, SUB * SUB)
        part = None
        for i in range(cells_y // SUB):
            rows_y, lanes = slice(i * SUB, (i + 1) * SUB), slice(i * cells_z, (i + 1) * cells_z)
            stiff[0, out, lanes] = force[:, rows_y].reshape(SUB * SUB, cells_z).astype(jnp.bfloat16)
            flat[out, lanes] = field[:, rows_y].reshape(SUB * SUB, cells_z).astype(jnp.bfloat16)
            part = weighed[:, rows_y] if part is None else part + weighed[:, rows_y]
        acc[modes] += part
        return carry

    lax.fori_loop(0, rows // SUB, group, 0)
    accumulate(total, stiff[0], flat[...])

    @pl.when(layer == last)
    def _():
        gram[...] = same_row_sum(total[...])
        mass[...] = jnp.broadcast_to(
            jnp.sum(jnp.sum(acc[...], axis=1), axis=1, keepdims=True), mass.shape
        )


def stiff_terms(own, low, high, coefs, masses):
    rows, layers, cells_y, cells_z = own.shape
    tall, wide = rows * SUB, cells_y // SUB * cells_z
    block = (rows, 1, cells_y, cells_z)
    cells = (1, cells_y, cells_z)
    return pl.pallas_call(
        stiff_kernel,
        grid=(layers,),
        in_specs=[
            pl.BlockSpec(block, lambda g: (0, g, 0, 0)),
            pl.BlockSpec(block, lambda g: (0, jnp.maximum(g - 1, 0), 0, 0)),
            pl.BlockSpec(block, lambda g: (0, jnp.minimum(g + 1, layers - 1), 0, 0)),
            pl.BlockSpec(block, lambda g: (0, 0, 0, 0)),
            pl.BlockSpec(block, lambda g: (0, 0, 0, 0)),
            pl.BlockSpec(cells, lambda g: (g, 0, 0)),
            pl.BlockSpec(cells, lambda g: (g, 0, 0)),
        ],
        out_specs=[
            pl.BlockSpec((1, tall, wide), lambda g: (g, 0, 0)),
            pl.BlockSpec((rows, rows), lambda g: (0, 0)),
            pl.BlockSpec((rows, rows), lambda g: (0, 0)),
        ],
        out_shape=[
            jax.ShapeDtypeStruct((layers, tall, wide), jnp.bfloat16),
            jax.ShapeDtypeStruct((rows, rows), jnp.float32),
            jax.ShapeDtypeStruct((rows, rows), jnp.float32),
        ],
        scratch_shapes=[
            pltpu.VMEM((tall, tall), jnp.float32),
            pltpu.VMEM((tall, wide), jnp.bfloat16),
            pltpu.VMEM((rows, SUB, cells_z), jnp.float32),
        ],
        compiler_params=params(),
        cost_estimate=SMALL,
        name="stiff_terms",
    )(own, own, own, low, high, coefs, masses)


def cross_kernel(at, skip, stiff, other, gram, total):
    step = pl.program_id(0)

    @pl.when(step == 0)
    def _():
        total[...] = jnp.zeros_like(total)

    accumulate(total, stiff[0], split_rows(other[:, 0]))

    @pl.when(step == pl.num_programs(0) - 1)
    def _():
        gram[...] = same_row_sum(total[...])


def cross_terms(stiff, other, at, skip, layers):
    rows, _, cells_y, cells_z = other.shape
    _, tall, wide = stiff.shape
    return pl.pallas_call(
        cross_kernel,
        grid_spec=pltpu.PrefetchScalarGridSpec(
            num_scalar_prefetch=2,
            grid=(layers,),
            in_specs=[
                pl.BlockSpec((1, tall, wide), lambda g, at, skip: (at[0] + g, 0, 0)),
                pl.BlockSpec((rows, 1, cells_y, cells_z), lambda g, at, skip: (0, skip[0] + g, 0, 0)),
            ],
            out_specs=pl.BlockSpec((rows, rows), lambda g, at, skip: (0, 0)),
            scratch_shapes=[pltpu.VMEM((tall, tall), jnp.float32)],
        ),
        out_shape=jax.ShapeDtypeStruct((rows, rows), jnp.float32),
        compiler_params=params(),
        cost_estimate=SMALL,
        name="cross_terms",
    )(at.reshape(1), skip.reshape(1), stiff, other)


def cut_kernel(at, whole, order, out, sem):
    copy = pltpu.make_async_copy(whole.at[:, pl.ds(at[0], out.shape[1])], out, sem)
    copy.start()
    copy.wait()


def cut(whole, at, count, order):
    rows, _, cells_y, cells_z = whole.shape
    return pl.pallas_call(
        cut_kernel,
        grid_spec=pltpu.PrefetchScalarGridSpec(
            num_scalar_prefetch=1,
            grid=(1,),
            in_specs=[pl.BlockSpec(memory_space=pl.ANY)] * 2,
            out_specs=pl.BlockSpec(memory_space=pl.ANY),
            scratch_shapes=[pltpu.SemaphoreType.DMA],
        ),
        out_shape=jax.ShapeDtypeStruct((rows, count, cells_y, cells_z), whole.dtype),
        compiler_params=params(),
        cost_estimate=SMALL,
        name="cut",
    )(at.reshape(1), whole, order)


def merge_kernel(blk, whole, theirs, node, root):
    nodes, rows, _ = whole.shape
    first = blk[0] == 0
    total = None
    for p in range(nodes):
        gram = whole[p, :, :rows]
        cross = whole[p, :, rows : 2 * rows] + theirs[p, :, :rows].T
        scale = 1.0 / jnp.sqrt(whole[p, :, 2 * rows :])
        scale_gram = scale.T
        scale_cross = (1.0 / jnp.sqrt(theirs[p, :, rows:])).T
        low, high = jnp.where(first, gram, cross), jnp.where(first, cross, gram)
        scale_low = jnp.where(first, scale_gram, scale_cross)
        scale_high = jnp.where(first, scale_cross, scale_gram)
        node[p, :, :rows] = low
        node[p, :, rows:] = high
        here = jnp.concatenate([scale * low * scale_low, scale * high * scale_high], axis=1)
        total = here if total is None else total + here
    root[...] = total


def merge(whole, theirs, blk):
    nodes, rows, _ = whole.shape
    return pl.pallas_call(
        merge_kernel,
        grid_spec=pltpu.PrefetchScalarGridSpec(
            num_scalar_prefetch=1,
            grid=(1,),
            in_specs=[
                pl.BlockSpec(whole.shape, lambda g, blk: (0, 0, 0)),
                pl.BlockSpec(theirs.shape, lambda g, blk: (0, 0, 0)),
            ],
            out_specs=[
                pl.BlockSpec((nodes, rows, 2 * rows), lambda g, blk: (0, 0, 0)),
                pl.BlockSpec((rows, 2 * rows), lambda g, blk: (0, 0)),
            ],
        ),
        out_shape=[
            jax.ShapeDtypeStruct((nodes, rows, 2 * rows), jnp.float32),
            jax.ShapeDtypeStruct((rows, 2 * rows), jnp.float32),
        ],
        compiler_params=params(),
        cost_estimate=SMALL,
        name="merge",
    )(blk.astype(jnp.int32).reshape(1), whole, theirs)


def spread_kernel(block, out):
    tall, wide = out.shape
    eigs, modes = block.shape

    def shape_of(rows, cols, dim):
        index = lax.broadcasted_iota(jnp.int32, (rows, cols), dim)
        near = lax.broadcasted_iota(jnp.int32, (rows, cols), 1 - dim)
        return (index // SUB == near).astype(jnp.bfloat16)

    wider = jnp.dot(block[...], shape_of(modes, wide, 1), preferred_element_type=jnp.float32)
    full = jnp.dot(
        shape_of(tall, eigs, 0), wider.astype(jnp.bfloat16), preferred_element_type=jnp.float32
    )
    row = lax.broadcasted_iota(jnp.int32, (tall, wide), 0) % SUB
    col = lax.broadcasted_iota(jnp.int32, (tall, wide), 1) % SUB
    out[...] = jnp.where(row == col, full, 0.0).astype(out.dtype)


def spread_blocks(block):
    eigs, modes = block.shape
    return pl.pallas_call(
        spread_kernel,
        out_shape=jax.ShapeDtypeStruct((eigs * SUB, modes * SUB), block.dtype),
        compiler_params=pltpu.CompilerParams(vmem_limit_bytes=VMEM_BYTES),
        cost_estimate=SMALL,
        name="spread_blocks",
    )(block)


def vector_kernel(at, spread, own, other, *rest):
    out = rest[-1]
    rows, _, cells_y, cells_z = own.shape
    both = jnp.concatenate([split_rows(own[:, 0]), split_rows(other[:, 0])], axis=0)
    made = jnp.dot(spread[...], both, preferred_element_type=jnp.float32)
    eigs = out.shape[0]
    parts = [
        made[:, i * cells_z : (i + 1) * cells_z].reshape(eigs, SUB, cells_z)
        for i in range(cells_y // SUB)
    ]
    out[:, 0] = jnp.concatenate(parts, axis=1).astype(out.dtype)


def expand(spread, own, other, at, held):
    rows, layers, cells_y, cells_z = other.shape
    eigs = spread.shape[0] // SUB
    inputs = [at.reshape(1), spread, own, other]
    specs = [
        pl.BlockSpec(spread.shape, lambda g, at: (0, 0)),
        pl.BlockSpec((rows, 1, cells_y, cells_z), lambda g, at: (0, at[0] + g, 0, 0)),
        pl.BlockSpec((rows, 1, cells_y, cells_z), lambda g, at: (0, g, 0, 0)),
    ]
    aliases = {}
    if held is not None:
        aliases = {len(inputs): 0}
        inputs.append(held)
        specs.append(pl.BlockSpec(memory_space=pl.ANY))
    return pl.pallas_call(
        vector_kernel,
        grid_spec=pltpu.PrefetchScalarGridSpec(
            num_scalar_prefetch=1,
            grid=(layers,),
            in_specs=specs,
            out_specs=pl.BlockSpec((eigs, 1, cells_y, cells_z), lambda g, at: (0, at[0] + g, 0, 0)),
        ),
        out_shape=jax.ShapeDtypeStruct((eigs,) + own.shape[1:], jnp.bfloat16),
        input_output_aliases=aliases,
        compiler_params=params(),
        cost_estimate=SMALL,
        name="expand",
    )(*inputs)


def shares(total, parts):
    return [total // parts + (i < total % parts) for i in range(parts)]


def swap(x):
    return lax.ppermute(x, "blk", [(0, 1), (1, 0)])


def paired_sum(x, axis):
    size, step = lax.axis_size(axis), 1
    while step < size:
        x = x + lax.ppermute(x, axis, [(i, i ^ step) for i in range(size)])
        step *= 2
    return x


def line_sum(x, axis):
    x = x + lax.ppermute(x, axis, [(0, 1), (1, 0), (2, 3), (3, 2)])
    x = x + lax.ppermute(x, axis, [(1, 2), (2, 1)])
    outer = lax.ppermute(x, axis, [(1, 0), (2, 3)])
    place = lax.axis_index(axis)
    return jnp.where((place == 0) | (place == 3), outer, x)


def halved(modes, stiffness, density, eigen_blocks, parent):
    own = modes[0]
    rows, layers = own.shape[:2]
    half = layers // 2
    blk, dof, leaf = lax.axis_index("blk"), lax.axis_index("dof"), lax.axis_index("leaf")
    upper = (blk + dof) % 2

    def spot(offset, count, top):
        forward, back = half - 1 + offset, half + 1 - offset - count
        return jnp.where(top == 1, forward, back).astype(jnp.int32)

    def far_spot(offset, count, top):
        forward, back = half + 1 + offset, half - 1 - offset - count
        return jnp.where(top == 0, forward, back).astype(jnp.int32)

    def send(at, count):
        return swap(lax.dynamic_slice_in_dim(own, at, count, axis=1))

    nears = shares(half + 1, 2)
    last = half // 8
    fars = shares(half - 1 - last, 1)
    near_at = [sum(nears[:i]) for i in range(len(nears))]
    far_at = [sum(fars[:i]) for i in range(len(fars))]

    near = [send(spot(o, n, 1 - upper), n) for o, n in zip(near_at, nears)]
    far = [send(far_spot(o, n, 1 - upper), n) for o, n in zip(far_at, fars)]
    size = lax.axis_size("dof")
    low = lax.ppermute(own[:, -1:], "dof", [(i, i + 1) for i in range(size - 1)])
    high = lax.ppermute(own[:, :1], "dof", [(i + 1, i) for i in range(size - 1)])
    stiff, gram, mass = stiff_terms(own, low, high, stiffness[0], density[0])

    mine = lax.dynamic_slice_in_dim(eigen_blocks[0], blk * rows, rows, 0)
    other = lax.dynamic_slice_in_dim(eigen_blocks[0], (1 - blk) * rows, rows, 0)
    spread = spread_blocks(jnp.concatenate([mine, other], axis=0).T)

    own_in = lax.dynamic_slice_in_dim(own, spot(1, 1, upper), 1, axis=1)
    own_out = lax.dynamic_slice_in_dim(own, spot(0, 1, upper), 1, axis=1)
    first = spot(0, nears[0], upper)
    near_in = lax.dynamic_slice_in_dim(near[0], spot(1, 1, upper) - first, 1, axis=1)
    near_out = lax.dynamic_slice_in_dim(near[0], spot(0, 1, upper) - first, 1, axis=1)
    across = functools.partial(
        lax.dot_general,
        dimension_numbers=(((1, 2, 3), (1, 2, 3)), ((), ())),
        preferred_element_type=jnp.float32,
    )
    cross = 0.5 * (across(own_out, near_in) - across(own_in, near_out))
    for chunk, offset, count in zip(near, near_at, nears):
        chunk_at = spot(offset, count, upper)
        skipped = int(offset == 0)
        at = spot(offset + skipped, count - skipped, upper)
        cross = cross + cross_terms(stiff, chunk, at, at - chunk_at, count - skipped)

    whole = line_sum(jnp.concatenate([gram, cross, mass], axis=1), "dof")
    nodes = lax.axis_size("leaf") // 2
    belongs = (parent[leaf] == jnp.arange(nodes, dtype=jnp.int32)).astype(jnp.float32)
    whole = paired_sum(belongs[:, None, None] * whole[None], "leaf")
    theirs = swap(whole[:, :, rows:])
    final = swap(cut(own, far_spot(sum(fars), last, 1 - upper), last, whole))

    vectors = None
    for chunk, offset, count in zip(near, near_at, nears):
        vectors = expand(spread, own, chunk, spot(offset, count, upper), vectors)
    for chunk, offset, count in zip(far, far_at, fars):
        vectors = expand(spread, own, chunk, far_spot(offset, count, upper), vectors)
    node_stiffness, root_stiffness = merge(whole, theirs, blk)
    vectors = expand(spread, own, final, far_spot(sum(fars), last, upper), vectors)
    return (node_stiffness, root_stiffness, vectors[None])


def extended(x, sides, width):
    for axis, dim in sides:
        size, length = (lax.axis_size(axis), x.shape[dim])
        up = [(i, (i + 1) % size) for i in range(size - 1)]
        down = [(j, i) for i, j in up]
        last = lax.slice_in_dim(x, length - width, length, axis=dim)
        leading = lax.slice_in_dim(x, 0, width, axis=dim)
        before = lax.ppermute(last, axis, up)
        after = lax.ppermute(leading, axis, down)
        x = jnp.concatenate([before, x, after], axis=dim)
    return x


def neighbours(padded):
    inner = padded[:, 1:-1]
    sides = jnp.pad(inner, ((0, 0), (0, 0), (1, 1), (1, 1)))
    total = padded[:, 2:] + padded[:, :-2]
    total = total + sides[:, :, 2:, 1:-1] + sides[:, :, :-2, 1:-1]
    total = total + sides[:, :, 1:-1, 2:] + sides[:, :, 1:-1, :-2]
    return total


def gathered(modes, stiffness, density, eigen_blocks, parent):
    own = modes[0]
    rows, cells_x, cells_y, cells_z = own.shape
    cells = cells_x * cells_y * cells_z
    total_modes = rows * lax.axis_size("blk")
    padded = extended(own, (("dof", 1),), 1).astype(jnp.float32)
    field = padded[:, 1:-1]
    stiff = ((6.0 + stiffness[0]) * field - neighbours(padded)).astype(jnp.bfloat16)
    stiff_flat = stiff.reshape(rows, cells)
    own_flat = own.reshape(rows, cells)
    mass_flat = density[0].reshape(cells)
    weighed_own = (mass_flat[None, :] * own_flat.astype(jnp.float32)).astype(jnp.bfloat16)
    diag_own = jnp.einsum("rc,rc->r", weighed_own, own_flat, preferred_element_type=jnp.float32)
    diagonal = lax.all_gather(diag_own, "blk", axis=0, tiled=True)
    blocks = eigen_blocks[0]
    eig_rows = blocks.shape[1]
    piece = lax.all_gather(own_flat, "blk", axis=0, tiled=True)
    columns = lax.dot_general(
        stiff_flat, piece, (((1,), (1,)), ((), ())), preferred_element_type=jnp.float32
    )
    reduced = columns
    vectors = lax.dot_general(
        blocks, piece, (((0,), (0,)), ((), ())), preferred_element_type=jnp.float32
    )
    reduced, vectors = (reduced, vectors)
    vector_flat = vectors.astype(jnp.bfloat16)
    leaf_vectors = vector_flat.reshape(1, eig_rows, cells_x, cells_y, cells_z)
    leaves = lax.axis_size("leaf")
    nodes = leaves // 2
    node_ids = jnp.arange(nodes, dtype=jnp.int32)
    halves = lax.axis_size("dof")
    gathered_rows, gathered_diag = (
        lax.all_gather(reduced[None], ("leaf", "dof"), axis=0, tiled=True),
        lax.all_gather(diagonal[None], ("leaf", "dof"), axis=0, tiled=True),
    )
    leaf_rows = jnp.sum(gathered_rows.reshape(leaves, halves, rows, total_modes), axis=1)
    leaf_diag = jnp.sum(gathered_diag.reshape(leaves, halves, total_modes), axis=1)
    onehot = (parent[:, None] == node_ids[None, :]).astype(jnp.float32)
    node_stiffness = jnp.einsum("lp,lij->pij", onehot, leaf_rows, precision=lax.Precision.HIGHEST)
    node_mass = jnp.einsum("lp,li->pi", onehot, leaf_diag, precision=lax.Precision.HIGHEST)
    scale = 1.0 / jnp.sqrt(node_mass)
    scale_own = lax.dynamic_slice_in_dim(scale, lax.axis_index("blk") * rows, rows, 1)
    root_stiffness = jnp.sum(scale_own[:, :, None] * node_stiffness * scale[:, None, :], axis=0)
    return (node_stiffness, root_stiffness, leaf_vectors)


def solution(mesh):
    body = gathered
    if mesh.shape["blk"] == 2 and mesh.shape["dof"] == 4:
        body = halved
    in_specs = (
        P("leaf", "blk", "dof", None, None),
        P("leaf", "dof", None, None),
        P("leaf", "dof", None, None),
        P("leaf", None, "blk"),
        P(),
    )
    out_specs = (P(None, "blk", None), P("blk", None), P("leaf", "blk", "dof", None, None))
    return jax.shard_map(body, mesh=mesh, in_specs=in_specs, out_specs=out_specs, check_vma=False)
```

```python
import functools
import jax
import jax.numpy as jnp
from jax import lax
from jax.experimental import pallas as pl
from jax.experimental.pallas import tpu as pltpu
from jax.sharding import PartitionSpec as P

SUB = 8
VMEM_BYTES = 48 * 1024 * 1024
SMALL = pl.CostEstimate(flops=1024, bytes_accessed=1024, transcendentals=0)


def params():
    return pltpu.CompilerParams(
        dimension_semantics=("arbitrary",), vmem_limit_bytes=VMEM_BYTES
    )


def split_rows(x):
    wide = x.astype(jnp.float32)
    rows, cells_y, cells_z = wide.shape
    parts = [
        wide[:, i * SUB : (i + 1) * SUB].reshape(rows * SUB, cells_z).astype(jnp.bfloat16)
        for i in range(cells_y // SUB)
    ]
    return jnp.concatenate(parts, axis=1)


def accumulate(total, left, right):
    total[...] += lax.dot_general(
        left, right, (((1,), (1,)), ((), ())), preferred_element_type=jnp.float32
    )


def same_row_sum(total):
    tall, wide = total.shape
    row = lax.broadcasted_iota(jnp.int32, (tall, wide), 0) % SUB
    col = lax.broadcasted_iota(jnp.int32, (tall, wide), 1) % SUB
    kept = jnp.where(row == col, total, 0.0).reshape(tall // SUB, SUB, wide)
    folded = jnp.sum(kept, axis=1)
    group = lax.broadcasted_iota(jnp.int32, (wide, wide // SUB), 0) // SUB
    pick = (group == lax.broadcasted_iota(jnp.int32, (wide, wide // SUB), 1)).astype(jnp.float32)
    return jnp.dot(folded, pick, precision=lax.Precision.HIGHEST, preferred_element_type=jnp.float32)


def stiff_kernel(own, prev, after, low, high, coefs, masses, stiff, gram, mass, total, flat, acc):
    layer, last = pl.program_id(0), pl.num_programs(0) - 1
    rows, _, cells_y, cells_z = own.shape

    @pl.when(layer == 0)
    def _():
        total[...] = jnp.zeros_like(total)
        acc[...] = jnp.zeros_like(acc)

    y = lax.broadcasted_iota(jnp.int32, (SUB, cells_y, cells_z), 1)
    z = lax.broadcasted_iota(jnp.int32, (SUB, cells_y, cells_z), 2)
    diagonal = 6.0 + coefs[0]
    density = masses[0]

    def group(g, carry):
        modes = pl.ds(g * SUB, SUB)
        field = own[modes, 0].astype(jnp.float32)
        before = jnp.where(layer == 0, low[modes, 0], prev[modes, 0]).astype(jnp.float32)
        behind = jnp.where(layer == last, high[modes, 0], after[modes, 0]).astype(jnp.float32)
        around = before + behind
        around += jnp.where(y == 0, 0.0, pltpu.roll(field, 1, 1))
        around += jnp.where(y == cells_y - 1, 0.0, pltpu.roll(field, cells_y - 1, 1))
        around += jnp.where(z == 0, 0.0, pltpu.roll(field, 1, 2))
        around += jnp.where(z == cells_z - 1, 0.0, pltpu.roll(field, cells_z - 1, 2))
        force = diagonal[None] * field - around
        weighed = (density[None] * field).astype(jnp.bfloat16).astype(jnp.float32) * field
        out = pl.ds(g * SUB * SUB, SUB * SUB)
        part = None
        for i in range(cells_y // SUB):
            rows_y, lanes = slice(i * SUB, (i + 1) * SUB), slice(i * cells_z, (i + 1) * cells_z)
            stiff[0, out, lanes] = force[:, rows_y].reshape(SUB * SUB, cells_z).astype(jnp.bfloat16)
            flat[out, lanes] = field[:, rows_y].reshape(SUB * SUB, cells_z).astype(jnp.bfloat16)
            part = weighed[:, rows_y] if part is None else part + weighed[:, rows_y]
        acc[modes] += part
        return carry

    lax.fori_loop(0, rows // SUB, group, 0)
    accumulate(total, stiff[0], flat[...])

    @pl.when(layer == last)
    def _():
        gram[...] = same_row_sum(total[...])
        mass[...] = jnp.broadcast_to(
            jnp.sum(jnp.sum(acc[...], axis=1), axis=1, keepdims=True), mass.shape
        )


def stiff_terms(own, low, high, coefs, masses):
    rows, layers, cells_y, cells_z = own.shape
    tall, wide = rows * SUB, cells_y // SUB * cells_z
    block = (rows, 1, cells_y, cells_z)
    cells = (1, cells_y, cells_z)
    return pl.pallas_call(
        stiff_kernel,
        grid=(layers,),
        in_specs=[
            pl.BlockSpec(block, lambda g: (0, g, 0, 0)),
            pl.BlockSpec(block, lambda g: (0, jnp.maximum(g - 1, 0), 0, 0)),
            pl.BlockSpec(block, lambda g: (0, jnp.minimum(g + 1, layers - 1), 0, 0)),
            pl.BlockSpec(block, lambda g: (0, 0, 0, 0)),
            pl.BlockSpec(block, lambda g: (0, 0, 0, 0)),
            pl.BlockSpec(cells, lambda g: (g, 0, 0)),
            pl.BlockSpec(cells, lambda g: (g, 0, 0)),
        ],
        out_specs=[
            pl.BlockSpec((1, tall, wide), lambda g: (g, 0, 0)),
            pl.BlockSpec((rows, rows), lambda g: (0, 0)),
            pl.BlockSpec((rows, rows), lambda g: (0, 0)),
        ],
        out_shape=[
            jax.ShapeDtypeStruct((layers, tall, wide), jnp.bfloat16),
            jax.ShapeDtypeStruct((rows, rows), jnp.float32),
            jax.ShapeDtypeStruct((rows, rows), jnp.float32),
        ],
        scratch_shapes=[
            pltpu.VMEM((tall, tall), jnp.float32),
            pltpu.VMEM((tall, wide), jnp.bfloat16),
            pltpu.VMEM((rows, SUB, cells_z), jnp.float32),
        ],
        compiler_params=params(),
        cost_estimate=SMALL,
        name="stiff_terms",
    )(own, own, own, low, high, coefs, masses)


def cross_kernel(at, skip, stiff, other, gram, total):
    step = pl.program_id(0)

    @pl.when(step == 0)
    def _():
        total[...] = jnp.zeros_like(total)

    accumulate(total, stiff[0], split_rows(other[:, 0]))

    @pl.when(step == pl.num_programs(0) - 1)
    def _():
        gram[...] = same_row_sum(total[...])


def cross_terms(stiff, other, at, skip, layers):
    rows, _, cells_y, cells_z = other.shape
    _, tall, wide = stiff.shape
    return pl.pallas_call(
        cross_kernel,
        grid_spec=pltpu.PrefetchScalarGridSpec(
            num_scalar_prefetch=2,
            grid=(layers,),
            in_specs=[
                pl.BlockSpec((1, tall, wide), lambda g, at, skip: (at[0] + g, 0, 0)),
                pl.BlockSpec((rows, 1, cells_y, cells_z), lambda g, at, skip: (0, skip[0] + g, 0, 0)),
            ],
            out_specs=pl.BlockSpec((rows, rows), lambda g, at, skip: (0, 0)),
            scratch_shapes=[pltpu.VMEM((tall, tall), jnp.float32)],
        ),
        out_shape=jax.ShapeDtypeStruct((rows, rows), jnp.float32),
        compiler_params=params(),
        cost_estimate=SMALL,
        name="cross_terms",
    )(at.reshape(1), skip.reshape(1), stiff, other)


def cut_kernel(at, whole, *rest):
    out, sem = rest[-2:]
    copy = pltpu.make_async_copy(whole.at[:, pl.ds(at[0], out.shape[1])], out, sem)
    copy.start()
    copy.wait()


def cut(whole, at, count, *orders):
    rows, _, cells_y, cells_z = whole.shape
    return pl.pallas_call(
        cut_kernel,
        grid_spec=pltpu.PrefetchScalarGridSpec(
            num_scalar_prefetch=1,
            grid=(1,),
            in_specs=[pl.BlockSpec(memory_space=pl.ANY)] * (1 + len(orders)),
            out_specs=pl.BlockSpec(memory_space=pl.ANY),
            scratch_shapes=[pltpu.SemaphoreType.DMA],
        ),
        out_shape=jax.ShapeDtypeStruct((rows, count, cells_y, cells_z), whole.dtype),
        compiler_params=params(),
        cost_estimate=SMALL,
        name="cut",
    )(at.reshape(1), whole, *orders)


def merge_kernel(blk, whole, theirs, order, node, root):
    nodes, rows, _ = whole.shape
    first = blk[0] == 0
    total = None
    for p in range(nodes):
        gram = whole[p, :, :rows]
        cross = whole[p, :, rows : 2 * rows] + theirs[p, :, :rows].T
        scale = 1.0 / jnp.sqrt(whole[p, :, 2 * rows :])
        scale_gram = scale.T
        scale_cross = (1.0 / jnp.sqrt(theirs[p, :, rows:])).T
        low, high = jnp.where(first, gram, cross), jnp.where(first, cross, gram)
        scale_low = jnp.where(first, scale_gram, scale_cross)
        scale_high = jnp.where(first, scale_cross, scale_gram)
        node[p, :, :rows] = low
        node[p, :, rows:] = high
        here = jnp.concatenate([scale * low * scale_low, scale * high * scale_high], axis=1)
        total = here if total is None else total + here
    root[...] = total


def merge(whole, theirs, blk, order):
    nodes, rows, _ = whole.shape
    return pl.pallas_call(
        merge_kernel,
        grid_spec=pltpu.PrefetchScalarGridSpec(
            num_scalar_prefetch=1,
            grid=(1,),
            in_specs=[
                pl.BlockSpec(whole.shape, lambda g, blk: (0, 0, 0)),
                pl.BlockSpec(theirs.shape, lambda g, blk: (0, 0, 0)),
                pl.BlockSpec(memory_space=pl.ANY),
            ],
            out_specs=[
                pl.BlockSpec((nodes, rows, 2 * rows), lambda g, blk: (0, 0, 0)),
                pl.BlockSpec((rows, 2 * rows), lambda g, blk: (0, 0)),
            ],
        ),
        out_shape=[
            jax.ShapeDtypeStruct((nodes, rows, 2 * rows), jnp.float32),
            jax.ShapeDtypeStruct((rows, 2 * rows), jnp.float32),
        ],
        compiler_params=params(),
        cost_estimate=SMALL,
        name="merge",
    )(blk.astype(jnp.int32).reshape(1), whole, theirs, order)


def spread_kernel(block, out):
    tall, wide = out.shape
    eigs, modes = block.shape

    def shape_of(rows, cols, dim):
        index = lax.broadcasted_iota(jnp.int32, (rows, cols), dim)
        near = lax.broadcasted_iota(jnp.int32, (rows, cols), 1 - dim)
        return (index // SUB == near).astype(jnp.bfloat16)

    wider = jnp.dot(block[...], shape_of(modes, wide, 1), preferred_element_type=jnp.float32)
    full = jnp.dot(
        shape_of(tall, eigs, 0), wider.astype(jnp.bfloat16), preferred_element_type=jnp.float32
    )
    row = lax.broadcasted_iota(jnp.int32, (tall, wide), 0) % SUB
    col = lax.broadcasted_iota(jnp.int32, (tall, wide), 1) % SUB
    out[...] = jnp.where(row == col, full, 0.0).astype(out.dtype)


def spread_blocks(block):
    eigs, modes = block.shape
    return pl.pallas_call(
        spread_kernel,
        out_shape=jax.ShapeDtypeStruct((eigs * SUB, modes * SUB), block.dtype),
        compiler_params=pltpu.CompilerParams(vmem_limit_bytes=VMEM_BYTES),
        cost_estimate=SMALL,
        name="spread_blocks",
    )(block)


def vector_kernel(at, spread, own, other, *rest):
    out, order = rest[-2:]
    order[...] = jnp.zeros_like(order)
    rows, _, cells_y, cells_z = own.shape
    both = jnp.concatenate([split_rows(own[:, 0]), split_rows(other[:, 0])], axis=0)
    made = jnp.dot(spread[...], both, preferred_element_type=jnp.float32)
    eigs = out.shape[0]
    parts = [
        made[:, i * cells_z : (i + 1) * cells_z].reshape(eigs, SUB, cells_z)
        for i in range(cells_y // SUB)
    ]
    out[:, 0] = jnp.concatenate(parts, axis=1).astype(out.dtype)


def expand(spread, own, other, at, held):
    rows, layers, cells_y, cells_z = other.shape
    eigs = spread.shape[0] // SUB
    inputs = [at.reshape(1), spread, own, other]
    specs = [
        pl.BlockSpec(spread.shape, lambda g, at: (0, 0)),
        pl.BlockSpec((rows, 1, cells_y, cells_z), lambda g, at: (0, at[0] + g, 0, 0)),
        pl.BlockSpec((rows, 1, cells_y, cells_z), lambda g, at: (0, g, 0, 0)),
    ]
    aliases = {}
    if held is not None:
        aliases = {len(inputs): 0}
        inputs.append(held)
        specs.append(pl.BlockSpec(memory_space=pl.ANY))
    return pl.pallas_call(
        vector_kernel,
        grid_spec=pltpu.PrefetchScalarGridSpec(
            num_scalar_prefetch=1,
            grid=(layers,),
            in_specs=specs,
            out_specs=[
                pl.BlockSpec((eigs, 1, cells_y, cells_z), lambda g, at: (0, at[0] + g, 0, 0)),
                pl.BlockSpec((SUB, cells_z), lambda g, at: (0, 0)),
            ],
        ),
        out_shape=[
            jax.ShapeDtypeStruct((eigs,) + own.shape[1:], jnp.bfloat16),
            jax.ShapeDtypeStruct((SUB, cells_z), jnp.float32),
        ],
        input_output_aliases=aliases,
        compiler_params=params(),
        cost_estimate=SMALL,
        name="expand",
    )(*inputs)


def shares(total, parts):
    return [total // parts + (i < total % parts) for i in range(parts)]


def swap(x):
    return lax.ppermute(x, "blk", [(0, 1), (1, 0)])


def paired_sum(x, axis):
    size, step = lax.axis_size(axis), 1
    while step < size:
        x = x + lax.ppermute(x, axis, [(i, i ^ step) for i in range(size)])
        step *= 2
    return x


def line_sum(x, axis):
    x = x + lax.ppermute(x, axis, [(0, 1), (1, 0), (2, 3), (3, 2)])
    x = x + lax.ppermute(x, axis, [(1, 2), (2, 1)])
    outer = lax.ppermute(x, axis, [(1, 0), (2, 3)])
    place = lax.axis_index(axis)
    return jnp.where((place == 0) | (place == 3), outer, x)


def halved(modes, stiffness, density, eigen_blocks, parent):
    own = modes[0]
    rows, layers = own.shape[:2]
    half = layers // 2
    blk, dof, leaf = lax.axis_index("blk"), lax.axis_index("dof"), lax.axis_index("leaf")
    upper = (blk + dof) % 2

    def spot(offset, count, top):
        forward, back = half - 1 + offset, half + 1 - offset - count
        return jnp.where(top == 1, forward, back).astype(jnp.int32)

    def far_spot(offset, count, top):
        forward, back = half + 1 + offset, half - 1 - offset - count
        return jnp.where(top == 0, forward, back).astype(jnp.int32)

    def send(at, count, *orders):
        return swap(cut(own, at, count, *orders))

    nears = shares(half + 1, 2)
    last = half // 16
    middle = half // 4
    fars = [half - 1 - middle - last, middle, last]
    near_at = [sum(nears[:i]) for i in range(len(nears))]
    far_at = [sum(fars[:i]) for i in range(len(fars))]

    near = [send(spot(o, n, 1 - upper), n) for o, n in zip(near_at, nears)]
    far = [send(far_spot(far_at[0], fars[0], 1 - upper), fars[0])]
    size = lax.axis_size("dof")
    low = lax.ppermute(own[:, -1:], "dof", [(i, i + 1) for i in range(size - 1)])
    high = lax.ppermute(own[:, :1], "dof", [(i + 1, i) for i in range(size - 1)])
    stiff, gram, mass = stiff_terms(own, low, high, stiffness[0], density[0])

    mine = lax.dynamic_slice_in_dim(eigen_blocks[0], blk * rows, rows, 0)
    other = lax.dynamic_slice_in_dim(eigen_blocks[0], (1 - blk) * rows, rows, 0)
    spread = spread_blocks(jnp.concatenate([mine, other], axis=0).T)

    own_in = lax.dynamic_slice_in_dim(own, spot(1, 1, upper), 1, axis=1)
    own_out = lax.dynamic_slice_in_dim(own, spot(0, 1, upper), 1, axis=1)
    first = spot(0, nears[0], upper)
    near_in = lax.dynamic_slice_in_dim(near[0], spot(1, 1, upper) - first, 1, axis=1)
    near_out = lax.dynamic_slice_in_dim(near[0], spot(0, 1, upper) - first, 1, axis=1)
    across = functools.partial(
        lax.dot_general,
        dimension_numbers=(((1, 2, 3), (1, 2, 3)), ((), ())),
        preferred_element_type=jnp.float32,
    )
    cross = 0.5 * (across(own_out, near_in) - across(own_in, near_out))
    for chunk, offset, count in zip(near, near_at, nears):
        chunk_at = spot(offset, count, upper)
        skipped = int(offset == 0)
        at = spot(offset + skipped, count - skipped, upper)
        cross = cross + cross_terms(stiff, chunk, at, at - chunk_at, count - skipped)

    whole = line_sum(jnp.concatenate([gram, cross, mass], axis=1), "dof")
    nodes = lax.axis_size("leaf") // 2
    belongs = (parent[leaf] == jnp.arange(nodes, dtype=jnp.int32)).astype(jnp.float32)
    whole = paired_sum(belongs[:, None, None] * whole[None], "leaf")
    theirs = swap(whole[:, :, rows:])
    far += [send(far_spot(o, n, 1 - upper), n, whole) for o, n in zip(far_at[1:], fars[1:])]

    vectors = None
    for chunk, offset, count in zip(near, near_at, nears):
        vectors, _ = expand(spread, own, chunk, spot(offset, count, upper), vectors)
    places = [far_spot(o, n, upper) for o, n in zip(far_at, fars)]
    for chunk, at in zip(far[:-1], places[:-1]):
        vectors, order = expand(spread, own, chunk, at, vectors)
    node_stiffness, root_stiffness = merge(whole, theirs, blk, order)
    vectors, _ = expand(spread, own, far[-1], places[-1], vectors)
    return (node_stiffness, root_stiffness, vectors[None])


def extended(x, sides, width):
    for axis, dim in sides:
        size, length = (lax.axis_size(axis), x.shape[dim])
        up = [(i, (i + 1) % size) for i in range(size - 1)]
        down = [(j, i) for i, j in up]
        last = lax.slice_in_dim(x, length - width, length, axis=dim)
        leading = lax.slice_in_dim(x, 0, width, axis=dim)
        before = lax.ppermute(last, axis, up)
        after = lax.ppermute(leading, axis, down)
        x = jnp.concatenate([before, x, after], axis=dim)
    return x


def neighbours(padded):
    inner = padded[:, 1:-1]
    sides = jnp.pad(inner, ((0, 0), (0, 0), (1, 1), (1, 1)))
    total = padded[:, 2:] + padded[:, :-2]
    total = total + sides[:, :, 2:, 1:-1] + sides[:, :, :-2, 1:-1]
    total = total + sides[:, :, 1:-1, 2:] + sides[:, :, 1:-1, :-2]
    return total


def gathered(modes, stiffness, density, eigen_blocks, parent):
    own = modes[0]
    rows, cells_x, cells_y, cells_z = own.shape
    cells = cells_x * cells_y * cells_z
    total_modes = rows * lax.axis_size("blk")
    padded = extended(own, (("dof", 1),), 1).astype(jnp.float32)
    field = padded[:, 1:-1]
    stiff = ((6.0 + stiffness[0]) * field - neighbours(padded)).astype(jnp.bfloat16)
    stiff_flat = stiff.reshape(rows, cells)
    own_flat = own.reshape(rows, cells)
    mass_flat = density[0].reshape(cells)
    weighed_own = (mass_flat[None, :] * own_flat.astype(jnp.float32)).astype(jnp.bfloat16)
    diag_own = jnp.einsum("rc,rc->r", weighed_own, own_flat, preferred_element_type=jnp.float32)
    diagonal = lax.all_gather(diag_own, "blk", axis=0, tiled=True)
    blocks = eigen_blocks[0]
    eig_rows = blocks.shape[1]
    piece = lax.all_gather(own_flat, "blk", axis=0, tiled=True)
    columns = lax.dot_general(
        stiff_flat, piece, (((1,), (1,)), ((), ())), preferred_element_type=jnp.float32
    )
    reduced = columns
    vectors = lax.dot_general(
        blocks, piece, (((0,), (0,)), ((), ())), preferred_element_type=jnp.float32
    )
    reduced, vectors = (reduced, vectors)
    vector_flat = vectors.astype(jnp.bfloat16)
    leaf_vectors = vector_flat.reshape(1, eig_rows, cells_x, cells_y, cells_z)
    leaves = lax.axis_size("leaf")
    nodes = leaves // 2
    node_ids = jnp.arange(nodes, dtype=jnp.int32)
    halves = lax.axis_size("dof")
    gathered_rows, gathered_diag = (
        lax.all_gather(reduced[None], ("leaf", "dof"), axis=0, tiled=True),
        lax.all_gather(diagonal[None], ("leaf", "dof"), axis=0, tiled=True),
    )
    leaf_rows = jnp.sum(gathered_rows.reshape(leaves, halves, rows, total_modes), axis=1)
    leaf_diag = jnp.sum(gathered_diag.reshape(leaves, halves, total_modes), axis=1)
    onehot = (parent[:, None] == node_ids[None, :]).astype(jnp.float32)
    node_stiffness = jnp.einsum("lp,lij->pij", onehot, leaf_rows, precision=lax.Precision.HIGHEST)
    node_mass = jnp.einsum("lp,li->pi", onehot, leaf_diag, precision=lax.Precision.HIGHEST)
    scale = 1.0 / jnp.sqrt(node_mass)
    scale_own = lax.dynamic_slice_in_dim(scale, lax.axis_index("blk") * rows, rows, 1)
    root_stiffness = jnp.sum(scale_own[:, :, None] * node_stiffness * scale[:, None, :], axis=0)
    return (node_stiffness, root_stiffness, leaf_vectors)


def solution(mesh):
    body = gathered
    if mesh.shape["blk"] == 2 and mesh.shape["dof"] == 4:
        body = halved
    in_specs = (
        P("leaf", "blk", "dof", None, None),
        P("leaf", "dof", None, None),
        P("leaf", "dof", None, None),
        P("leaf", None, "blk"),
        P(),
    )
    out_specs = (P(None, "blk", None), P("blk", None), P("leaf", "blk", "dof", None, None))
    return jax.shard_map(body, mesh=mesh, in_specs=in_specs, out_specs=out_specs, check_vma=False)
```

```python
import functools
import jax
import jax.numpy as jnp
from jax import lax
from jax.experimental import pallas as pl
from jax.experimental.pallas import tpu as pltpu
from jax.sharding import PartitionSpec as P

SUB = 8
VMEM_BYTES = 48 * 1024 * 1024
SMALL = pl.CostEstimate(flops=1024, bytes_accessed=1024, transcendentals=0)


def params():
    return pltpu.CompilerParams(
        dimension_semantics=("arbitrary",), vmem_limit_bytes=VMEM_BYTES
    )


def split_rows(x):
    wide = x.astype(jnp.float32)
    rows, cells_y, cells_z = wide.shape
    parts = [
        wide[:, i * SUB : (i + 1) * SUB].reshape(rows * SUB, cells_z).astype(jnp.bfloat16)
        for i in range(cells_y // SUB)
    ]
    return jnp.concatenate(parts, axis=1)


def accumulate(total, left, right):
    total[...] += lax.dot_general(
        left, right, (((1,), (1,)), ((), ())), preferred_element_type=jnp.float32
    )


def same_row_sum(total):
    tall, wide = total.shape
    row = lax.broadcasted_iota(jnp.int32, (tall, wide), 0) % SUB
    col = lax.broadcasted_iota(jnp.int32, (tall, wide), 1) % SUB
    kept = jnp.where(row == col, total, 0.0).reshape(tall // SUB, SUB, wide)
    folded = jnp.sum(kept, axis=1)
    group = lax.broadcasted_iota(jnp.int32, (wide, wide // SUB), 0) // SUB
    pick = (group == lax.broadcasted_iota(jnp.int32, (wide, wide // SUB), 1)).astype(jnp.float32)
    return jnp.dot(folded, pick, precision=lax.Precision.HIGHEST, preferred_element_type=jnp.float32)


def stiff_kernel(own, prev, after, low, high, coefs, masses, stiff, gram, mass, total, flat, acc):
    layer, last = pl.program_id(0), pl.num_programs(0) - 1
    rows, _, cells_y, cells_z = own.shape

    @pl.when(layer == 0)
    def _():
        total[...] = jnp.zeros_like(total)
        acc[...] = jnp.zeros_like(acc)

    y = lax.broadcasted_iota(jnp.int32, (SUB, cells_y, cells_z), 1)
    z = lax.broadcasted_iota(jnp.int32, (SUB, cells_y, cells_z), 2)
    diagonal = 6.0 + coefs[0]
    density = masses[0]

    def group(g, carry):
        modes = pl.ds(g * SUB, SUB)
        field = own[modes, 0].astype(jnp.float32)
        before = jnp.where(layer == 0, low[modes, 0], prev[modes, 0]).astype(jnp.float32)
        behind = jnp.where(layer == last, high[modes, 0], after[modes, 0]).astype(jnp.float32)
        around = before + behind
        around += jnp.where(y == 0, 0.0, pltpu.roll(field, 1, 1))
        around += jnp.where(y == cells_y - 1, 0.0, pltpu.roll(field, cells_y - 1, 1))
        around += jnp.where(z == 0, 0.0, pltpu.roll(field, 1, 2))
        around += jnp.where(z == cells_z - 1, 0.0, pltpu.roll(field, cells_z - 1, 2))
        force = diagonal[None] * field - around
        weighed = (density[None] * field).astype(jnp.bfloat16).astype(jnp.float32) * field
        out = pl.ds(g * SUB * SUB, SUB * SUB)
        part = None
        for i in range(cells_y // SUB):
            rows_y, lanes = slice(i * SUB, (i + 1) * SUB), slice(i * cells_z, (i + 1) * cells_z)
            stiff[0, out, lanes] = force[:, rows_y].reshape(SUB * SUB, cells_z).astype(jnp.bfloat16)
            flat[out, lanes] = field[:, rows_y].reshape(SUB * SUB, cells_z).astype(jnp.bfloat16)
            part = weighed[:, rows_y] if part is None else part + weighed[:, rows_y]
        acc[modes] += part
        return carry

    lax.fori_loop(0, rows // SUB, group, 0)
    accumulate(total, stiff[0], flat[...])

    @pl.when(layer == last)
    def _():
        gram[...] = same_row_sum(total[...])
        mass[...] = jnp.broadcast_to(
            jnp.sum(jnp.sum(acc[...], axis=1), axis=1, keepdims=True), mass.shape
        )


def stiff_terms(own, low, high, coefs, masses):
    rows, layers, cells_y, cells_z = own.shape
    tall, wide = rows * SUB, cells_y // SUB * cells_z
    block = (rows, 1, cells_y, cells_z)
    cells = (1, cells_y, cells_z)
    return pl.pallas_call(
        stiff_kernel,
        grid=(layers,),
        in_specs=[
            pl.BlockSpec(block, lambda g: (0, g, 0, 0)),
            pl.BlockSpec(block, lambda g: (0, jnp.maximum(g - 1, 0), 0, 0)),
            pl.BlockSpec(block, lambda g: (0, jnp.minimum(g + 1, layers - 1), 0, 0)),
            pl.BlockSpec(block, lambda g: (0, 0, 0, 0)),
            pl.BlockSpec(block, lambda g: (0, 0, 0, 0)),
            pl.BlockSpec(cells, lambda g: (g, 0, 0)),
            pl.BlockSpec(cells, lambda g: (g, 0, 0)),
        ],
        out_specs=[
            pl.BlockSpec((1, tall, wide), lambda g: (g, 0, 0)),
            pl.BlockSpec((rows, rows), lambda g: (0, 0)),
            pl.BlockSpec((rows, rows), lambda g: (0, 0)),
        ],
        out_shape=[
            jax.ShapeDtypeStruct((layers, tall, wide), jnp.bfloat16),
            jax.ShapeDtypeStruct((rows, rows), jnp.float32),
            jax.ShapeDtypeStruct((rows, rows), jnp.float32),
        ],
        scratch_shapes=[
            pltpu.VMEM((tall, tall), jnp.float32),
            pltpu.VMEM((tall, wide), jnp.bfloat16),
            pltpu.VMEM((rows, SUB, cells_z), jnp.float32),
        ],
        compiler_params=params(),
        cost_estimate=SMALL,
        name="stiff_terms",
    )(own, own, own, low, high, coefs, masses)


def cross_kernel(at, skip, stiff, other, gram, total):
    step = pl.program_id(0)

    @pl.when(step == 0)
    def _():
        total[...] = jnp.zeros_like(total)

    accumulate(total, stiff[0], split_rows(other[:, 0]))

    @pl.when(step == pl.num_programs(0) - 1)
    def _():
        gram[...] = same_row_sum(total[...])


def cross_terms(stiff, other, at, skip, layers):
    rows, _, cells_y, cells_z = other.shape
    _, tall, wide = stiff.shape
    return pl.pallas_call(
        cross_kernel,
        grid_spec=pltpu.PrefetchScalarGridSpec(
            num_scalar_prefetch=2,
            grid=(layers,),
            in_specs=[
                pl.BlockSpec((1, tall, wide), lambda g, at, skip: (at[0] + g, 0, 0)),
                pl.BlockSpec((rows, 1, cells_y, cells_z), lambda g, at, skip: (0, skip[0] + g, 0, 0)),
            ],
            out_specs=pl.BlockSpec((rows, rows), lambda g, at, skip: (0, 0)),
            scratch_shapes=[pltpu.VMEM((tall, tall), jnp.float32)],
        ),
        out_shape=jax.ShapeDtypeStruct((rows, rows), jnp.float32),
        compiler_params=params(),
        cost_estimate=SMALL,
        name="cross_terms",
    )(at.reshape(1), skip.reshape(1), stiff, other)


def cut_kernel(at, whole, *rest):
    out, held, reads, writes = rest[-4:]
    pieces = held.shape[0]
    layers = out.shape[1]
    bounds = [layers * i // pieces for i in range(pieces + 1)]
    ins, outs = [], []
    for i in range(pieces):
        start, size = bounds[i], bounds[i + 1] - bounds[i]
        piece = held.at[i, :, pl.ds(0, size)]
        ins.append(
            pltpu.make_async_copy(whole.at[:, pl.ds(at[0] + start, size)], piece, reads.at[i])
        )
        outs.append(pltpu.make_async_copy(piece, out.at[:, pl.ds(start, size)], writes.at[i]))
    for copy in ins:
        copy.start()
    for i in range(pieces):
        ins[i].wait()
        outs[i].start()
    for copy in outs:
        copy.wait()


def cut(whole, at, count, *orders):
    rows, _, cells_y, cells_z = whole.shape
    pieces = min(4, count)
    longest = -(-count // pieces)
    return pl.pallas_call(
        cut_kernel,
        grid_spec=pltpu.PrefetchScalarGridSpec(
            num_scalar_prefetch=1,
            grid=(1,),
            in_specs=[pl.BlockSpec(memory_space=pl.ANY)] * (1 + len(orders)),
            out_specs=pl.BlockSpec(memory_space=pl.ANY),
            scratch_shapes=[
                pltpu.VMEM((pieces, rows, longest, cells_y, cells_z), whole.dtype),
                pltpu.SemaphoreType.DMA((pieces,)),
                pltpu.SemaphoreType.DMA((pieces,)),
            ],
        ),
        out_shape=jax.ShapeDtypeStruct((rows, count, cells_y, cells_z), whole.dtype),
        compiler_params=params(),
        cost_estimate=SMALL,
        name="cut",
    )(at.reshape(1), whole, *orders)


def merge_kernel(blk, whole, theirs, order, node, root):
    nodes, rows, _ = whole.shape
    first = blk[0] == 0
    total = None
    for p in range(nodes):
        gram = whole[p, :, :rows]
        cross = whole[p, :, rows : 2 * rows] + theirs[p, :, :rows].T
        scale = 1.0 / jnp.sqrt(whole[p, :, 2 * rows :])
        scale_gram = scale.T
        scale_cross = (1.0 / jnp.sqrt(theirs[p, :, rows:])).T
        low, high = jnp.where(first, gram, cross), jnp.where(first, cross, gram)
        scale_low = jnp.where(first, scale_gram, scale_cross)
        scale_high = jnp.where(first, scale_cross, scale_gram)
        node[p, :, :rows] = low
        node[p, :, rows:] = high
        here = jnp.concatenate([scale * low * scale_low, scale * high * scale_high], axis=1)
        total = here if total is None else total + here
    root[...] = total


def merge(whole, theirs, blk, order):
    nodes, rows, _ = whole.shape
    return pl.pallas_call(
        merge_kernel,
        grid_spec=pltpu.PrefetchScalarGridSpec(
            num_scalar_prefetch=1,
            grid=(1,),
            in_specs=[
                pl.BlockSpec(whole.shape, lambda g, blk: (0, 0, 0)),
                pl.BlockSpec(theirs.shape, lambda g, blk: (0, 0, 0)),
                pl.BlockSpec(memory_space=pl.ANY),
            ],
            out_specs=[
                pl.BlockSpec((nodes, rows, 2 * rows), lambda g, blk: (0, 0, 0)),
                pl.BlockSpec((rows, 2 * rows), lambda g, blk: (0, 0)),
            ],
        ),
        out_shape=[
            jax.ShapeDtypeStruct((nodes, rows, 2 * rows), jnp.float32),
            jax.ShapeDtypeStruct((rows, 2 * rows), jnp.float32),
        ],
        compiler_params=params(),
        cost_estimate=SMALL,
        name="merge",
    )(blk.astype(jnp.int32).reshape(1), whole, theirs, order)


def spread_kernel(block, out):
    tall, wide = out.shape
    eigs, modes = block.shape

    def shape_of(rows, cols, dim):
        index = lax.broadcasted_iota(jnp.int32, (rows, cols), dim)
        near = lax.broadcasted_iota(jnp.int32, (rows, cols), 1 - dim)
        return (index // SUB == near).astype(jnp.bfloat16)

    wider = jnp.dot(block[...], shape_of(modes, wide, 1), preferred_element_type=jnp.float32)
    full = jnp.dot(
        shape_of(tall, eigs, 0), wider.astype(jnp.bfloat16), preferred_element_type=jnp.float32
    )
    row = lax.broadcasted_iota(jnp.int32, (tall, wide), 0) % SUB
    col = lax.broadcasted_iota(jnp.int32, (tall, wide), 1) % SUB
    out[...] = jnp.where(row == col, full, 0.0).astype(out.dtype)


def spread_blocks(block):
    eigs, modes = block.shape
    return pl.pallas_call(
        spread_kernel,
        out_shape=jax.ShapeDtypeStruct((eigs * SUB, modes * SUB), block.dtype),
        compiler_params=pltpu.CompilerParams(vmem_limit_bytes=VMEM_BYTES),
        cost_estimate=SMALL,
        name="spread_blocks",
    )(block)


def vector_kernel(at, spread, own, other, *rest):
    out, order = rest[-2:]
    order[...] = jnp.zeros_like(order)
    rows, _, cells_y, cells_z = own.shape
    both = jnp.concatenate([split_rows(own[:, 0]), split_rows(other[:, 0])], axis=0)
    made = jnp.dot(spread[...], both, preferred_element_type=jnp.float32)
    eigs = out.shape[0]
    parts = [
        made[:, i * cells_z : (i + 1) * cells_z].reshape(eigs, SUB, cells_z)
        for i in range(cells_y // SUB)
    ]
    out[:, 0] = jnp.concatenate(parts, axis=1).astype(out.dtype)


def expand(spread, own, other, at, held):
    rows, layers, cells_y, cells_z = other.shape
    eigs = spread.shape[0] // SUB
    inputs = [at.reshape(1), spread, own, other]
    specs = [
        pl.BlockSpec(spread.shape, lambda g, at: (0, 0)),
        pl.BlockSpec((rows, 1, cells_y, cells_z), lambda g, at: (0, at[0] + g, 0, 0)),
        pl.BlockSpec((rows, 1, cells_y, cells_z), lambda g, at: (0, g, 0, 0)),
    ]
    aliases = {}
    if held is not None:
        aliases = {len(inputs): 0}
        inputs.append(held)
        specs.append(pl.BlockSpec(memory_space=pl.ANY))
    return pl.pallas_call(
        vector_kernel,
        grid_spec=pltpu.PrefetchScalarGridSpec(
            num_scalar_prefetch=1,
            grid=(layers,),
            in_specs=specs,
            out_specs=[
                pl.BlockSpec((eigs, 1, cells_y, cells_z), lambda g, at: (0, at[0] + g, 0, 0)),
                pl.BlockSpec((SUB, cells_z), lambda g, at: (0, 0)),
            ],
        ),
        out_shape=[
            jax.ShapeDtypeStruct((eigs,) + own.shape[1:], jnp.bfloat16),
            jax.ShapeDtypeStruct((SUB, cells_z), jnp.float32),
        ],
        input_output_aliases=aliases,
        compiler_params=params(),
        cost_estimate=SMALL,
        name="expand",
    )(*inputs)


def shares(total, parts):
    return [total // parts + (i < total % parts) for i in range(parts)]


def swap(x):
    return lax.ppermute(x, "blk", [(0, 1), (1, 0)])


def paired_sum(x, axis):
    size, step = lax.axis_size(axis), 1
    while step < size:
        x = x + lax.ppermute(x, axis, [(i, i ^ step) for i in range(size)])
        step *= 2
    return x


def line_sum(x, axis):
    x = x + lax.ppermute(x, axis, [(0, 1), (1, 0), (2, 3), (3, 2)])
    x = x + lax.ppermute(x, axis, [(1, 2), (2, 1)])
    outer = lax.ppermute(x, axis, [(1, 0), (2, 3)])
    place = lax.axis_index(axis)
    return jnp.where((place == 0) | (place == 3), outer, x)


def halved(modes, stiffness, density, eigen_blocks, parent):
    own = modes[0]
    rows, layers = own.shape[:2]
    half = layers // 2
    blk, dof, leaf = lax.axis_index("blk"), lax.axis_index("dof"), lax.axis_index("leaf")
    upper = (blk + dof) % 2

    def spot(offset, count, top):
        forward, back = half - 1 + offset, half + 1 - offset - count
        return jnp.where(top == 1, forward, back).astype(jnp.int32)

    def far_spot(offset, count, top):
        forward, back = half + 1 + offset, half - 1 - offset - count
        return jnp.where(top == 0, forward, back).astype(jnp.int32)

    def send(at, count, *orders):
        return swap(cut(own, at, count, *orders))

    nears = shares(half + 1, 2)
    last = half // 16
    middle = half // 4
    fars = [half - 1 - middle - last, middle, last]
    near_at = [sum(nears[:i]) for i in range(len(nears))]
    far_at = [sum(fars[:i]) for i in range(len(fars))]

    near = [send(spot(o, n, 1 - upper), n) for o, n in zip(near_at, nears)]
    far = [send(far_spot(far_at[0], fars[0], 1 - upper), fars[0])]
    size = lax.axis_size("dof")
    low = lax.ppermute(own[:, -1:], "dof", [(i, i + 1) for i in range(size - 1)])
    high = lax.ppermute(own[:, :1], "dof", [(i + 1, i) for i in range(size - 1)])
    stiff, gram, mass = stiff_terms(own, low, high, stiffness[0], density[0])

    mine = lax.dynamic_slice_in_dim(eigen_blocks[0], blk * rows, rows, 0)
    other = lax.dynamic_slice_in_dim(eigen_blocks[0], (1 - blk) * rows, rows, 0)
    spread = spread_blocks(jnp.concatenate([mine, other], axis=0).T)

    own_in = lax.dynamic_slice_in_dim(own, spot(1, 1, upper), 1, axis=1)
    own_out = lax.dynamic_slice_in_dim(own, spot(0, 1, upper), 1, axis=1)
    first = spot(0, nears[0], upper)
    near_in = lax.dynamic_slice_in_dim(near[0], spot(1, 1, upper) - first, 1, axis=1)
    near_out = lax.dynamic_slice_in_dim(near[0], spot(0, 1, upper) - first, 1, axis=1)
    across = functools.partial(
        lax.dot_general,
        dimension_numbers=(((1, 2, 3), (1, 2, 3)), ((), ())),
        preferred_element_type=jnp.float32,
    )
    cross = 0.5 * (across(own_out, near_in) - across(own_in, near_out))
    for chunk, offset, count in zip(near, near_at, nears):
        chunk_at = spot(offset, count, upper)
        skipped = int(offset == 0)
        at = spot(offset + skipped, count - skipped, upper)
        cross = cross + cross_terms(stiff, chunk, at, at - chunk_at, count - skipped)

    whole = line_sum(jnp.concatenate([gram, cross, mass], axis=1), "dof")
    nodes = lax.axis_size("leaf") // 2
    belongs = (parent[leaf] == jnp.arange(nodes, dtype=jnp.int32)).astype(jnp.float32)
    whole = paired_sum(belongs[:, None, None] * whole[None], "leaf")
    theirs = swap(whole[:, :, rows:])
    far += [send(far_spot(o, n, 1 - upper), n, whole) for o, n in zip(far_at[1:], fars[1:])]

    vectors = None
    for chunk, offset, count in zip(near, near_at, nears):
        vectors, _ = expand(spread, own, chunk, spot(offset, count, upper), vectors)
    places = [far_spot(o, n, upper) for o, n in zip(far_at, fars)]
    for chunk, at in zip(far[:-1], places[:-1]):
        vectors, order = expand(spread, own, chunk, at, vectors)
    node_stiffness, root_stiffness = merge(whole, theirs, blk, order)
    vectors, _ = expand(spread, own, far[-1], places[-1], vectors)
    return (node_stiffness, root_stiffness, vectors[None])


def extended(x, sides, width):
    for axis, dim in sides:
        size, length = (lax.axis_size(axis), x.shape[dim])
        up = [(i, (i + 1) % size) for i in range(size - 1)]
        down = [(j, i) for i, j in up]
        last = lax.slice_in_dim(x, length - width, length, axis=dim)
        leading = lax.slice_in_dim(x, 0, width, axis=dim)
        before = lax.ppermute(last, axis, up)
        after = lax.ppermute(leading, axis, down)
        x = jnp.concatenate([before, x, after], axis=dim)
    return x


def neighbours(padded):
    inner = padded[:, 1:-1]
    sides = jnp.pad(inner, ((0, 0), (0, 0), (1, 1), (1, 1)))
    total = padded[:, 2:] + padded[:, :-2]
    total = total + sides[:, :, 2:, 1:-1] + sides[:, :, :-2, 1:-1]
    total = total + sides[:, :, 1:-1, 2:] + sides[:, :, 1:-1, :-2]
    return total


def gathered(modes, stiffness, density, eigen_blocks, parent):
    own = modes[0]
    rows, cells_x, cells_y, cells_z = own.shape
    cells = cells_x * cells_y * cells_z
    total_modes = rows * lax.axis_size("blk")
    padded = extended(own, (("dof", 1),), 1).astype(jnp.float32)
    field = padded[:, 1:-1]
    stiff = ((6.0 + stiffness[0]) * field - neighbours(padded)).astype(jnp.bfloat16)
    stiff_flat = stiff.reshape(rows, cells)
    own_flat = own.reshape(rows, cells)
    mass_flat = density[0].reshape(cells)
    weighed_own = (mass_flat[None, :] * own_flat.astype(jnp.float32)).astype(jnp.bfloat16)
    diag_own = jnp.einsum("rc,rc->r", weighed_own, own_flat, preferred_element_type=jnp.float32)
    diagonal = lax.all_gather(diag_own, "blk", axis=0, tiled=True)
    blocks = eigen_blocks[0]
    eig_rows = blocks.shape[1]
    piece = lax.all_gather(own_flat, "blk", axis=0, tiled=True)
    columns = lax.dot_general(
        stiff_flat, piece, (((1,), (1,)), ((), ())), preferred_element_type=jnp.float32
    )
    reduced = columns
    vectors = lax.dot_general(
        blocks, piece, (((0,), (0,)), ((), ())), preferred_element_type=jnp.float32
    )
    reduced, vectors = (reduced, vectors)
    vector_flat = vectors.astype(jnp.bfloat16)
    leaf_vectors = vector_flat.reshape(1, eig_rows, cells_x, cells_y, cells_z)
    leaves = lax.axis_size("leaf")
    nodes = leaves // 2
    node_ids = jnp.arange(nodes, dtype=jnp.int32)
    halves = lax.axis_size("dof")
    gathered_rows, gathered_diag = (
        lax.all_gather(reduced[None], ("leaf", "dof"), axis=0, tiled=True),
        lax.all_gather(diagonal[None], ("leaf", "dof"), axis=0, tiled=True),
    )
    leaf_rows = jnp.sum(gathered_rows.reshape(leaves, halves, rows, total_modes), axis=1)
    leaf_diag = jnp.sum(gathered_diag.reshape(leaves, halves, total_modes), axis=1)
    onehot = (parent[:, None] == node_ids[None, :]).astype(jnp.float32)
    node_stiffness = jnp.einsum("lp,lij->pij", onehot, leaf_rows, precision=lax.Precision.HIGHEST)
    node_mass = jnp.einsum("lp,li->pi", onehot, leaf_diag, precision=lax.Precision.HIGHEST)
    scale = 1.0 / jnp.sqrt(node_mass)
    scale_own = lax.dynamic_slice_in_dim(scale, lax.axis_index("blk") * rows, rows, 1)
    root_stiffness = jnp.sum(scale_own[:, :, None] * node_stiffness * scale[:, None, :], axis=0)
    return (node_stiffness, root_stiffness, leaf_vectors)


def solution(mesh):
    body = gathered
    if mesh.shape["blk"] == 2 and mesh.shape["dof"] == 4:
        body = halved
    in_specs = (
        P("leaf", "blk", "dof", None, None),
        P("leaf", "dof", None, None),
        P("leaf", "dof", None, None),
        P("leaf", None, "blk"),
        P(),
    )
    out_specs = (P(None, "blk", None), P("blk", None), P("leaf", "blk", "dof", None, None))
    return jax.shard_map(body, mesh=mesh, in_specs=in_specs, out_specs=out_specs, check_vma=False)
```

```python
import functools
import jax
import jax.numpy as jnp
from jax import lax
from jax.experimental import pallas as pl
from jax.experimental.pallas import tpu as pltpu
from jax.sharding import PartitionSpec as P

SUB = 8
VMEM_BYTES = 48 * 1024 * 1024
LAST_BYTES = 16 * 1024 * 1024
PARTS = 5
SMALL = pl.CostEstimate(flops=1024, bytes_accessed=1024, transcendentals=0)


def params():
    return pltpu.CompilerParams(
        dimension_semantics=("arbitrary",), vmem_limit_bytes=VMEM_BYTES
    )


def split_rows(x):
    wide = x.astype(jnp.float32)
    rows, cells_y, cells_z = wide.shape
    parts = [
        wide[:, i * SUB : (i + 1) * SUB].reshape(rows * SUB, cells_z).astype(jnp.bfloat16)
        for i in range(cells_y // SUB)
    ]
    return jnp.concatenate(parts, axis=1)


def accumulate(total, left, right):
    total[...] += lax.dot_general(
        left, right, (((1,), (1,)), ((), ())), preferred_element_type=jnp.float32
    )


def same_row_sum(total):
    tall, wide = total.shape
    row = lax.broadcasted_iota(jnp.int32, (tall, wide), 0) % SUB
    col = lax.broadcasted_iota(jnp.int32, (tall, wide), 1) % SUB
    kept = jnp.where(row == col, total, 0.0).reshape(tall // SUB, SUB, wide)
    folded = jnp.sum(kept, axis=1)
    group = lax.broadcasted_iota(jnp.int32, (wide, wide // SUB), 0) // SUB
    pick = (group == lax.broadcasted_iota(jnp.int32, (wide, wide // SUB), 1)).astype(jnp.float32)
    return jnp.dot(folded, pick, precision=lax.Precision.HIGHEST, preferred_element_type=jnp.float32)


def stiff_kernel(own, prev, after, low, high, coefs, masses, order, stiff, gram, mass, total, flat, acc):
    layer, last = pl.program_id(0), pl.num_programs(0) - 1
    rows, _, cells_y, cells_z = own.shape

    @pl.when(layer == 0)
    def _():
        total[...] = jnp.zeros_like(total)
        acc[...] = jnp.zeros_like(acc)

    y = lax.broadcasted_iota(jnp.int32, (SUB, cells_y, cells_z), 1)
    z = lax.broadcasted_iota(jnp.int32, (SUB, cells_y, cells_z), 2)
    diagonal = 6.0 + coefs[0]
    density = masses[0]

    def group(g, carry):
        modes = pl.ds(g * SUB, SUB)
        field = own[modes, 0].astype(jnp.float32)
        before = jnp.where(layer == 0, low[modes, 0], prev[modes, 0]).astype(jnp.float32)
        behind = jnp.where(layer == last, high[modes, 0], after[modes, 0]).astype(jnp.float32)
        around = before + behind
        around += jnp.where(y == 0, 0.0, pltpu.roll(field, 1, 1))
        around += jnp.where(y == cells_y - 1, 0.0, pltpu.roll(field, cells_y - 1, 1))
        around += jnp.where(z == 0, 0.0, pltpu.roll(field, 1, 2))
        around += jnp.where(z == cells_z - 1, 0.0, pltpu.roll(field, cells_z - 1, 2))
        force = diagonal[None] * field - around
        weighed = (density[None] * field).astype(jnp.bfloat16).astype(jnp.float32) * field
        out = pl.ds(g * SUB * SUB, SUB * SUB)
        part = None
        for i in range(cells_y // SUB):
            rows_y, lanes = slice(i * SUB, (i + 1) * SUB), slice(i * cells_z, (i + 1) * cells_z)
            stiff[0, out, lanes] = force[:, rows_y].reshape(SUB * SUB, cells_z).astype(jnp.bfloat16)
            flat[out, lanes] = field[:, rows_y].reshape(SUB * SUB, cells_z).astype(jnp.bfloat16)
            part = weighed[:, rows_y] if part is None else part + weighed[:, rows_y]
        acc[modes] += part
        return carry

    lax.fori_loop(0, rows // SUB, group, 0)
    accumulate(total, stiff[0], flat[...])

    @pl.when(layer == last)
    def _():
        gram[...] = same_row_sum(total[...])
        column = jnp.sum(jnp.sum(acc[...], axis=1), axis=1, keepdims=True)
        mass[...] = jnp.broadcast_to(column, (rows, rows)).T[: mass.shape[0]]


def stiff_terms(own, low, high, coefs, masses, order):
    rows, layers, cells_y, cells_z = own.shape
    tall, wide = rows * SUB, cells_y // SUB * cells_z
    block = (rows, 1, cells_y, cells_z)
    cells = (1, cells_y, cells_z)
    return pl.pallas_call(
        stiff_kernel,
        grid=(layers,),
        in_specs=[
            pl.BlockSpec(block, lambda g: (0, g, 0, 0)),
            pl.BlockSpec(block, lambda g: (0, jnp.maximum(g - 1, 0), 0, 0)),
            pl.BlockSpec(block, lambda g: (0, jnp.minimum(g + 1, layers - 1), 0, 0)),
            pl.BlockSpec(block, lambda g: (0, 0, 0, 0)),
            pl.BlockSpec(block, lambda g: (0, 0, 0, 0)),
            pl.BlockSpec(cells, lambda g: (g, 0, 0)),
            pl.BlockSpec(cells, lambda g: (g, 0, 0)),
            pl.BlockSpec(memory_space=pl.ANY),
        ],
        out_specs=[
            pl.BlockSpec((1, tall, wide), lambda g: (g, 0, 0)),
            pl.BlockSpec((rows, rows), lambda g: (0, 0)),
            pl.BlockSpec((2 * SUB, rows), lambda g: (0, 0)),
        ],
        out_shape=[
            jax.ShapeDtypeStruct((layers, tall, wide), jnp.bfloat16),
            jax.ShapeDtypeStruct((rows, rows), jnp.float32),
            jax.ShapeDtypeStruct((2 * SUB, rows), jnp.float32),
        ],
        scratch_shapes=[
            pltpu.VMEM((tall, tall), jnp.float32),
            pltpu.VMEM((tall, wide), jnp.bfloat16),
            pltpu.VMEM((rows, SUB, cells_z), jnp.float32),
        ],
        compiler_params=params(),
        cost_estimate=SMALL,
        name="stiff_terms",
    )(own, own, own, low, high, coefs, masses, order)


def cross_kernel(at, skip, stiff, other, gram, total):
    step = pl.program_id(0)

    @pl.when(step == 0)
    def _():
        total[...] = jnp.zeros_like(total)

    accumulate(total, stiff[0], split_rows(other[:, 0]))

    @pl.when(step == pl.num_programs(0) - 1)
    def _():
        gram[...] = same_row_sum(total[...])


def cross_terms(stiff, other, at, skip, layers):
    rows, _, cells_y, cells_z = other.shape
    _, tall, wide = stiff.shape
    return pl.pallas_call(
        cross_kernel,
        grid_spec=pltpu.PrefetchScalarGridSpec(
            num_scalar_prefetch=2,
            grid=(layers,),
            in_specs=[
                pl.BlockSpec((1, tall, wide), lambda g, at, skip: (at[0] + g, 0, 0)),
                pl.BlockSpec((rows, 1, cells_y, cells_z), lambda g, at, skip: (0, skip[0] + g, 0, 0)),
            ],
            out_specs=pl.BlockSpec((rows, rows), lambda g, at, skip: (0, 0)),
            scratch_shapes=[pltpu.VMEM((tall, tall), jnp.float32)],
        ),
        out_shape=jax.ShapeDtypeStruct((rows, rows), jnp.float32),
        compiler_params=params(),
        cost_estimate=SMALL,
        name="cross_terms",
    )(at.reshape(1), skip.reshape(1), stiff, other)


def cut_kernel(at, whole, *rest):
    out, held, reads, writes = rest[-4:]
    pieces = held.shape[0]
    layers = out.shape[1]
    bounds = [layers * i // pieces for i in range(pieces + 1)]
    ins, outs = [], []
    for i in range(pieces):
        start, size = bounds[i], bounds[i + 1] - bounds[i]
        piece = held.at[i, :, pl.ds(0, size)]
        ins.append(
            pltpu.make_async_copy(whole.at[:, pl.ds(at[0] + start, size)], piece, reads.at[i])
        )
        outs.append(pltpu.make_async_copy(piece, out.at[:, pl.ds(start, size)], writes.at[i]))
    for copy in ins:
        copy.start()
    for i in range(pieces):
        ins[i].wait()
        outs[i].start()
    for copy in outs:
        copy.wait()


def cut(whole, at, count, *orders):
    rows, _, cells_y, cells_z = whole.shape
    pieces = min(4, count)
    longest = -(-count // pieces)
    return pl.pallas_call(
        cut_kernel,
        grid_spec=pltpu.PrefetchScalarGridSpec(
            num_scalar_prefetch=1,
            grid=(1,),
            in_specs=[pl.BlockSpec(memory_space=pl.ANY)] * (1 + len(orders)),
            out_specs=pl.BlockSpec(memory_space=pl.ANY),
            scratch_shapes=[
                pltpu.VMEM((pieces, rows, longest, cells_y, cells_z), whole.dtype),
                pltpu.SemaphoreType.DMA((pieces,)),
                pltpu.SemaphoreType.DMA((pieces,)),
            ],
        ),
        out_shape=jax.ShapeDtypeStruct((rows, count, cells_y, cells_z), whole.dtype),
        compiler_params=params(),
        cost_estimate=SMALL,
        name="cut",
    )(at.reshape(1), whole, *orders)


def merge_kernel(blk, whole, theirs, node, root):
    nodes, _, both = whole.shape
    rows = both // 2
    first = blk[0] == 0
    total = None
    for p in range(nodes):
        here = slice(p * rows, (p + 1) * rows)
        gram = whole[p, :rows, :rows]
        cross = whole[p, :rows, rows:] + theirs[:rows, here].T
        scale_gram = 1.0 / jnp.sqrt(whole[p, rows : rows + 1, :rows])
        scale_cross = 1.0 / jnp.sqrt(theirs[rows : rows + 1, here])
        scale = jnp.broadcast_to(scale_gram, (rows, rows)).T
        low, high = jnp.where(first, gram, cross), jnp.where(first, cross, gram)
        scale_low = jnp.where(first, scale_gram, scale_cross)
        scale_high = jnp.where(first, scale_cross, scale_gram)
        node[p, :, :rows] = low
        node[p, :, rows:] = high
        scaled = jnp.concatenate([scale * low * scale_low, scale * high * scale_high], axis=1)
        total = scaled if total is None else total + scaled
    root[...] = total


def merge(whole, theirs, blk):
    nodes, _, both = whole.shape
    rows = both // 2
    return pl.pallas_call(
        merge_kernel,
        grid_spec=pltpu.PrefetchScalarGridSpec(
            num_scalar_prefetch=1,
            grid=(1,),
            in_specs=[
                pl.BlockSpec(whole.shape, lambda g, blk: (0, 0, 0)),
                pl.BlockSpec(theirs.shape, lambda g, blk: (0, 0)),
            ],
            out_specs=[
                pl.BlockSpec((nodes, rows, 2 * rows), lambda g, blk: (0, 0, 0)),
                pl.BlockSpec((rows, 2 * rows), lambda g, blk: (0, 0)),
            ],
        ),
        out_shape=[
            jax.ShapeDtypeStruct((nodes, rows, 2 * rows), jnp.float32),
            jax.ShapeDtypeStruct((rows, 2 * rows), jnp.float32),
        ],
        compiler_params=params(),
        cost_estimate=SMALL,
        name="merge",
    )(blk.astype(jnp.int32).reshape(1), whole, theirs)


def spread_kernel(block, out):
    tall, wide = out.shape
    eigs, modes = block.shape

    def shape_of(rows, cols, dim):
        index = lax.broadcasted_iota(jnp.int32, (rows, cols), dim)
        near = lax.broadcasted_iota(jnp.int32, (rows, cols), 1 - dim)
        return (index // SUB == near).astype(jnp.bfloat16)

    wider = jnp.dot(block[...], shape_of(modes, wide, 1), preferred_element_type=jnp.float32)
    full = jnp.dot(
        shape_of(tall, eigs, 0), wider.astype(jnp.bfloat16), preferred_element_type=jnp.float32
    )
    row = lax.broadcasted_iota(jnp.int32, (tall, wide), 0) % SUB
    col = lax.broadcasted_iota(jnp.int32, (tall, wide), 1) % SUB
    out[...] = jnp.where(row == col, full, 0.0).astype(out.dtype)


def spread_blocks(block):
    eigs, modes = block.shape
    return pl.pallas_call(
        spread_kernel,
        out_shape=jax.ShapeDtypeStruct((eigs * SUB, modes * SUB), block.dtype),
        compiler_params=pltpu.CompilerParams(vmem_limit_bytes=VMEM_BYTES),
        cost_estimate=SMALL,
        name="spread_blocks",
    )(block)


def vector_kernel(at, spread, own, other, *rest):
    out = rest[-1]
    rows, _, cells_y, cells_z = own.shape
    both = jnp.concatenate([split_rows(own[:, 0]), split_rows(other[:, 0])], axis=0)
    made = jnp.dot(spread[...], both, preferred_element_type=jnp.float32)
    eigs = out.shape[0]
    parts = [
        made[:, i * cells_z : (i + 1) * cells_z].reshape(eigs, SUB, cells_z)
        for i in range(cells_y // SUB)
    ]
    out[:, 0] = jnp.concatenate(parts, axis=1).astype(out.dtype)


def expand(spread, own, other, at, held, *orders):
    rows, layers, cells_y, cells_z = other.shape
    eigs = spread.shape[0] // SUB
    inputs = [at.reshape(1), spread, own, other]
    specs = [
        pl.BlockSpec(spread.shape, lambda g, at: (0, 0)),
        pl.BlockSpec((rows, 1, cells_y, cells_z), lambda g, at: (0, at[0] + g, 0, 0)),
        pl.BlockSpec((rows, 1, cells_y, cells_z), lambda g, at: (0, g, 0, 0)),
    ]
    aliases = {}
    if held is not None:
        aliases = {len(inputs): 0}
        inputs.append(held)
    inputs += orders
    specs += [pl.BlockSpec(memory_space=pl.ANY)] * (len(inputs) - 1 - len(specs))
    return pl.pallas_call(
        vector_kernel,
        grid_spec=pltpu.PrefetchScalarGridSpec(
            num_scalar_prefetch=1,
            grid=(layers,),
            in_specs=specs,
            out_specs=pl.BlockSpec((eigs, 1, cells_y, cells_z), lambda g, at: (0, at[0] + g, 0, 0)),
        ),
        out_shape=jax.ShapeDtypeStruct((eigs,) + own.shape[1:], jnp.bfloat16),
        input_output_aliases=aliases,
        compiler_params=params(),
        cost_estimate=SMALL,
        name="expand",
    )(*inputs)


def last_kernel(at, spread, own, other, held, out, made, sems):
    rows, layers, cells_y, cells_z = own.shape
    eigs = out.shape[0]
    parts = made.shape[0]
    copies = []
    for layer in range(layers):
        both = jnp.concatenate([split_rows(own[:, layer]), split_rows(other[:, layer])], axis=0)
        for part in range(parts):
            size = eigs // parts
            some = jnp.dot(
                spread[part * size * SUB : (part + 1) * size * SUB],
                both,
                preferred_element_type=jnp.float32,
            )
            tiles = [
                some[:, i * cells_z : (i + 1) * cells_z].reshape(size, SUB, cells_z)
                for i in range(cells_y // SUB)
            ]
            made[part, :, layer] = jnp.concatenate(tiles, axis=1).astype(made.dtype)
            if layer == layers - 1:
                place = out.at[pl.ds(part * size, size), pl.ds(at[0], layers)]
                copies.append(pltpu.make_async_copy(made.at[part], place, sems.at[part]))
                copies[-1].start()
    for copy in copies:
        copy.wait()


def expand_last(spread, own, other, at, held):
    rows, layers, cells_y, cells_z = other.shape
    eigs, parts = spread.shape[0] // SUB, 2
    inside = pl.BlockSpec(memory_space=pltpu.VMEM)
    return pl.pallas_call(
        last_kernel,
        in_specs=[pl.BlockSpec(memory_space=pltpu.SMEM), inside, inside, inside, pl.BlockSpec(memory_space=pl.ANY)],
        out_specs=pl.BlockSpec(memory_space=pl.ANY),
        out_shape=jax.ShapeDtypeStruct(held.shape, held.dtype),
        scratch_shapes=[
            pltpu.VMEM((parts, eigs // parts, layers, cells_y, cells_z), held.dtype),
            pltpu.SemaphoreType.DMA((parts,)),
        ],
        input_output_aliases={4: 0},
        compiler_params=pltpu.CompilerParams(vmem_limit_bytes=LAST_BYTES),
        cost_estimate=SMALL,
        name="expand_last",
    )(at.reshape(1), spread, own, other, held)


def shares(total, parts):
    return [total // parts + (i < total % parts) for i in range(parts)]


def swap(x):
    return lax.ppermute(x, "blk", [(0, 1), (1, 0)])


def crossed(x):
    leaves, leaf = lax.axis_size("leaf"), lax.axis_index("leaf")
    pairs = [(2 * i + j, 2 * (i ^ (leaves // 2)) + 1 - j) for i in range(leaves) for j in range(2)]
    count = x.shape[0] // 2
    part = lax.dynamic_slice_in_dim(x, leaf % 2 * count, count, 0)
    part = lax.ppermute(part, ("leaf", "blk"), pairs)
    rest = lax.ppermute(part, "leaf", [(i, i ^ 1) for i in range(leaves)])
    return jnp.where(
        leaf % 2 == 0, jnp.concatenate([part, rest], 0), jnp.concatenate([rest, part], 0)
    )


def paired_sum(x, axis):
    size, step = lax.axis_size(axis), 1
    while step < size:
        x = x + lax.ppermute(x, axis, [(i, i ^ step) for i in range(size)])
        step *= 2
    return x


def line_sum(x, axis):
    x = x + lax.ppermute(x, axis, [(0, 1), (1, 0), (2, 3), (3, 2)])
    x = x + lax.ppermute(x, axis, [(1, 2), (2, 1)])
    outer = lax.ppermute(x, axis, [(1, 0), (2, 3)])
    place = lax.axis_index(axis)
    return jnp.where((place == 0) | (place == 3), outer, x)


def halved(modes, stiffness, density, eigen_blocks, parent):
    own = modes[0]
    rows, layers = own.shape[:2]
    half = layers // 2
    blk, dof, leaf = lax.axis_index("blk"), lax.axis_index("dof"), lax.axis_index("leaf")
    upper = (blk + dof) % 2

    def spot(offset, count, top):
        forward, back = half - 1 + offset, half + 1 - offset - count
        return jnp.where(top == 1, forward, back).astype(jnp.int32)

    def far_spot(offset, count, top):
        forward, back = half + 1 + offset, half - 1 - offset - count
        return jnp.where(top == 0, forward, back).astype(jnp.int32)

    def send(at, count, *orders):
        return swap(cut(own, at, count, *orders))

    last = half // 16
    middle = half // 8
    fars = [half - 1 - middle - last, middle, last]
    far_at = [sum(fars[:i]) for i in range(len(fars))]

    pair = own[:, half - 1 : half + 1]
    met = swap(pair)
    nears = shares(half - 1, PARTS)
    near_at = [2 + sum(nears[:i]) for i in range(len(nears))]
    near = [send(spot(o, n, 1 - upper), n) for o, n in zip(near_at, nears)]
    far = [send(far_spot(far_at[0], fars[0], 1 - upper), fars[0])]
    size = lax.axis_size("dof")
    low = lax.ppermute(own[:, -1:], "dof", [(i, i + 1) for i in range(size - 1)])
    high = lax.ppermute(own[:, :1], "dof", [(i + 1, i) for i in range(size - 1)])
    stiff, gram, mass = stiff_terms(own, low, high, stiffness[0], density[0], met)

    mine = lax.dynamic_slice_in_dim(eigen_blocks[0], blk * rows, rows, 0)
    other = lax.dynamic_slice_in_dim(eigen_blocks[0], (1 - blk) * rows, rows, 0)
    spread = spread_blocks(jnp.concatenate([mine, other], axis=0).T)

    across = functools.partial(
        lax.dot_general,
        dimension_numbers=(((1, 2), (1, 2)), ((), ())),
        preferred_element_type=jnp.float32,
    )
    border = across(pair[:, 0], met[:, 1]) - across(pair[:, 1], met[:, 0])
    cross = jnp.where(upper == 1, 0.5 * border, -0.5 * border)
    cross = cross + cross_terms(stiff, met, half - 1 + upper, upper, 1)
    for chunk, offset, count in zip(near, near_at, nears):
        at = spot(offset, count, upper)
        cross = cross + cross_terms(stiff, chunk, at, jnp.zeros_like(at), count)

    tops, masses = jnp.concatenate([gram, cross], axis=1), jnp.concatenate([mass, mass], axis=1)
    whole = line_sum(jnp.concatenate([tops, masses], axis=0), "dof")
    nodes = lax.axis_size("leaf") // 2
    belongs = (parent[leaf] == jnp.arange(nodes, dtype=jnp.int32)).astype(jnp.float32)
    whole = paired_sum(belongs[:, None, None] * whole[None], "leaf")
    theirs = crossed(jnp.concatenate([whole[p, :, rows:] for p in range(nodes)], axis=1))
    far += [send(far_spot(o, n, 1 - upper), n, whole) for o, n in zip(far_at[1:], fars[1:])]

    vectors = expand(spread, own, met, jnp.full_like(upper, half - 1), None)
    for chunk, offset, count in zip(near, near_at, nears):
        vectors = expand(spread, own, chunk, spot(offset, count, upper), vectors)
    node_stiffness, root_stiffness = merge(whole, theirs, blk)
    places = [far_spot(o, n, upper) for o, n in zip(far_at, fars)]
    order = (root_stiffness,)
    for chunk, at in zip(far[:-1], places[:-1]):
        vectors = expand(spread, own, chunk, at, vectors, *order)
        order = ()
    vectors = expand_last(spread, cut(own, places[-1], last, whole), far[-1], places[-1], vectors)
    return (node_stiffness, root_stiffness, vectors[None])


def extended(x, sides, width):
    for axis, dim in sides:
        size, length = (lax.axis_size(axis), x.shape[dim])
        up = [(i, (i + 1) % size) for i in range(size - 1)]
        down = [(j, i) for i, j in up]
        last = lax.slice_in_dim(x, length - width, length, axis=dim)
        leading = lax.slice_in_dim(x, 0, width, axis=dim)
        before = lax.ppermute(last, axis, up)
        after = lax.ppermute(leading, axis, down)
        x = jnp.concatenate([before, x, after], axis=dim)
    return x


def neighbours(padded):
    inner = padded[:, 1:-1]
    sides = jnp.pad(inner, ((0, 0), (0, 0), (1, 1), (1, 1)))
    total = padded[:, 2:] + padded[:, :-2]
    total = total + sides[:, :, 2:, 1:-1] + sides[:, :, :-2, 1:-1]
    total = total + sides[:, :, 1:-1, 2:] + sides[:, :, 1:-1, :-2]
    return total


def gathered(modes, stiffness, density, eigen_blocks, parent):
    own = modes[0]
    rows, cells_x, cells_y, cells_z = own.shape
    cells = cells_x * cells_y * cells_z
    total_modes = rows * lax.axis_size("blk")
    padded = extended(own, (("dof", 1),), 1).astype(jnp.float32)
    field = padded[:, 1:-1]
    stiff = ((6.0 + stiffness[0]) * field - neighbours(padded)).astype(jnp.bfloat16)
    stiff_flat = stiff.reshape(rows, cells)
    own_flat = own.reshape(rows, cells)
    mass_flat = density[0].reshape(cells)
    weighed_own = (mass_flat[None, :] * own_flat.astype(jnp.float32)).astype(jnp.bfloat16)
    diag_own = jnp.einsum("rc,rc->r", weighed_own, own_flat, preferred_element_type=jnp.float32)
    diagonal = lax.all_gather(diag_own, "blk", axis=0, tiled=True)
    blocks = eigen_blocks[0]
    eig_rows = blocks.shape[1]
    piece = lax.all_gather(own_flat, "blk", axis=0, tiled=True)
    columns = lax.dot_general(
        stiff_flat, piece, (((1,), (1,)), ((), ())), preferred_element_type=jnp.float32
    )
    reduced = columns
    vectors = lax.dot_general(
        blocks, piece, (((0,), (0,)), ((), ())), preferred_element_type=jnp.float32
    )
    reduced, vectors = (reduced, vectors)
    vector_flat = vectors.astype(jnp.bfloat16)
    leaf_vectors = vector_flat.reshape(1, eig_rows, cells_x, cells_y, cells_z)
    leaves = lax.axis_size("leaf")
    nodes = leaves // 2
    node_ids = jnp.arange(nodes, dtype=jnp.int32)
    halves = lax.axis_size("dof")
    gathered_rows, gathered_diag = (
        lax.all_gather(reduced[None], ("leaf", "dof"), axis=0, tiled=True),
        lax.all_gather(diagonal[None], ("leaf", "dof"), axis=0, tiled=True),
    )
    leaf_rows = jnp.sum(gathered_rows.reshape(leaves, halves, rows, total_modes), axis=1)
    leaf_diag = jnp.sum(gathered_diag.reshape(leaves, halves, total_modes), axis=1)
    onehot = (parent[:, None] == node_ids[None, :]).astype(jnp.float32)
    node_stiffness = jnp.einsum("lp,lij->pij", onehot, leaf_rows, precision=lax.Precision.HIGHEST)
    node_mass = jnp.einsum("lp,li->pi", onehot, leaf_diag, precision=lax.Precision.HIGHEST)
    scale = 1.0 / jnp.sqrt(node_mass)
    scale_own = lax.dynamic_slice_in_dim(scale, lax.axis_index("blk") * rows, rows, 1)
    root_stiffness = jnp.sum(scale_own[:, :, None] * node_stiffness * scale[:, None, :], axis=0)
    return (node_stiffness, root_stiffness, leaf_vectors)


def solution(mesh):
    body = gathered
    if dict(mesh.shape) == {"leaf": 4, "dof": 4, "blk": 2}:
        body = halved
    in_specs = (
        P("leaf", "blk", "dof", None, None),
        P("leaf", "dof", None, None),
        P("leaf", "dof", None, None),
        P("leaf", None, "blk"),
        P(),
    )
    out_specs = (P(None, "blk", None), P("blk", None), P("leaf", "blk", "dof", None, None))
    return jax.shard_map(body, mesh=mesh, in_specs=in_specs, out_specs=out_specs, check_vma=False)
```

```python
import functools
import jax
import jax.numpy as jnp
from jax import lax
from jax.experimental import pallas as pl
from jax.experimental.pallas import tpu as pltpu
from jax.sharding import PartitionSpec as P

SUB = 8
VMEM_BYTES = 48 * 1024 * 1024
LAST_BYTES = 16 * 1024 * 1024
PARTS = 5
SMALL = pl.CostEstimate(flops=1024, bytes_accessed=1024, transcendentals=0)


def params():
    return pltpu.CompilerParams(
        dimension_semantics=("arbitrary",), vmem_limit_bytes=VMEM_BYTES
    )


def split_rows(x):
    wide = x.astype(jnp.float32)
    rows, cells_y, cells_z = wide.shape
    parts = [
        wide[:, i * SUB : (i + 1) * SUB].reshape(rows * SUB, cells_z).astype(jnp.bfloat16)
        for i in range(cells_y // SUB)
    ]
    return jnp.concatenate(parts, axis=1)


def accumulate(total, left, right):
    total[...] += lax.dot_general(
        left, right, (((1,), (1,)), ((), ())), preferred_element_type=jnp.float32
    )


def same_row_sum(total):
    tall, wide = total.shape
    row = lax.broadcasted_iota(jnp.int32, (tall, wide), 0) % SUB
    col = lax.broadcasted_iota(jnp.int32, (tall, wide), 1) % SUB
    kept = jnp.where(row == col, total, 0.0).reshape(tall // SUB, SUB, wide)
    folded = jnp.sum(kept, axis=1)
    group = lax.broadcasted_iota(jnp.int32, (wide, wide // SUB), 0) // SUB
    pick = (group == lax.broadcasted_iota(jnp.int32, (wide, wide // SUB), 1)).astype(jnp.float32)
    return jnp.dot(folded, pick, precision=lax.Precision.HIGHEST, preferred_element_type=jnp.float32)


def stiff_kernel(own, prev, after, low, high, coefs, masses, order, stiff, gram, mass, total, flat, acc):
    layer, last = pl.program_id(0), pl.num_programs(0) - 1
    rows, _, cells_y, cells_z = own.shape

    @pl.when(layer == 0)
    def _():
        total[...] = jnp.zeros_like(total)
        acc[...] = jnp.zeros_like(acc)

    y = lax.broadcasted_iota(jnp.int32, (SUB, cells_y, cells_z), 1)
    z = lax.broadcasted_iota(jnp.int32, (SUB, cells_y, cells_z), 2)
    diagonal = 6.0 + coefs[0]
    density = masses[0]

    def group(g, carry):
        modes = pl.ds(g * SUB, SUB)
        field = own[modes, 0].astype(jnp.float32)
        before = jnp.where(layer == 0, low[modes, 0], prev[modes, 0]).astype(jnp.float32)
        behind = jnp.where(layer == last, high[modes, 0], after[modes, 0]).astype(jnp.float32)
        around = before + behind
        around += jnp.where(y == 0, 0.0, pltpu.roll(field, 1, 1))
        around += jnp.where(y == cells_y - 1, 0.0, pltpu.roll(field, cells_y - 1, 1))
        around += jnp.where(z == 0, 0.0, pltpu.roll(field, 1, 2))
        around += jnp.where(z == cells_z - 1, 0.0, pltpu.roll(field, cells_z - 1, 2))
        force = diagonal[None] * field - around
        weighed = (density[None] * field).astype(jnp.bfloat16).astype(jnp.float32) * field
        out = pl.ds(g * SUB * SUB, SUB * SUB)
        part = None
        for i in range(cells_y // SUB):
            rows_y, lanes = slice(i * SUB, (i + 1) * SUB), slice(i * cells_z, (i + 1) * cells_z)
            stiff[0, out, lanes] = force[:, rows_y].reshape(SUB * SUB, cells_z).astype(jnp.bfloat16)
            flat[out, lanes] = field[:, rows_y].reshape(SUB * SUB, cells_z).astype(jnp.bfloat16)
            part = weighed[:, rows_y] if part is None else part + weighed[:, rows_y]
        acc[modes] += part
        return carry

    lax.fori_loop(0, rows // SUB, group, 0)
    accumulate(total, stiff[0], flat[...])

    @pl.when(layer == last)
    def _():
        gram[...] = same_row_sum(total[...])
        column = jnp.sum(jnp.sum(acc[...], axis=1), axis=1, keepdims=True)
        mass[...] = jnp.broadcast_to(column, (rows, rows)).T[: mass.shape[0]]


def stiff_terms(own, low, high, coefs, masses, order):
    rows, layers, cells_y, cells_z = own.shape
    tall, wide = rows * SUB, cells_y // SUB * cells_z
    block = (rows, 1, cells_y, cells_z)
    cells = (1, cells_y, cells_z)
    return pl.pallas_call(
        stiff_kernel,
        grid=(layers,),
        in_specs=[
            pl.BlockSpec(block, lambda g: (0, g, 0, 0)),
            pl.BlockSpec(block, lambda g: (0, jnp.maximum(g - 1, 0), 0, 0)),
            pl.BlockSpec(block, lambda g: (0, jnp.minimum(g + 1, layers - 1), 0, 0)),
            pl.BlockSpec(block, lambda g: (0, 0, 0, 0)),
            pl.BlockSpec(block, lambda g: (0, 0, 0, 0)),
            pl.BlockSpec(cells, lambda g: (g, 0, 0)),
            pl.BlockSpec(cells, lambda g: (g, 0, 0)),
            pl.BlockSpec(memory_space=pl.ANY),
        ],
        out_specs=[
            pl.BlockSpec((1, tall, wide), lambda g: (g, 0, 0)),
            pl.BlockSpec((rows, rows), lambda g: (0, 0)),
            pl.BlockSpec((2 * SUB, rows), lambda g: (0, 0)),
        ],
        out_shape=[
            jax.ShapeDtypeStruct((layers, tall, wide), jnp.bfloat16),
            jax.ShapeDtypeStruct((rows, rows), jnp.float32),
            jax.ShapeDtypeStruct((2 * SUB, rows), jnp.float32),
        ],
        scratch_shapes=[
            pltpu.VMEM((tall, tall), jnp.float32),
            pltpu.VMEM((tall, wide), jnp.bfloat16),
            pltpu.VMEM((rows, SUB, cells_z), jnp.float32),
        ],
        compiler_params=params(),
        cost_estimate=SMALL,
        name="stiff_terms",
    )(own, own, own, low, high, coefs, masses, order)


def cross_kernel(at, skip, stiff, other, gram, total):
    step = pl.program_id(0)

    @pl.when(step == 0)
    def _():
        total[...] = jnp.zeros_like(total)

    accumulate(total, stiff[0], split_rows(other[:, 0]))

    @pl.when(step == pl.num_programs(0) - 1)
    def _():
        gram[...] = same_row_sum(total[...])


def cross_terms(stiff, other, at, skip, layers):
    rows, _, cells_y, cells_z = other.shape
    _, tall, wide = stiff.shape
    return pl.pallas_call(
        cross_kernel,
        grid_spec=pltpu.PrefetchScalarGridSpec(
            num_scalar_prefetch=2,
            grid=(layers,),
            in_specs=[
                pl.BlockSpec((1, tall, wide), lambda g, at, skip: (at[0] + g, 0, 0)),
                pl.BlockSpec((rows, 1, cells_y, cells_z), lambda g, at, skip: (0, skip[0] + g, 0, 0)),
            ],
            out_specs=pl.BlockSpec((rows, rows), lambda g, at, skip: (0, 0)),
            scratch_shapes=[pltpu.VMEM((tall, tall), jnp.float32)],
        ),
        out_shape=jax.ShapeDtypeStruct((rows, rows), jnp.float32),
        compiler_params=params(),
        cost_estimate=SMALL,
        name="cross_terms",
    )(at.reshape(1), skip.reshape(1), stiff, other)


def after_kernel(at, order, out):
    out[0] = at[0]


def after(at, order):
    return pl.pallas_call(
        after_kernel,
        in_specs=[pl.BlockSpec(memory_space=pltpu.SMEM), pl.BlockSpec(memory_space=pl.ANY)],
        out_specs=pl.BlockSpec(memory_space=pltpu.SMEM),
        out_shape=jax.ShapeDtypeStruct((1,), jnp.int32),
        cost_estimate=SMALL,
        name="after",
    )(at.reshape(1), order)[0]


def merge_kernel(blk, whole, theirs, node, root):
    nodes, _, both = whole.shape
    rows = both // 2
    first = blk[0] == 0
    total = None
    for p in range(nodes):
        here = slice(p * rows, (p + 1) * rows)
        gram = whole[p, :rows, :rows]
        cross = whole[p, :rows, rows:] + theirs[:rows, here].T
        scale_gram = 1.0 / jnp.sqrt(whole[p, rows : rows + 1, :rows])
        scale_cross = 1.0 / jnp.sqrt(theirs[rows : rows + 1, here])
        scale = jnp.broadcast_to(scale_gram, (rows, rows)).T
        low, high = jnp.where(first, gram, cross), jnp.where(first, cross, gram)
        scale_low = jnp.where(first, scale_gram, scale_cross)
        scale_high = jnp.where(first, scale_cross, scale_gram)
        node[p, :, :rows] = low
        node[p, :, rows:] = high
        scaled = jnp.concatenate([scale * low * scale_low, scale * high * scale_high], axis=1)
        total = scaled if total is None else total + scaled
    root[...] = total


def merge(whole, theirs, blk):
    nodes, _, both = whole.shape
    rows = both // 2
    return pl.pallas_call(
        merge_kernel,
        grid_spec=pltpu.PrefetchScalarGridSpec(
            num_scalar_prefetch=1,
            grid=(1,),
            in_specs=[
                pl.BlockSpec(whole.shape, lambda g, blk: (0, 0, 0)),
                pl.BlockSpec(theirs.shape, lambda g, blk: (0, 0)),
            ],
            out_specs=[
                pl.BlockSpec((nodes, rows, 2 * rows), lambda g, blk: (0, 0, 0)),
                pl.BlockSpec((rows, 2 * rows), lambda g, blk: (0, 0)),
            ],
        ),
        out_shape=[
            jax.ShapeDtypeStruct((nodes, rows, 2 * rows), jnp.float32),
            jax.ShapeDtypeStruct((rows, 2 * rows), jnp.float32),
        ],
        compiler_params=params(),
        cost_estimate=SMALL,
        name="merge",
    )(blk.astype(jnp.int32).reshape(1), whole, theirs)


def spread_kernel(block, out):
    tall, wide = out.shape
    eigs, modes = block.shape

    def shape_of(rows, cols, dim):
        index = lax.broadcasted_iota(jnp.int32, (rows, cols), dim)
        near = lax.broadcasted_iota(jnp.int32, (rows, cols), 1 - dim)
        return (index // SUB == near).astype(jnp.bfloat16)

    wider = jnp.dot(block[...], shape_of(modes, wide, 1), preferred_element_type=jnp.float32)
    full = jnp.dot(
        shape_of(tall, eigs, 0), wider.astype(jnp.bfloat16), preferred_element_type=jnp.float32
    )
    row = lax.broadcasted_iota(jnp.int32, (tall, wide), 0) % SUB
    col = lax.broadcasted_iota(jnp.int32, (tall, wide), 1) % SUB
    out[...] = jnp.where(row == col, full, 0.0).astype(out.dtype)


def spread_blocks(block):
    eigs, modes = block.shape
    return pl.pallas_call(
        spread_kernel,
        out_shape=jax.ShapeDtypeStruct((eigs * SUB, modes * SUB), block.dtype),
        compiler_params=pltpu.CompilerParams(vmem_limit_bytes=VMEM_BYTES),
        cost_estimate=SMALL,
        name="spread_blocks",
    )(block)


def vector_kernel(at, spread, own, other, *rest):
    out = rest[-1]
    rows, _, cells_y, cells_z = own.shape
    both = jnp.concatenate([split_rows(own[:, 0]), split_rows(other[:, 0])], axis=0)
    made = jnp.dot(spread[...], both, preferred_element_type=jnp.float32)
    eigs = out.shape[0]
    parts = [
        made[:, i * cells_z : (i + 1) * cells_z].reshape(eigs, SUB, cells_z)
        for i in range(cells_y // SUB)
    ]
    out[:, 0] = jnp.concatenate(parts, axis=1).astype(out.dtype)


def expand(spread, own, other, at, held, *orders):
    rows, layers, cells_y, cells_z = other.shape
    eigs = spread.shape[0] // SUB
    inputs = [at.reshape(1), spread, own, other]
    specs = [
        pl.BlockSpec(spread.shape, lambda g, at: (0, 0)),
        pl.BlockSpec((rows, 1, cells_y, cells_z), lambda g, at: (0, at[0] + g, 0, 0)),
        pl.BlockSpec((rows, 1, cells_y, cells_z), lambda g, at: (0, g, 0, 0)),
    ]
    aliases = {}
    if held is not None:
        aliases = {len(inputs): 0}
        inputs.append(held)
    inputs += orders
    specs += [pl.BlockSpec(memory_space=pl.ANY)] * (len(inputs) - 1 - len(specs))
    return pl.pallas_call(
        vector_kernel,
        grid_spec=pltpu.PrefetchScalarGridSpec(
            num_scalar_prefetch=1,
            grid=(layers,),
            in_specs=specs,
            out_specs=pl.BlockSpec((eigs, 1, cells_y, cells_z), lambda g, at: (0, at[0] + g, 0, 0)),
        ),
        out_shape=jax.ShapeDtypeStruct((eigs,) + own.shape[1:], jnp.bfloat16),
        input_output_aliases=aliases,
        compiler_params=params(),
        cost_estimate=SMALL,
        name="expand",
    )(*inputs)


def last_kernel(at, spread, own, other, held, out, made, sems):
    rows, layers, cells_y, cells_z = own.shape
    eigs = out.shape[0]
    parts = made.shape[0]
    copies = []
    for layer in range(layers):
        both = jnp.concatenate([split_rows(own[:, layer]), split_rows(other[:, layer])], axis=0)
        for part in range(parts):
            size = eigs // parts
            some = jnp.dot(
                spread[part * size * SUB : (part + 1) * size * SUB],
                both,
                preferred_element_type=jnp.float32,
            )
            tiles = [
                some[:, i * cells_z : (i + 1) * cells_z].reshape(size, SUB, cells_z)
                for i in range(cells_y // SUB)
            ]
            made[part, :, layer] = jnp.concatenate(tiles, axis=1).astype(made.dtype)
            if layer == layers - 1:
                place = out.at[pl.ds(part * size, size), pl.ds(at[0], layers)]
                copies.append(pltpu.make_async_copy(made.at[part], place, sems.at[part]))
                copies[-1].start()
    for copy in copies:
        copy.wait()


def expand_last(spread, own, other, at, held):
    rows, layers, cells_y, cells_z = other.shape
    eigs, parts = spread.shape[0] // SUB, 2
    inside = pl.BlockSpec(memory_space=pltpu.VMEM)
    return pl.pallas_call(
        last_kernel,
        in_specs=[pl.BlockSpec(memory_space=pltpu.SMEM), inside, inside, inside, pl.BlockSpec(memory_space=pl.ANY)],
        out_specs=pl.BlockSpec(memory_space=pl.ANY),
        out_shape=jax.ShapeDtypeStruct(held.shape, held.dtype),
        scratch_shapes=[
            pltpu.VMEM((parts, eigs // parts, layers, cells_y, cells_z), held.dtype),
            pltpu.SemaphoreType.DMA((parts,)),
        ],
        input_output_aliases={4: 0},
        compiler_params=pltpu.CompilerParams(vmem_limit_bytes=LAST_BYTES),
        cost_estimate=SMALL,
        name="expand_last",
    )(at.reshape(1), spread, own, other, held)


def shares(total, parts):
    return [total // parts + (i < total % parts) for i in range(parts)]


def swap(x):
    return lax.ppermute(x, "blk", [(0, 1), (1, 0)])


def crossed(x):
    leaves, leaf = lax.axis_size("leaf"), lax.axis_index("leaf")
    pairs = [(2 * i + j, 2 * (i ^ (leaves // 2)) + 1 - j) for i in range(leaves) for j in range(2)]
    count = x.shape[0] // 2
    part = lax.dynamic_slice_in_dim(x, leaf % 2 * count, count, 0)
    part = lax.ppermute(part, ("leaf", "blk"), pairs)
    rest = lax.ppermute(part, "leaf", [(i, i ^ 1) for i in range(leaves)])
    return jnp.where(
        leaf % 2 == 0, jnp.concatenate([part, rest], 0), jnp.concatenate([rest, part], 0)
    )


def paired_sum(x, axis):
    size, step = lax.axis_size(axis), 1
    while step < size:
        x = x + lax.ppermute(x, axis, [(i, i ^ step) for i in range(size)])
        step *= 2
    return x


def line_sum(x, axis):
    if lax.axis_size(axis) != 4:
        return lax.psum(x, axis)
    x = x + lax.ppermute(x, axis, [(0, 1), (1, 0), (2, 3), (3, 2)])
    x = x + lax.ppermute(x, axis, [(1, 2), (2, 1)])
    outer = lax.ppermute(x, axis, [(1, 0), (2, 3)])
    place = lax.axis_index(axis)
    return jnp.where((place == 0) | (place == 3), outer, x)


def halved(modes, stiffness, density, eigen_blocks, parent):
    own = modes[0]
    rows, layers = own.shape[:2]
    half = layers // 2
    blk, dof, leaf = lax.axis_index("blk"), lax.axis_index("dof"), lax.axis_index("leaf")
    upper = (blk + dof) % 2

    def spot(offset, count, top):
        forward, back = half - 1 + offset, half + 1 - offset - count
        return jnp.where(top == 1, forward, back).astype(jnp.int32)

    def far_spot(offset, count, top):
        forward, back = half + 1 + offset, half - 1 - offset - count
        return jnp.where(top == 0, forward, back).astype(jnp.int32)

    def cut(at, count):
        return lax.dynamic_slice_in_dim(own, at, count, axis=1)

    def send(at, count):
        return swap(cut(at, count))

    last = half // 16
    middle = half // 8
    fars = [half - 1 - middle - last, middle, last]
    far_at = [sum(fars[:i]) for i in range(len(fars))]

    pair = own[:, half - 1 : half + 1]
    met = swap(pair)
    nears = shares(half - 1, PARTS)
    near_at = [2 + sum(nears[:i]) for i in range(len(nears))]
    near = [send(spot(o, n, 1 - upper), n) for o, n in zip(near_at, nears)]
    far = [send(far_spot(far_at[0], fars[0], 1 - upper), fars[0])]
    size = lax.axis_size("dof")
    low = lax.ppermute(own[:, -1:], "dof", [(i, i + 1) for i in range(size - 1)])
    high = lax.ppermute(own[:, :1], "dof", [(i + 1, i) for i in range(size - 1)])
    stiff, gram, mass = stiff_terms(own, low, high, stiffness[0], density[0], met)

    mine = lax.dynamic_slice_in_dim(eigen_blocks[0], blk * rows, rows, 0)
    other = lax.dynamic_slice_in_dim(eigen_blocks[0], (1 - blk) * rows, rows, 0)
    spread = spread_blocks(jnp.concatenate([mine, other], axis=0).T)

    across = functools.partial(
        lax.dot_general,
        dimension_numbers=(((1, 2), (1, 2)), ((), ())),
        preferred_element_type=jnp.float32,
    )
    border = across(pair[:, 0], met[:, 1]) - across(pair[:, 1], met[:, 0])
    cross = jnp.where(upper == 1, 0.5 * border, -0.5 * border)
    cross = cross + cross_terms(stiff, met, half - 1 + upper, upper, 1)
    for chunk, offset, count in zip(near, near_at, nears):
        at = spot(offset, count, upper)
        cross = cross + cross_terms(stiff, chunk, at, jnp.zeros_like(at), count)

    tops, masses = jnp.concatenate([gram, cross], axis=1), jnp.concatenate([mass, mass], axis=1)
    whole = line_sum(jnp.concatenate([tops, masses], axis=0), "dof")
    nodes = lax.axis_size("leaf") // 2
    belongs = (parent[leaf] == jnp.arange(nodes, dtype=jnp.int32)).astype(jnp.float32)
    whole = paired_sum(belongs[:, None, None] * whole[None], "leaf")
    theirs = crossed(jnp.concatenate([whole[p, :, rows:] for p in range(nodes)], axis=1))
    far += [send(after(far_spot(o, n, 1 - upper), whole), n) for o, n in zip(far_at[1:], fars[1:])]

    vectors = expand(spread, own, met, jnp.full_like(upper, half - 1), None)
    for chunk, offset, count in zip(near, near_at, nears):
        vectors = expand(spread, own, chunk, spot(offset, count, upper), vectors)
    node_stiffness, root_stiffness = merge(whole, theirs, blk)
    places = [far_spot(o, n, upper) for o, n in zip(far_at, fars)]
    order = (root_stiffness,)
    for chunk, at in zip(far[:-1], places[:-1]):
        vectors = expand(spread, own, chunk, at, vectors, *order)
        order = ()
    vectors = expand_last(spread, cut(after(places[-1], whole), last), far[-1], places[-1], vectors)
    return (node_stiffness, root_stiffness, vectors[None])


def extended(x, sides, width):
    for axis, dim in sides:
        size, length = (lax.axis_size(axis), x.shape[dim])
        up = [(i, (i + 1) % size) for i in range(size - 1)]
        down = [(j, i) for i, j in up]
        last = lax.slice_in_dim(x, length - width, length, axis=dim)
        leading = lax.slice_in_dim(x, 0, width, axis=dim)
        before = lax.ppermute(last, axis, up)
        after = lax.ppermute(leading, axis, down)
        x = jnp.concatenate([before, x, after], axis=dim)
    return x


def neighbours(padded):
    inner = padded[:, 1:-1]
    sides = jnp.pad(inner, ((0, 0), (0, 0), (1, 1), (1, 1)))
    total = padded[:, 2:] + padded[:, :-2]
    total = total + sides[:, :, 2:, 1:-1] + sides[:, :, :-2, 1:-1]
    total = total + sides[:, :, 1:-1, 2:] + sides[:, :, 1:-1, :-2]
    return total


def gathered(modes, stiffness, density, eigen_blocks, parent):
    own = modes[0]
    rows, cells_x, cells_y, cells_z = own.shape
    cells = cells_x * cells_y * cells_z
    total_modes = rows * lax.axis_size("blk")
    padded = extended(own, (("dof", 1),), 1).astype(jnp.float32)
    field = padded[:, 1:-1]
    stiff = ((6.0 + stiffness[0]) * field - neighbours(padded)).astype(jnp.bfloat16)
    stiff_flat = stiff.reshape(rows, cells)
    own_flat = own.reshape(rows, cells)
    mass_flat = density[0].reshape(cells)
    weighed_own = (mass_flat[None, :] * own_flat.astype(jnp.float32)).astype(jnp.bfloat16)
    diag_own = jnp.einsum("rc,rc->r", weighed_own, own_flat, preferred_element_type=jnp.float32)
    diagonal = lax.all_gather(diag_own, "blk", axis=0, tiled=True)
    blocks = eigen_blocks[0]
    eig_rows = blocks.shape[1]
    piece = lax.all_gather(own_flat, "blk", axis=0, tiled=True)
    columns = lax.dot_general(
        stiff_flat, piece, (((1,), (1,)), ((), ())), preferred_element_type=jnp.float32
    )
    reduced = columns
    vectors = lax.dot_general(
        blocks, piece, (((0,), (0,)), ((), ())), preferred_element_type=jnp.float32
    )
    reduced, vectors = (reduced, vectors)
    vector_flat = vectors.astype(jnp.bfloat16)
    leaf_vectors = vector_flat.reshape(1, eig_rows, cells_x, cells_y, cells_z)
    leaves = lax.axis_size("leaf")
    nodes = leaves // 2
    node_ids = jnp.arange(nodes, dtype=jnp.int32)
    halves = lax.axis_size("dof")
    gathered_rows, gathered_diag = (
        lax.all_gather(reduced[None], ("leaf", "dof"), axis=0, tiled=True),
        lax.all_gather(diagonal[None], ("leaf", "dof"), axis=0, tiled=True),
    )
    leaf_rows = jnp.sum(gathered_rows.reshape(leaves, halves, rows, total_modes), axis=1)
    leaf_diag = jnp.sum(gathered_diag.reshape(leaves, halves, total_modes), axis=1)
    onehot = (parent[:, None] == node_ids[None, :]).astype(jnp.float32)
    node_stiffness = jnp.einsum("lp,lij->pij", onehot, leaf_rows, precision=lax.Precision.HIGHEST)
    node_mass = jnp.einsum("lp,li->pi", onehot, leaf_diag, precision=lax.Precision.HIGHEST)
    scale = 1.0 / jnp.sqrt(node_mass)
    scale_own = lax.dynamic_slice_in_dim(scale, lax.axis_index("blk") * rows, rows, 1)
    root_stiffness = jnp.sum(scale_own[:, :, None] * node_stiffness * scale[:, None, :], axis=0)
    return (node_stiffness, root_stiffness, leaf_vectors)


def body(modes, *others):
    leaves = lax.axis_size("leaf")
    paired = leaves >= 4 and leaves & (leaves - 1) == 0
    layers, cells_y = modes.shape[2:4]
    fits = layers % 2 == 0 and layers >= 32 and cells_y % SUB == 0 and modes.shape[1] % SUB == 0
    if lax.axis_size("blk") == 2 and paired and fits:
        return halved(modes, *others)
    return gathered(modes, *others)


def solution(mesh):
    in_specs = (
        P("leaf", "blk", "dof", None, None),
        P("leaf", "dof", None, None),
        P("leaf", "dof", None, None),
        P("leaf", None, "blk"),
        P(),
    )
    out_specs = (P(None, "blk", None), P("blk", None), P("leaf", "blk", "dof", None, None))
    return jax.shard_map(body, mesh=mesh, in_specs=in_specs, out_specs=out_specs, check_vma=False)
```

```python
import functools
import jax
import jax.numpy as jnp
from jax import lax
from jax.experimental import pallas as pl
from jax.experimental.pallas import tpu as pltpu
from jax.sharding import PartitionSpec as P

SUB = 8
VMEM_BYTES = 48 * 1024 * 1024
LAST_BYTES = 16 * 1024 * 1024
PARTS = 5
SMALL = pl.CostEstimate(flops=1024, bytes_accessed=1024, transcendentals=0)


def params():
    return pltpu.CompilerParams(
        dimension_semantics=("arbitrary",), vmem_limit_bytes=VMEM_BYTES
    )


def split_rows(x):
    wide = x.astype(jnp.float32)
    rows, cells_y, cells_z = wide.shape
    parts = [
        wide[:, i * SUB : (i + 1) * SUB].reshape(rows * SUB, cells_z).astype(jnp.bfloat16)
        for i in range(cells_y // SUB)
    ]
    return jnp.concatenate(parts, axis=1)


def accumulate(total, left, right):
    total[...] += lax.dot_general(
        left, right, (((1,), (1,)), ((), ())), preferred_element_type=jnp.float32
    )


def same_row_sum(total):
    tall, wide = total.shape
    row = lax.broadcasted_iota(jnp.int32, (tall, wide), 0) % SUB
    col = lax.broadcasted_iota(jnp.int32, (tall, wide), 1) % SUB
    kept = jnp.where(row == col, total, 0.0).reshape(tall // SUB, SUB, wide)
    folded = jnp.sum(kept, axis=1)
    group = lax.broadcasted_iota(jnp.int32, (wide, wide // SUB), 0) // SUB
    pick = (group == lax.broadcasted_iota(jnp.int32, (wide, wide // SUB), 1)).astype(jnp.float32)
    return jnp.dot(folded, pick, precision=lax.Precision.HIGHEST, preferred_element_type=jnp.float32)


def stiff_kernel(own, prev, after, low, high, coefs, masses, order, stiff, gram, mass, total, flat, acc):
    layer, last = pl.program_id(0), pl.num_programs(0) - 1
    rows, _, cells_y, cells_z = own.shape

    @pl.when(layer == 0)
    def _():
        total[...] = jnp.zeros_like(total)
        acc[...] = jnp.zeros_like(acc)

    y = lax.broadcasted_iota(jnp.int32, (SUB, cells_y, cells_z), 1)
    z = lax.broadcasted_iota(jnp.int32, (SUB, cells_y, cells_z), 2)
    diagonal = 6.0 + coefs[0]
    density = masses[0]

    def group(g, carry):
        modes = pl.ds(g * SUB, SUB)
        field = own[modes, 0].astype(jnp.float32)
        before = jnp.where(layer == 0, low[modes, 0], prev[modes, 0]).astype(jnp.float32)
        behind = jnp.where(layer == last, high[modes, 0], after[modes, 0]).astype(jnp.float32)
        around = before + behind
        around += jnp.where(y == 0, 0.0, pltpu.roll(field, 1, 1))
        around += jnp.where(y == cells_y - 1, 0.0, pltpu.roll(field, cells_y - 1, 1))
        around += jnp.where(z == 0, 0.0, pltpu.roll(field, 1, 2))
        around += jnp.where(z == cells_z - 1, 0.0, pltpu.roll(field, cells_z - 1, 2))
        force = diagonal[None] * field - around
        weighed = (density[None] * field).astype(jnp.bfloat16).astype(jnp.float32) * field
        out = pl.ds(g * SUB * SUB, SUB * SUB)
        part = None
        for i in range(cells_y // SUB):
            rows_y, lanes = slice(i * SUB, (i + 1) * SUB), slice(i * cells_z, (i + 1) * cells_z)
            stiff[0, out, lanes] = force[:, rows_y].reshape(SUB * SUB, cells_z).astype(jnp.bfloat16)
            flat[out, lanes] = field[:, rows_y].reshape(SUB * SUB, cells_z).astype(jnp.bfloat16)
            part = weighed[:, rows_y] if part is None else part + weighed[:, rows_y]
        acc[modes] += part
        return carry

    lax.fori_loop(0, rows // SUB, group, 0)
    accumulate(total, stiff[0], flat[...])

    @pl.when(layer == last)
    def _():
        gram[...] = same_row_sum(total[...])
        column = jnp.sum(jnp.sum(acc[...], axis=1), axis=1, keepdims=True)
        mass[...] = jnp.broadcast_to(column, (rows, rows)).T[: mass.shape[0]]


def stiff_terms(own, low, high, coefs, masses, order):
    rows, layers, cells_y, cells_z = own.shape
    tall, wide = rows * SUB, cells_y // SUB * cells_z
    block = (rows, 1, cells_y, cells_z)
    cells = (1, cells_y, cells_z)
    return pl.pallas_call(
        stiff_kernel,
        grid=(layers,),
        in_specs=[
            pl.BlockSpec(block, lambda g: (0, g, 0, 0)),
            pl.BlockSpec(block, lambda g: (0, jnp.maximum(g - 1, 0), 0, 0)),
            pl.BlockSpec(block, lambda g: (0, jnp.minimum(g + 1, layers - 1), 0, 0)),
            pl.BlockSpec(block, lambda g: (0, 0, 0, 0)),
            pl.BlockSpec(block, lambda g: (0, 0, 0, 0)),
            pl.BlockSpec(cells, lambda g: (g, 0, 0)),
            pl.BlockSpec(cells, lambda g: (g, 0, 0)),
            pl.BlockSpec(memory_space=pl.ANY),
        ],
        out_specs=[
            pl.BlockSpec((1, tall, wide), lambda g: (g, 0, 0)),
            pl.BlockSpec((rows, rows), lambda g: (0, 0)),
            pl.BlockSpec((2 * SUB, rows), lambda g: (0, 0)),
        ],
        out_shape=[
            jax.ShapeDtypeStruct((layers, tall, wide), jnp.bfloat16),
            jax.ShapeDtypeStruct((rows, rows), jnp.float32),
            jax.ShapeDtypeStruct((2 * SUB, rows), jnp.float32),
        ],
        scratch_shapes=[
            pltpu.VMEM((tall, tall), jnp.float32),
            pltpu.VMEM((tall, wide), jnp.bfloat16),
            pltpu.VMEM((rows, SUB, cells_z), jnp.float32),
        ],
        compiler_params=params(),
        cost_estimate=SMALL,
        name="stiff_terms",
    )(own, own, own, low, high, coefs, masses, order)


def cross_kernel(at, skip, stiff, other, order, gram, total):
    step = pl.program_id(0)

    @pl.when(step == 0)
    def _():
        total[...] = jnp.zeros_like(total)

    accumulate(total, stiff[0], split_rows(other[:, 0]))

    @pl.when(step == pl.num_programs(0) - 1)
    def _():
        gram[...] = same_row_sum(total[...])


def cross_terms(stiff, other, at, skip, layers, order):
    rows, _, cells_y, cells_z = other.shape
    _, tall, wide = stiff.shape
    return pl.pallas_call(
        cross_kernel,
        grid_spec=pltpu.PrefetchScalarGridSpec(
            num_scalar_prefetch=2,
            grid=(layers,),
            in_specs=[
                pl.BlockSpec((1, tall, wide), lambda g, at, skip: (at[0] + g, 0, 0)),
                pl.BlockSpec((rows, 1, cells_y, cells_z), lambda g, at, skip: (0, skip[0] + g, 0, 0)),
                pl.BlockSpec(memory_space=pl.ANY),
            ],
            out_specs=pl.BlockSpec((rows, rows), lambda g, at, skip: (0, 0)),
            scratch_shapes=[pltpu.VMEM((tall, tall), jnp.float32)],
        ),
        out_shape=jax.ShapeDtypeStruct((rows, rows), jnp.float32),
        compiler_params=params(),
        cost_estimate=SMALL,
        name="cross_terms",
    )(at.reshape(1), skip.reshape(1), stiff, other, order)


def cut_kernel(at, whole, *rest):
    out, held, reads, writes = rest[-4:]
    pieces = held.shape[0]
    layers = out.shape[1]
    bounds = [layers * i // pieces for i in range(pieces + 1)]
    ins, outs = [], []
    for i in range(pieces):
        start, size = bounds[i], bounds[i + 1] - bounds[i]
        piece = held.at[i, :, pl.ds(0, size)]
        ins.append(
            pltpu.make_async_copy(whole.at[:, pl.ds(at[0] + start, size)], piece, reads.at[i])
        )
        outs.append(pltpu.make_async_copy(piece, out.at[:, pl.ds(start, size)], writes.at[i]))
    for copy in ins:
        copy.start()
    for i in range(pieces):
        ins[i].wait()
        outs[i].start()
    for copy in outs:
        copy.wait()


def cut(whole, at, count, *orders):
    rows, _, cells_y, cells_z = whole.shape
    pieces = min(4, count)
    longest = -(-count // pieces)
    return pl.pallas_call(
        cut_kernel,
        grid_spec=pltpu.PrefetchScalarGridSpec(
            num_scalar_prefetch=1,
            grid=(1,),
            in_specs=[pl.BlockSpec(memory_space=pl.ANY)] * (1 + len(orders)),
            out_specs=pl.BlockSpec(memory_space=pl.ANY),
            scratch_shapes=[
                pltpu.VMEM((pieces, rows, longest, cells_y, cells_z), whole.dtype),
                pltpu.SemaphoreType.DMA((pieces,)),
                pltpu.SemaphoreType.DMA((pieces,)),
            ],
        ),
        out_shape=jax.ShapeDtypeStruct((rows, count, cells_y, cells_z), whole.dtype),
        compiler_params=params(),
        cost_estimate=SMALL,
        name="cut",
    )(at.reshape(1), whole, *orders)


def cut_middle_kernel(start, whole, out, held, reads, writes):
    layers = out.shape[1]
    ins, outs = [], []
    for i in range(layers):
        piece = held.at[:, pl.ds(i, 1)]
        ins.append(pltpu.make_async_copy(whole.at[:, pl.ds(start + i, 1)], piece, reads.at[i]))
        outs.append(pltpu.make_async_copy(piece, out.at[:, pl.ds(i, 1)], writes.at[i]))
    for copy in ins:
        copy.start()
    for i in range(layers):
        ins[i].wait()
        outs[i].start()
    for copy in outs:
        copy.wait()


def cut_middle(whole, count):
    rows, layers, cells_y, cells_z = whole.shape
    shape = (rows, count, cells_y, cells_z)
    return pl.pallas_call(
        functools.partial(cut_middle_kernel, (layers - count) // 2),
        in_specs=[pl.BlockSpec(memory_space=pl.ANY)],
        out_specs=pl.BlockSpec(memory_space=pl.ANY),
        scratch_shapes=[
            pltpu.VMEM(shape, whole.dtype),
            pltpu.SemaphoreType.DMA((count,)),
            pltpu.SemaphoreType.DMA((count,)),
        ],
        out_shape=jax.ShapeDtypeStruct(shape, whole.dtype),
        compiler_params=pltpu.CompilerParams(vmem_limit_bytes=VMEM_BYTES),
        cost_estimate=SMALL,
        name="cut_middle",
    )(whole)


def merge_kernel(blk, whole, theirs, node, root):
    nodes, _, both = whole.shape
    rows = both // 2
    first = blk[0] == 0
    total = None
    for p in range(nodes):
        here = slice(p * rows, (p + 1) * rows)
        gram = whole[p, :rows, :rows]
        cross = whole[p, :rows, rows:] + theirs[:rows, here].T
        scale_gram = 1.0 / jnp.sqrt(whole[p, rows : rows + 1, :rows])
        scale_cross = 1.0 / jnp.sqrt(theirs[rows : rows + 1, here])
        scale = jnp.broadcast_to(scale_gram, (rows, rows)).T
        low, high = jnp.where(first, gram, cross), jnp.where(first, cross, gram)
        scale_low = jnp.where(first, scale_gram, scale_cross)
        scale_high = jnp.where(first, scale_cross, scale_gram)
        node[p, :, :rows] = low
        node[p, :, rows:] = high
        scaled = jnp.concatenate([scale * low * scale_low, scale * high * scale_high], axis=1)
        total = scaled if total is None else total + scaled
    root[...] = total


def merge(whole, theirs, blk):
    nodes, _, both = whole.shape
    rows = both // 2
    return pl.pallas_call(
        merge_kernel,
        grid_spec=pltpu.PrefetchScalarGridSpec(
            num_scalar_prefetch=1,
            grid=(1,),
            in_specs=[
                pl.BlockSpec(whole.shape, lambda g, blk: (0, 0, 0)),
                pl.BlockSpec(theirs.shape, lambda g, blk: (0, 0)),
            ],
            out_specs=[
                pl.BlockSpec((nodes, rows, 2 * rows), lambda g, blk: (0, 0, 0)),
                pl.BlockSpec((rows, 2 * rows), lambda g, blk: (0, 0)),
            ],
        ),
        out_shape=[
            jax.ShapeDtypeStruct((nodes, rows, 2 * rows), jnp.float32),
            jax.ShapeDtypeStruct((rows, 2 * rows), jnp.float32),
        ],
        compiler_params=params(),
        cost_estimate=SMALL,
        name="merge",
    )(blk.astype(jnp.int32).reshape(1), whole, theirs)


def spread_kernel(block, out):
    tall, wide = out.shape
    eigs, modes = block.shape

    def shape_of(rows, cols, dim):
        index = lax.broadcasted_iota(jnp.int32, (rows, cols), dim)
        near = lax.broadcasted_iota(jnp.int32, (rows, cols), 1 - dim)
        return (index // SUB == near).astype(jnp.bfloat16)

    wider = jnp.dot(block[...], shape_of(modes, wide, 1), preferred_element_type=jnp.float32)
    full = jnp.dot(
        shape_of(tall, eigs, 0), wider.astype(jnp.bfloat16), preferred_element_type=jnp.float32
    )
    row = lax.broadcasted_iota(jnp.int32, (tall, wide), 0) % SUB
    col = lax.broadcasted_iota(jnp.int32, (tall, wide), 1) % SUB
    out[...] = jnp.where(row == col, full, 0.0).astype(out.dtype)


def spread_blocks(block):
    eigs, modes = block.shape
    return pl.pallas_call(
        spread_kernel,
        out_shape=jax.ShapeDtypeStruct((eigs * SUB, modes * SUB), block.dtype),
        compiler_params=pltpu.CompilerParams(vmem_limit_bytes=VMEM_BYTES),
        cost_estimate=SMALL,
        name="spread_blocks",
    )(block)


def vector_kernel(at, spread, own, other, *rest):
    out, done = rest[-2:]
    done[...] = jnp.zeros_like(done)
    rows, _, cells_y, cells_z = own.shape
    both = jnp.concatenate([split_rows(own[:, 0]), split_rows(other[:, 0])], axis=0)
    made = jnp.dot(spread[...], both, preferred_element_type=jnp.float32)
    eigs = out.shape[0]
    parts = [
        made[:, i * cells_z : (i + 1) * cells_z].reshape(eigs, SUB, cells_z)
        for i in range(cells_y // SUB)
    ]
    out[:, 0] = jnp.concatenate(parts, axis=1).astype(out.dtype)


def expand(spread, own, other, at, held, *orders):
    rows, layers, cells_y, cells_z = other.shape
    eigs = spread.shape[0] // SUB
    inputs = [at.reshape(1), spread, own, other]
    specs = [
        pl.BlockSpec(spread.shape, lambda g, at: (0, 0)),
        pl.BlockSpec((rows, 1, cells_y, cells_z), lambda g, at: (0, at[0] + g, 0, 0)),
        pl.BlockSpec((rows, 1, cells_y, cells_z), lambda g, at: (0, g, 0, 0)),
    ]
    aliases = {}
    if held is not None:
        aliases = {len(inputs): 0}
        inputs.append(held)
    inputs += orders
    specs += [pl.BlockSpec(memory_space=pl.ANY)] * (len(inputs) - 1 - len(specs))
    return pl.pallas_call(
        vector_kernel,
        grid_spec=pltpu.PrefetchScalarGridSpec(
            num_scalar_prefetch=1,
            grid=(layers,),
            in_specs=specs,
            out_specs=[
                pl.BlockSpec((eigs, 1, cells_y, cells_z), lambda g, at: (0, at[0] + g, 0, 0)),
                pl.BlockSpec((SUB, cells_z), lambda g, at: (0, 0)),
            ],
        ),
        out_shape=[
            jax.ShapeDtypeStruct((eigs,) + own.shape[1:], jnp.bfloat16),
            jax.ShapeDtypeStruct((SUB, cells_z), jnp.float32),
        ],
        input_output_aliases=aliases,
        compiler_params=params(),
        cost_estimate=SMALL,
        name="expand",
    )(*inputs)


def last_kernel(at, spread, own, other, held, out, made, sems):
    rows, layers, cells_y, cells_z = own.shape
    eigs = out.shape[0]
    parts = made.shape[0]
    copies = []
    for layer in range(layers):
        both = jnp.concatenate([split_rows(own[:, layer]), split_rows(other[:, layer])], axis=0)
        for part in range(parts):
            size = eigs // parts
            some = jnp.dot(
                spread[part * size * SUB : (part + 1) * size * SUB],
                both,
                preferred_element_type=jnp.float32,
            )
            tiles = [
                some[:, i * cells_z : (i + 1) * cells_z].reshape(size, SUB, cells_z)
                for i in range(cells_y // SUB)
            ]
            made[part, :, layer] = jnp.concatenate(tiles, axis=1).astype(made.dtype)
            if layer == layers - 1:
                place = out.at[pl.ds(part * size, size), pl.ds(at[0], layers)]
                copies.append(pltpu.make_async_copy(made.at[part], place, sems.at[part]))
                copies[-1].start()
    for copy in copies:
        copy.wait()


def expand_last(spread, own, other, at, held):
    rows, layers, cells_y, cells_z = other.shape
    eigs, parts = spread.shape[0] // SUB, 2
    inside = pl.BlockSpec(memory_space=pltpu.VMEM)
    return pl.pallas_call(
        last_kernel,
        in_specs=[pl.BlockSpec(memory_space=pltpu.SMEM), inside, inside, inside, pl.BlockSpec(memory_space=pl.ANY)],
        out_specs=pl.BlockSpec(memory_space=pl.ANY),
        out_shape=jax.ShapeDtypeStruct(held.shape, held.dtype),
        scratch_shapes=[
            pltpu.VMEM((parts, eigs // parts, layers, cells_y, cells_z), held.dtype),
            pltpu.SemaphoreType.DMA((parts,)),
        ],
        input_output_aliases={4: 0},
        compiler_params=pltpu.CompilerParams(vmem_limit_bytes=LAST_BYTES),
        cost_estimate=SMALL,
        name="expand_last",
    )(at.reshape(1), spread, own, other, held)


def shares(total, parts):
    return [total // parts + (i < total % parts) for i in range(parts)]


def swap(x):
    return lax.ppermute(x, "blk", [(0, 1), (1, 0)])


def crossed(x):
    leaves, leaf = lax.axis_size("leaf"), lax.axis_index("leaf")
    pairs = [(2 * i + j, 2 * (i ^ (leaves // 2)) + 1 - j) for i in range(leaves) for j in range(2)]
    count = x.shape[0] // 2
    part = lax.dynamic_slice_in_dim(x, leaf % 2 * count, count, 0)
    part = lax.ppermute(part, ("leaf", "blk"), pairs)
    rest = lax.ppermute(part, "leaf", [(i, i ^ 1) for i in range(leaves)])
    return jnp.where(
        leaf % 2 == 0, jnp.concatenate([part, rest], 0), jnp.concatenate([rest, part], 0)
    )


def paired_sum(x, axis):
    size, step = lax.axis_size(axis), 1
    while step < size:
        x = x + lax.ppermute(x, axis, [(i, i ^ step) for i in range(size)])
        step *= 2
    return x


def line_sum(x, axis):
    if lax.axis_size(axis) != 4:
        return lax.psum(x, axis)
    x = x + lax.ppermute(x, axis, [(0, 1), (1, 0), (2, 3), (3, 2)])
    x = x + lax.ppermute(x, axis, [(1, 2), (2, 1)])
    outer = lax.ppermute(x, axis, [(1, 0), (2, 3)])
    place = lax.axis_index(axis)
    return jnp.where((place == 0) | (place == 3), outer, x)


def halved(modes, stiffness, density, eigen_blocks, parent):
    own = modes[0]
    rows, layers = own.shape[:2]
    half = layers // 2
    blk, dof, leaf = lax.axis_index("blk"), lax.axis_index("dof"), lax.axis_index("leaf")
    upper = (blk + dof) % 2

    def spot(offset, count, top):
        forward, back = half - 1 + offset, half + 1 - offset - count
        return jnp.where(top == 1, forward, back).astype(jnp.int32)

    def far_spot(offset, count, top):
        forward, back = half + 1 + offset, half - 1 - offset - count
        return jnp.where(top == 0, forward, back).astype(jnp.int32)

    def send(at, count, *orders):
        return swap(cut(own, at, count, *orders))

    last, middle, reach = half // 16, half // 8, half // 8
    fars = [half - reach - middle - last, middle, last]
    far_at = [reach - 1 + sum(fars[:i]) for i in range(len(fars))]
    nears = shares(half - reach, PARTS)
    near_at = [reach + 1 + sum(nears[:i]) for i in range(len(nears))]

    core = cut_middle(own, 2 * reach)
    met = swap(core)
    near = [send(spot(o, n, 1 - upper), n, core) for o, n in zip(near_at, nears)]
    far = [send(far_spot(far_at[0], fars[0], 1 - upper), fars[0], core)]
    size = lax.axis_size("dof")
    low = lax.ppermute(own[:, -1:], "dof", [(i, i + 1) for i in range(size - 1)])
    high = lax.ppermute(own[:, :1], "dof", [(i + 1, i) for i in range(size - 1)])
    stiff, gram, mass = stiff_terms(own, low, high, stiffness[0], density[0], met)

    mine = lax.dynamic_slice_in_dim(eigen_blocks[0], blk * rows, rows, 0)
    other = lax.dynamic_slice_in_dim(eigen_blocks[0], (1 - blk) * rows, rows, 0)
    spread = spread_blocks(jnp.concatenate([mine, other], axis=0).T)

    across = functools.partial(
        lax.dot_general,
        dimension_numbers=(((1, 2), (1, 2)), ((), ())),
        preferred_element_type=jnp.float32,
    )
    border = across(core[:, reach - 1], met[:, reach]) - across(core[:, reach], met[:, reach - 1])
    cross = jnp.where(upper == 1, 0.5 * border, -0.5 * border)
    within = upper * reach
    vectors, order = expand(spread, own, met, jnp.full_like(upper, half - reach), None, mass)
    cross = cross + cross_terms(stiff, met, half - reach + within, within, reach, order)
    for chunk, offset, count in zip(near, near_at, nears):
        at = spot(offset, count, upper)
        vectors, order = expand(spread, own, chunk, at, vectors)
        cross = cross + cross_terms(stiff, chunk, at, jnp.zeros_like(at), count, order)

    tops, masses = jnp.concatenate([gram, cross], axis=1), jnp.concatenate([mass, mass], axis=1)
    whole = line_sum(jnp.concatenate([tops, masses], axis=0), "dof")
    nodes = lax.axis_size("leaf") // 2
    belongs = (parent[leaf] == jnp.arange(nodes, dtype=jnp.int32)).astype(jnp.float32)
    whole = paired_sum(belongs[:, None, None] * whole[None], "leaf")
    theirs = crossed(jnp.concatenate([whole[p, :, rows:] for p in range(nodes)], axis=1))
    far += [send(far_spot(o, n, 1 - upper), n, whole) for o, n in zip(far_at[1:], fars[1:])]

    node_stiffness, root_stiffness = merge(whole, theirs, blk)
    places = [far_spot(o, n, upper) for o, n in zip(far_at, fars)]
    order = (root_stiffness,)
    for chunk, at in zip(far[:-1], places[:-1]):
        vectors, _ = expand(spread, own, chunk, at, vectors, *order)
        order = ()
    vectors = expand_last(spread, cut(own, places[-1], last, whole), far[-1], places[-1], vectors)
    return (node_stiffness, root_stiffness, vectors[None])


def extended(x, sides, width):
    for axis, dim in sides:
        size, length = (lax.axis_size(axis), x.shape[dim])
        up = [(i, (i + 1) % size) for i in range(size - 1)]
        down = [(j, i) for i, j in up]
        last = lax.slice_in_dim(x, length - width, length, axis=dim)
        leading = lax.slice_in_dim(x, 0, width, axis=dim)
        before = lax.ppermute(last, axis, up)
        after = lax.ppermute(leading, axis, down)
        x = jnp.concatenate([before, x, after], axis=dim)
    return x


def neighbours(padded):
    inner = padded[:, 1:-1]
    sides = jnp.pad(inner, ((0, 0), (0, 0), (1, 1), (1, 1)))
    total = padded[:, 2:] + padded[:, :-2]
    total = total + sides[:, :, 2:, 1:-1] + sides[:, :, :-2, 1:-1]
    total = total + sides[:, :, 1:-1, 2:] + sides[:, :, 1:-1, :-2]
    return total


def gathered(modes, stiffness, density, eigen_blocks, parent):
    own = modes[0]
    rows, cells_x, cells_y, cells_z = own.shape
    cells = cells_x * cells_y * cells_z
    total_modes = rows * lax.axis_size("blk")
    padded = extended(own, (("dof", 1),), 1).astype(jnp.float32)
    field = padded[:, 1:-1]
    stiff = ((6.0 + stiffness[0]) * field - neighbours(padded)).astype(jnp.bfloat16)
    stiff_flat = stiff.reshape(rows, cells)
    own_flat = own.reshape(rows, cells)
    mass_flat = density[0].reshape(cells)
    weighed_own = (mass_flat[None, :] * own_flat.astype(jnp.float32)).astype(jnp.bfloat16)
    diag_own = jnp.einsum("rc,rc->r", weighed_own, own_flat, preferred_element_type=jnp.float32)
    diagonal = lax.all_gather(diag_own, "blk", axis=0, tiled=True)
    blocks = eigen_blocks[0]
    eig_rows = blocks.shape[1]
    piece = lax.all_gather(own_flat, "blk", axis=0, tiled=True)
    columns = lax.dot_general(
        stiff_flat, piece, (((1,), (1,)), ((), ())), preferred_element_type=jnp.float32
    )
    reduced = columns
    vectors = lax.dot_general(
        blocks, piece, (((0,), (0,)), ((), ())), preferred_element_type=jnp.float32
    )
    reduced, vectors = (reduced, vectors)
    vector_flat = vectors.astype(jnp.bfloat16)
    leaf_vectors = vector_flat.reshape(1, eig_rows, cells_x, cells_y, cells_z)
    leaves = lax.axis_size("leaf")
    nodes = leaves // 2
    node_ids = jnp.arange(nodes, dtype=jnp.int32)
    halves = lax.axis_size("dof")
    gathered_rows, gathered_diag = (
        lax.all_gather(reduced[None], ("leaf", "dof"), axis=0, tiled=True),
        lax.all_gather(diagonal[None], ("leaf", "dof"), axis=0, tiled=True),
    )
    leaf_rows = jnp.sum(gathered_rows.reshape(leaves, halves, rows, total_modes), axis=1)
    leaf_diag = jnp.sum(gathered_diag.reshape(leaves, halves, total_modes), axis=1)
    onehot = (parent[:, None] == node_ids[None, :]).astype(jnp.float32)
    node_stiffness = jnp.einsum("lp,lij->pij", onehot, leaf_rows, precision=lax.Precision.HIGHEST)
    node_mass = jnp.einsum("lp,li->pi", onehot, leaf_diag, precision=lax.Precision.HIGHEST)
    scale = 1.0 / jnp.sqrt(node_mass)
    scale_own = lax.dynamic_slice_in_dim(scale, lax.axis_index("blk") * rows, rows, 1)
    root_stiffness = jnp.sum(scale_own[:, :, None] * node_stiffness * scale[:, None, :], axis=0)
    return (node_stiffness, root_stiffness, leaf_vectors)


def body(modes, *others):
    leaves = lax.axis_size("leaf")
    paired = leaves >= 4 and leaves & (leaves - 1) == 0
    layers, cells_y = modes.shape[2:4]
    fits = layers % 2 == 0 and layers >= 32 and cells_y % SUB == 0 and modes.shape[1] % SUB == 0
    if lax.axis_size("blk") == 2 and paired and fits:
        return halved(modes, *others)
    return gathered(modes, *others)


def solution(mesh):
    in_specs = (
        P("leaf", "blk", "dof", None, None),
        P("leaf", "dof", None, None),
        P("leaf", "dof", None, None),
        P("leaf", None, "blk"),
        P(),
    )
    out_specs = (P(None, "blk", None), P("blk", None), P("leaf", "blk", "dof", None, None))
    return jax.shard_map(body, mesh=mesh, in_specs=in_specs, out_specs=out_specs, check_vma=False)
```

```python
import functools
import jax
import jax.numpy as jnp
from jax import lax
from jax.experimental import pallas as pl
from jax.experimental.pallas import tpu as pltpu
from jax.sharding import PartitionSpec as P

SUB = 8
VMEM_BYTES = 48 * 1024 * 1024
LAST_BYTES = 16 * 1024 * 1024
PARTS = 5
SMALL = pl.CostEstimate(flops=1024, bytes_accessed=1024, transcendentals=0)


def params():
    return pltpu.CompilerParams(
        dimension_semantics=("arbitrary",), vmem_limit_bytes=VMEM_BYTES
    )


def split_rows(x):
    wide = x.astype(jnp.float32)
    rows, cells_y, cells_z = wide.shape
    parts = [
        wide[:, i * SUB : (i + 1) * SUB].reshape(rows * SUB, cells_z).astype(jnp.bfloat16)
        for i in range(cells_y // SUB)
    ]
    return jnp.concatenate(parts, axis=1)


def accumulate(total, left, right):
    total[...] += lax.dot_general(
        left, right, (((1,), (1,)), ((), ())), preferred_element_type=jnp.float32
    )


def same_row_sum(total):
    tall, wide = total.shape
    row = lax.broadcasted_iota(jnp.int32, (tall, wide), 0) % SUB
    col = lax.broadcasted_iota(jnp.int32, (tall, wide), 1) % SUB
    kept = jnp.where(row == col, total, 0.0).reshape(tall // SUB, SUB, wide)
    folded = jnp.sum(kept, axis=1)
    group = lax.broadcasted_iota(jnp.int32, (wide, wide // SUB), 0) // SUB
    pick = (group == lax.broadcasted_iota(jnp.int32, (wide, wide // SUB), 1)).astype(jnp.float32)
    return jnp.dot(folded, pick, precision=lax.Precision.HIGHEST, preferred_element_type=jnp.float32)


def stiff_kernel(own, prev, after, low, high, coefs, masses, order, stiff, gram, mass, total, flat, acc):
    layer, last = pl.program_id(0), pl.num_programs(0) - 1
    rows, _, cells_y, cells_z = own.shape

    @pl.when(layer == 0)
    def _():
        total[...] = jnp.zeros_like(total)
        acc[...] = jnp.zeros_like(acc)

    y = lax.broadcasted_iota(jnp.int32, (SUB, cells_y, cells_z), 1)
    z = lax.broadcasted_iota(jnp.int32, (SUB, cells_y, cells_z), 2)
    diagonal = 6.0 + coefs[0]
    density = masses[0]

    def group(g, carry):
        modes = pl.ds(g * SUB, SUB)
        field = own[modes, 0].astype(jnp.float32)
        before = jnp.where(layer == 0, low[modes, 0], prev[modes, 0]).astype(jnp.float32)
        behind = jnp.where(layer == last, high[modes, 0], after[modes, 0]).astype(jnp.float32)
        around = before + behind
        around += jnp.where(y == 0, 0.0, pltpu.roll(field, 1, 1))
        around += jnp.where(y == cells_y - 1, 0.0, pltpu.roll(field, cells_y - 1, 1))
        around += jnp.where(z == 0, 0.0, pltpu.roll(field, 1, 2))
        around += jnp.where(z == cells_z - 1, 0.0, pltpu.roll(field, cells_z - 1, 2))
        force = diagonal[None] * field - around
        weighed = (density[None] * field).astype(jnp.bfloat16).astype(jnp.float32) * field
        out = pl.ds(g * SUB * SUB, SUB * SUB)
        part = None
        for i in range(cells_y // SUB):
            rows_y, lanes = slice(i * SUB, (i + 1) * SUB), slice(i * cells_z, (i + 1) * cells_z)
            stiff[0, out, lanes] = force[:, rows_y].reshape(SUB * SUB, cells_z).astype(jnp.bfloat16)
            flat[out, lanes] = field[:, rows_y].reshape(SUB * SUB, cells_z).astype(jnp.bfloat16)
            part = weighed[:, rows_y] if part is None else part + weighed[:, rows_y]
        acc[modes] += part
        return carry

    lax.fori_loop(0, rows // SUB, group, 0)
    accumulate(total, stiff[0], flat[...])

    @pl.when(layer == last)
    def _():
        gram[...] = same_row_sum(total[...])
        column = jnp.sum(jnp.sum(acc[...], axis=1), axis=1, keepdims=True)
        mass[...] = jnp.broadcast_to(column, (rows, rows)).T[: mass.shape[0]]


def stiff_terms(own, low, high, coefs, masses, order):
    rows, layers, cells_y, cells_z = own.shape
    tall, wide = rows * SUB, cells_y // SUB * cells_z
    block = (rows, 1, cells_y, cells_z)
    cells = (1, cells_y, cells_z)
    return pl.pallas_call(
        stiff_kernel,
        grid=(layers,),
        in_specs=[
            pl.BlockSpec(block, lambda g: (0, g, 0, 0)),
            pl.BlockSpec(block, lambda g: (0, jnp.maximum(g - 1, 0), 0, 0)),
            pl.BlockSpec(block, lambda g: (0, jnp.minimum(g + 1, layers - 1), 0, 0)),
            pl.BlockSpec(block, lambda g: (0, 0, 0, 0)),
            pl.BlockSpec(block, lambda g: (0, 0, 0, 0)),
            pl.BlockSpec(cells, lambda g: (g, 0, 0)),
            pl.BlockSpec(cells, lambda g: (g, 0, 0)),
            pl.BlockSpec(memory_space=pl.ANY),
        ],
        out_specs=[
            pl.BlockSpec((1, tall, wide), lambda g: (g, 0, 0)),
            pl.BlockSpec((rows, rows), lambda g: (0, 0)),
            pl.BlockSpec((2 * SUB, rows), lambda g: (0, 0)),
        ],
        out_shape=[
            jax.ShapeDtypeStruct((layers, tall, wide), jnp.bfloat16),
            jax.ShapeDtypeStruct((rows, rows), jnp.float32),
            jax.ShapeDtypeStruct((2 * SUB, rows), jnp.float32),
        ],
        scratch_shapes=[
            pltpu.VMEM((tall, tall), jnp.float32),
            pltpu.VMEM((tall, wide), jnp.bfloat16),
            pltpu.VMEM((rows, SUB, cells_z), jnp.float32),
        ],
        compiler_params=params(),
        cost_estimate=SMALL,
        name="stiff_terms",
    )(own, own, own, low, high, coefs, masses, order)


def cross_kernel(at, skip, stiff, other, order, gram, total):
    step = pl.program_id(0)

    @pl.when(step == 0)
    def _():
        total[...] = jnp.zeros_like(total)

    accumulate(total, stiff[0], split_rows(other[:, 0]))

    @pl.when(step == pl.num_programs(0) - 1)
    def _():
        gram[...] = same_row_sum(total[...])


def cross_terms(stiff, other, at, skip, layers, order):
    rows, _, cells_y, cells_z = other.shape
    _, tall, wide = stiff.shape
    return pl.pallas_call(
        cross_kernel,
        grid_spec=pltpu.PrefetchScalarGridSpec(
            num_scalar_prefetch=2,
            grid=(layers,),
            in_specs=[
                pl.BlockSpec((1, tall, wide), lambda g, at, skip: (at[0] + g, 0, 0)),
                pl.BlockSpec((rows, 1, cells_y, cells_z), lambda g, at, skip: (0, skip[0] + g, 0, 0)),
                pl.BlockSpec(memory_space=pl.ANY),
            ],
            out_specs=pl.BlockSpec((rows, rows), lambda g, at, skip: (0, 0)),
            scratch_shapes=[pltpu.VMEM((tall, tall), jnp.float32)],
        ),
        out_shape=jax.ShapeDtypeStruct((rows, rows), jnp.float32),
        compiler_params=params(),
        cost_estimate=SMALL,
        name="cross_terms",
    )(at.reshape(1), skip.reshape(1), stiff, other, order)


def cut_kernel(at, whole, *rest):
    out, held, reads, writes = rest[-4:]
    pieces = held.shape[0]
    layers = out.shape[1]
    bounds = [layers * i // pieces for i in range(pieces + 1)]
    ins, outs = [], []
    for i in range(pieces):
        start, size = bounds[i], bounds[i + 1] - bounds[i]
        piece = held.at[i, :, pl.ds(0, size)]
        ins.append(
            pltpu.make_async_copy(whole.at[:, pl.ds(at[0] + start, size)], piece, reads.at[i])
        )
        outs.append(pltpu.make_async_copy(piece, out.at[:, pl.ds(start, size)], writes.at[i]))
    for copy in ins:
        copy.start()
    for i in range(pieces):
        ins[i].wait()
        outs[i].start()
    for copy in outs:
        copy.wait()


def cut(whole, at, count, *orders):
    rows, _, cells_y, cells_z = whole.shape
    pieces = min(4, count)
    longest = -(-count // pieces)
    return pl.pallas_call(
        cut_kernel,
        grid_spec=pltpu.PrefetchScalarGridSpec(
            num_scalar_prefetch=1,
            grid=(1,),
            in_specs=[pl.BlockSpec(memory_space=pl.ANY)] * (1 + len(orders)),
            out_specs=pl.BlockSpec(memory_space=pl.ANY),
            scratch_shapes=[
                pltpu.VMEM((pieces, rows, longest, cells_y, cells_z), whole.dtype),
                pltpu.SemaphoreType.DMA((pieces,)),
                pltpu.SemaphoreType.DMA((pieces,)),
            ],
        ),
        out_shape=jax.ShapeDtypeStruct((rows, count, cells_y, cells_z), whole.dtype),
        compiler_params=params(),
        cost_estimate=SMALL,
        name="cut",
    )(at.reshape(1), whole, *orders)


def cut_middle_kernel(start, whole, out, held, reads, writes):
    layers = out.shape[1]
    ins, outs = [], []
    for i in range(layers):
        piece = held.at[:, pl.ds(i, 1)]
        ins.append(pltpu.make_async_copy(whole.at[:, pl.ds(start + i, 1)], piece, reads.at[i]))
        outs.append(pltpu.make_async_copy(piece, out.at[:, pl.ds(i, 1)], writes.at[i]))
    for copy in ins:
        copy.start()
    for i in range(layers):
        ins[i].wait()
        outs[i].start()
    for copy in outs:
        copy.wait()


def cut_middle(whole, count):
    rows, layers, cells_y, cells_z = whole.shape
    shape = (rows, count, cells_y, cells_z)
    return pl.pallas_call(
        functools.partial(cut_middle_kernel, (layers - count) // 2),
        in_specs=[pl.BlockSpec(memory_space=pl.ANY)],
        out_specs=pl.BlockSpec(memory_space=pl.ANY),
        scratch_shapes=[
            pltpu.VMEM(shape, whole.dtype),
            pltpu.SemaphoreType.DMA((count,)),
            pltpu.SemaphoreType.DMA((count,)),
        ],
        out_shape=jax.ShapeDtypeStruct(shape, whole.dtype),
        compiler_params=pltpu.CompilerParams(vmem_limit_bytes=VMEM_BYTES),
        cost_estimate=SMALL,
        name="cut_middle",
    )(whole)


def merge_kernel(blk, whole, theirs, node, root):
    nodes, _, both = whole.shape
    rows = both // 2
    first = blk[0] == 0
    total = None
    for p in range(nodes):
        here = slice(p * rows, (p + 1) * rows)
        gram = whole[p, :rows, :rows]
        cross = whole[p, :rows, rows:] + theirs[:rows, here].T
        scale_gram = 1.0 / jnp.sqrt(whole[p, rows : rows + 1, :rows])
        scale_cross = 1.0 / jnp.sqrt(theirs[rows : rows + 1, here])
        scale = jnp.broadcast_to(scale_gram, (rows, rows)).T
        low, high = jnp.where(first, gram, cross), jnp.where(first, cross, gram)
        scale_low = jnp.where(first, scale_gram, scale_cross)
        scale_high = jnp.where(first, scale_cross, scale_gram)
        node[p, :, :rows] = low
        node[p, :, rows:] = high
        scaled = jnp.concatenate([scale * low * scale_low, scale * high * scale_high], axis=1)
        total = scaled if total is None else total + scaled
    root[...] = total


def merge(whole, theirs, blk):
    nodes, _, both = whole.shape
    rows = both // 2
    return pl.pallas_call(
        merge_kernel,
        grid_spec=pltpu.PrefetchScalarGridSpec(
            num_scalar_prefetch=1,
            grid=(1,),
            in_specs=[
                pl.BlockSpec(whole.shape, lambda g, blk: (0, 0, 0)),
                pl.BlockSpec(theirs.shape, lambda g, blk: (0, 0)),
            ],
            out_specs=[
                pl.BlockSpec((nodes, rows, 2 * rows), lambda g, blk: (0, 0, 0)),
                pl.BlockSpec((rows, 2 * rows), lambda g, blk: (0, 0)),
            ],
        ),
        out_shape=[
            jax.ShapeDtypeStruct((nodes, rows, 2 * rows), jnp.float32),
            jax.ShapeDtypeStruct((rows, 2 * rows), jnp.float32),
        ],
        compiler_params=params(),
        cost_estimate=SMALL,
        name="merge",
    )(blk.astype(jnp.int32).reshape(1), whole, theirs)


def spread_kernel(block, out):
    tall, wide = out.shape
    eigs, modes = block.shape

    def shape_of(rows, cols, dim):
        index = lax.broadcasted_iota(jnp.int32, (rows, cols), dim)
        near = lax.broadcasted_iota(jnp.int32, (rows, cols), 1 - dim)
        return (index // SUB == near).astype(jnp.bfloat16)

    wider = jnp.dot(block[...], shape_of(modes, wide, 1), preferred_element_type=jnp.float32)
    full = jnp.dot(
        shape_of(tall, eigs, 0), wider.astype(jnp.bfloat16), preferred_element_type=jnp.float32
    )
    row = lax.broadcasted_iota(jnp.int32, (tall, wide), 0) % SUB
    col = lax.broadcasted_iota(jnp.int32, (tall, wide), 1) % SUB
    out[...] = jnp.where(row == col, full, 0.0).astype(out.dtype)


def spread_blocks(block):
    eigs, modes = block.shape
    return pl.pallas_call(
        spread_kernel,
        out_shape=jax.ShapeDtypeStruct((eigs * SUB, modes * SUB), block.dtype),
        compiler_params=pltpu.CompilerParams(vmem_limit_bytes=VMEM_BYTES),
        cost_estimate=SMALL,
        name="spread_blocks",
    )(block)


def vector_kernel(at, spread, own, other, *rest):
    out, done = rest[-2:]
    done[...] = jnp.zeros_like(done)
    rows, _, cells_y, cells_z = own.shape
    both = jnp.concatenate([split_rows(own[:, 0]), split_rows(other[:, 0])], axis=0)
    made = jnp.dot(spread[...], both, preferred_element_type=jnp.float32)
    eigs = out.shape[0]
    parts = [
        made[:, i * cells_z : (i + 1) * cells_z].reshape(eigs, SUB, cells_z)
        for i in range(cells_y // SUB)
    ]
    out[:, 0] = jnp.concatenate(parts, axis=1).astype(out.dtype)


def expand(spread, own, other, at, held, *orders):
    rows, layers, cells_y, cells_z = other.shape
    eigs = spread.shape[0] // SUB
    inputs = [at.reshape(1), spread, own, other]
    specs = [
        pl.BlockSpec(spread.shape, lambda g, at: (0, 0)),
        pl.BlockSpec((rows, 1, cells_y, cells_z), lambda g, at: (0, at[0] + g, 0, 0)),
        pl.BlockSpec((rows, 1, cells_y, cells_z), lambda g, at: (0, g, 0, 0)),
    ]
    aliases = {}
    if held is not None:
        aliases = {len(inputs): 0}
        inputs.append(held)
    inputs += orders
    specs += [pl.BlockSpec(memory_space=pl.ANY)] * (len(inputs) - 1 - len(specs))
    return pl.pallas_call(
        vector_kernel,
        grid_spec=pltpu.PrefetchScalarGridSpec(
            num_scalar_prefetch=1,
            grid=(layers,),
            in_specs=specs,
            out_specs=[
                pl.BlockSpec((eigs, 1, cells_y, cells_z), lambda g, at: (0, at[0] + g, 0, 0)),
                pl.BlockSpec((SUB, cells_z), lambda g, at: (0, 0)),
            ],
        ),
        out_shape=[
            jax.ShapeDtypeStruct((eigs,) + own.shape[1:], jnp.bfloat16),
            jax.ShapeDtypeStruct((SUB, cells_z), jnp.float32),
        ],
        input_output_aliases=aliases,
        compiler_params=params(),
        cost_estimate=SMALL,
        name="expand",
    )(*inputs)


def last_kernel(at, spread, own, other, held, out, made, sems):
    rows, layers, cells_y, cells_z = own.shape
    eigs = out.shape[0]
    parts = made.shape[0]
    copies = []
    for layer in range(layers):
        both = jnp.concatenate([split_rows(own[:, layer]), split_rows(other[:, layer])], axis=0)
        for part in range(parts):
            size = eigs // parts
            some = jnp.dot(
                spread[part * size * SUB : (part + 1) * size * SUB],
                both,
                preferred_element_type=jnp.float32,
            )
            tiles = [
                some[:, i * cells_z : (i + 1) * cells_z].reshape(size, SUB, cells_z)
                for i in range(cells_y // SUB)
            ]
            made[part, :, layer] = jnp.concatenate(tiles, axis=1).astype(made.dtype)
            if layer == layers - 1:
                place = out.at[pl.ds(part * size, size), pl.ds(at[0], layers)]
                copies.append(pltpu.make_async_copy(made.at[part], place, sems.at[part]))
                copies[-1].start()
    for copy in copies:
        copy.wait()


def expand_last(spread, own, other, at, held):
    rows, layers, cells_y, cells_z = other.shape
    eigs, parts = spread.shape[0] // SUB, 4
    inside = pl.BlockSpec(memory_space=pltpu.VMEM)
    return pl.pallas_call(
        last_kernel,
        in_specs=[pl.BlockSpec(memory_space=pltpu.SMEM), inside, inside, inside, pl.BlockSpec(memory_space=pl.ANY)],
        out_specs=pl.BlockSpec(memory_space=pl.ANY),
        out_shape=jax.ShapeDtypeStruct(held.shape, held.dtype),
        scratch_shapes=[
            pltpu.VMEM((parts, eigs // parts, layers, cells_y, cells_z), held.dtype),
            pltpu.SemaphoreType.DMA((parts,)),
        ],
        input_output_aliases={4: 0},
        compiler_params=pltpu.CompilerParams(vmem_limit_bytes=LAST_BYTES),
        cost_estimate=SMALL,
        name="expand_last",
    )(at.reshape(1), spread, own, other, held)


def shares(total, parts):
    return [total // parts + (i < total % parts) for i in range(parts)]


def swap(x):
    return lax.ppermute(x, "blk", [(0, 1), (1, 0)])


def crossed(x):
    leaves, leaf = lax.axis_size("leaf"), lax.axis_index("leaf")
    places, place = lax.axis_size("dof"), lax.axis_index("dof")
    pairs = [(2 * i + j, 2 * (i ^ (leaves // 2)) + 1 - j) for i in range(leaves) for j in range(2)]
    count = x.shape[0] // (2 * places)
    part = lax.dynamic_slice_in_dim(x, (leaf % 2 * places + place) * count, count, 0)
    part = lax.ppermute(part, ("leaf", "blk"), pairs)
    step = 1
    while step < places:
        part = joined(part, "dof", step)
        step *= 2
    return joined(part, "leaf", 1)


def joined(part, axis, step):
    rest = lax.ppermute(part, axis, [(i, i ^ step) for i in range(lax.axis_size(axis))])
    first = lax.axis_index(axis) // step % 2 == 0
    return jnp.where(first, jnp.concatenate([part, rest], 0), jnp.concatenate([rest, part], 0))


def paired_sum(x, axis):
    size, step = lax.axis_size(axis), 1
    while step < size:
        x = x + lax.ppermute(x, axis, [(i, i ^ step) for i in range(size)])
        step *= 2
    return x


def line_sum(x, axis):
    if lax.axis_size(axis) != 4:
        return lax.psum(x, axis)
    x = x + lax.ppermute(x, axis, [(0, 1), (1, 0), (2, 3), (3, 2)])
    x = x + lax.ppermute(x, axis, [(1, 2), (2, 1)])
    outer = lax.ppermute(x, axis, [(1, 0), (2, 3)])
    place = lax.axis_index(axis)
    return jnp.where((place == 0) | (place == 3), outer, x)


def halved(modes, stiffness, density, eigen_blocks, parent):
    own = modes[0]
    rows, layers = own.shape[:2]
    half = layers // 2
    blk, dof, leaf = lax.axis_index("blk"), lax.axis_index("dof"), lax.axis_index("leaf")
    upper = (blk + dof) % 2

    def spot(offset, count, top):
        forward, back = half - 1 + offset, half + 1 - offset - count
        return jnp.where(top == 1, forward, back).astype(jnp.int32)

    def far_spot(offset, count, top):
        forward, back = half + 1 + offset, half - 1 - offset - count
        return jnp.where(top == 0, forward, back).astype(jnp.int32)

    def send(at, count, *orders):
        return swap(cut(own, at, count, *orders))

    last, middle, reach = half // 16, half // 8, half // 8
    fars = [half - reach - middle - last, middle, last]
    far_at = [reach - 1 + sum(fars[:i]) for i in range(len(fars))]
    nears = shares(half - reach, PARTS)
    near_at = [reach + 1 + sum(nears[:i]) for i in range(len(nears))]

    core = cut_middle(own, 2 * reach)
    met = swap(core)
    near = [send(spot(o, n, 1 - upper), n, core) for o, n in zip(near_at, nears)]
    far = [send(far_spot(far_at[0], fars[0], 1 - upper), fars[0], core)]
    size = lax.axis_size("dof")
    low = lax.ppermute(own[:, -1:], "dof", [(i, i + 1) for i in range(size - 1)])
    high = lax.ppermute(own[:, :1], "dof", [(i + 1, i) for i in range(size - 1)])
    stiff, gram, mass = stiff_terms(own, low, high, stiffness[0], density[0], met)

    mine = lax.dynamic_slice_in_dim(eigen_blocks[0], blk * rows, rows, 0)
    other = lax.dynamic_slice_in_dim(eigen_blocks[0], (1 - blk) * rows, rows, 0)
    spread = spread_blocks(jnp.concatenate([mine, other], axis=0).T)

    across = functools.partial(
        lax.dot_general,
        dimension_numbers=(((1, 2), (1, 2)), ((), ())),
        preferred_element_type=jnp.float32,
    )
    border = across(core[:, reach - 1], met[:, reach]) - across(core[:, reach], met[:, reach - 1])
    cross = jnp.where(upper == 1, 0.5 * border, -0.5 * border)
    within = upper * reach
    vectors, order = expand(spread, own, met, jnp.full_like(upper, half - reach), None, mass)
    cross = cross + cross_terms(stiff, met, half - reach + within, within, reach, order)
    for chunk, offset, count in zip(near, near_at, nears):
        at = spot(offset, count, upper)
        vectors, order = expand(spread, own, chunk, at, vectors)
        cross = cross + cross_terms(stiff, chunk, at, jnp.zeros_like(at), count, order)

    tops, masses = jnp.concatenate([gram, cross], axis=1), jnp.concatenate([mass, mass], axis=1)
    whole = line_sum(jnp.concatenate([tops, masses], axis=0), "dof")
    nodes = lax.axis_size("leaf") // 2
    belongs = (parent[leaf] == jnp.arange(nodes, dtype=jnp.int32)).astype(jnp.float32)
    whole = paired_sum(belongs[:, None, None] * whole[None], "leaf")
    theirs = crossed(jnp.concatenate([whole[p, :, rows:] for p in range(nodes)], axis=1))
    far += [send(far_spot(o, n, 1 - upper), n, whole) for o, n in zip(far_at[1:], fars[1:])]

    node_stiffness, root_stiffness = merge(whole, theirs, blk)
    places = [far_spot(o, n, upper) for o, n in zip(far_at, fars)]
    order = (root_stiffness,)
    for chunk, at in zip(far[:-1], places[:-1]):
        vectors, _ = expand(spread, own, chunk, at, vectors, *order)
        order = ()
    vectors = expand_last(spread, cut(own, places[-1], last, whole), far[-1], places[-1], vectors)
    return (node_stiffness, root_stiffness, vectors[None])


def extended(x, sides, width):
    for axis, dim in sides:
        size, length = (lax.axis_size(axis), x.shape[dim])
        up = [(i, (i + 1) % size) for i in range(size - 1)]
        down = [(j, i) for i, j in up]
        last = lax.slice_in_dim(x, length - width, length, axis=dim)
        leading = lax.slice_in_dim(x, 0, width, axis=dim)
        before = lax.ppermute(last, axis, up)
        after = lax.ppermute(leading, axis, down)
        x = jnp.concatenate([before, x, after], axis=dim)
    return x


def neighbours(padded):
    inner = padded[:, 1:-1]
    sides = jnp.pad(inner, ((0, 0), (0, 0), (1, 1), (1, 1)))
    total = padded[:, 2:] + padded[:, :-2]
    total = total + sides[:, :, 2:, 1:-1] + sides[:, :, :-2, 1:-1]
    total = total + sides[:, :, 1:-1, 2:] + sides[:, :, 1:-1, :-2]
    return total


def gathered(modes, stiffness, density, eigen_blocks, parent):
    own = modes[0]
    rows, cells_x, cells_y, cells_z = own.shape
    cells = cells_x * cells_y * cells_z
    total_modes = rows * lax.axis_size("blk")
    padded = extended(own, (("dof", 1),), 1).astype(jnp.float32)
    field = padded[:, 1:-1]
    stiff = ((6.0 + stiffness[0]) * field - neighbours(padded)).astype(jnp.bfloat16)
    stiff_flat = stiff.reshape(rows, cells)
    own_flat = own.reshape(rows, cells)
    mass_flat = density[0].reshape(cells)
    weighed_own = (mass_flat[None, :] * own_flat.astype(jnp.float32)).astype(jnp.bfloat16)
    diag_own = jnp.einsum("rc,rc->r", weighed_own, own_flat, preferred_element_type=jnp.float32)
    diagonal = lax.all_gather(diag_own, "blk", axis=0, tiled=True)
    blocks = eigen_blocks[0]
    eig_rows = blocks.shape[1]
    piece = lax.all_gather(own_flat, "blk", axis=0, tiled=True)
    columns = lax.dot_general(
        stiff_flat, piece, (((1,), (1,)), ((), ())), preferred_element_type=jnp.float32
    )
    reduced = columns
    vectors = lax.dot_general(
        blocks, piece, (((0,), (0,)), ((), ())), preferred_element_type=jnp.float32
    )
    reduced, vectors = (reduced, vectors)
    vector_flat = vectors.astype(jnp.bfloat16)
    leaf_vectors = vector_flat.reshape(1, eig_rows, cells_x, cells_y, cells_z)
    leaves = lax.axis_size("leaf")
    nodes = leaves // 2
    node_ids = jnp.arange(nodes, dtype=jnp.int32)
    halves = lax.axis_size("dof")
    gathered_rows, gathered_diag = (
        lax.all_gather(reduced[None], ("leaf", "dof"), axis=0, tiled=True),
        lax.all_gather(diagonal[None], ("leaf", "dof"), axis=0, tiled=True),
    )
    leaf_rows = jnp.sum(gathered_rows.reshape(leaves, halves, rows, total_modes), axis=1)
    leaf_diag = jnp.sum(gathered_diag.reshape(leaves, halves, total_modes), axis=1)
    onehot = (parent[:, None] == node_ids[None, :]).astype(jnp.float32)
    node_stiffness = jnp.einsum("lp,lij->pij", onehot, leaf_rows, precision=lax.Precision.HIGHEST)
    node_mass = jnp.einsum("lp,li->pi", onehot, leaf_diag, precision=lax.Precision.HIGHEST)
    scale = 1.0 / jnp.sqrt(node_mass)
    scale_own = lax.dynamic_slice_in_dim(scale, lax.axis_index("blk") * rows, rows, 1)
    root_stiffness = jnp.sum(scale_own[:, :, None] * node_stiffness * scale[:, None, :], axis=0)
    return (node_stiffness, root_stiffness, leaf_vectors)


def body(modes, *others):
    leaves = lax.axis_size("leaf")
    paired = leaves >= 4 and leaves & (leaves - 1) == 0
    layers, cells_y = modes.shape[2:4]
    fits = layers % 2 == 0 and layers >= 32 and cells_y % SUB == 0 and modes.shape[1] % SUB == 0
    if lax.axis_size("blk") == 2 and paired and fits:
        return halved(modes, *others)
    return gathered(modes, *others)


def solution(mesh):
    in_specs = (
        P("leaf", "blk", "dof", None, None),
        P("leaf", "dof", None, None),
        P("leaf", "dof", None, None),
        P("leaf", None, "blk"),
        P(),
    )
    out_specs = (P(None, "blk", None), P("blk", None), P("leaf", "blk", "dof", None, None))
    return jax.shard_map(body, mesh=mesh, in_specs=in_specs, out_specs=out_specs, check_vma=False)
```

```python
import functools
import jax
import jax.numpy as jnp
from jax import lax
from jax.experimental import pallas as pl
from jax.experimental.pallas import tpu as pltpu
from jax.sharding import PartitionSpec as P

SUB = 8
VMEM_BYTES = 48 * 1024 * 1024
LAST_BYTES = 16 * 1024 * 1024
PARTS = 5
SMALL = pl.CostEstimate(flops=1024, bytes_accessed=1024, transcendentals=0)


def params():
    return pltpu.CompilerParams(
        dimension_semantics=("arbitrary",), vmem_limit_bytes=VMEM_BYTES
    )


def split_rows(x):
    wide = x.astype(jnp.float32)
    rows, cells_y, cells_z = wide.shape
    parts = [
        wide[:, i * SUB : (i + 1) * SUB].reshape(rows * SUB, cells_z).astype(jnp.bfloat16)
        for i in range(cells_y // SUB)
    ]
    return jnp.concatenate(parts, axis=1)


def accumulate(total, left, right):
    total[...] += lax.dot_general(
        left, right, (((1,), (1,)), ((), ())), preferred_element_type=jnp.float32
    )


def same_row_sum(total):
    tall, wide = total.shape
    row = lax.broadcasted_iota(jnp.int32, (tall, wide), 0) % SUB
    col = lax.broadcasted_iota(jnp.int32, (tall, wide), 1) % SUB
    kept = jnp.where(row == col, total, 0.0).reshape(tall // SUB, SUB, wide)
    folded = jnp.sum(kept, axis=1)
    group = lax.broadcasted_iota(jnp.int32, (wide, wide // SUB), 0) // SUB
    pick = (group == lax.broadcasted_iota(jnp.int32, (wide, wide // SUB), 1)).astype(jnp.float32)
    return jnp.dot(folded, pick, precision=lax.Precision.HIGHEST, preferred_element_type=jnp.float32)


def stiff_kernel(own, prev, after, low, high, coefs, masses, order, stiff, gram, mass, total, flat, acc):
    layer, last = pl.program_id(0), pl.num_programs(0) - 1
    rows, _, cells_y, cells_z = own.shape

    @pl.when(layer == 0)
    def _():
        total[...] = jnp.zeros_like(total)
        acc[...] = jnp.zeros_like(acc)

    y = lax.broadcasted_iota(jnp.int32, (SUB, cells_y, cells_z), 1)
    z = lax.broadcasted_iota(jnp.int32, (SUB, cells_y, cells_z), 2)
    diagonal = 6.0 + coefs[0]
    density = masses[0]

    def group(g, carry):
        modes = pl.ds(g * SUB, SUB)
        field = own[modes, 0].astype(jnp.float32)
        before = jnp.where(layer == 0, low[modes, 0], prev[modes, 0]).astype(jnp.float32)
        behind = jnp.where(layer == last, high[modes, 0], after[modes, 0]).astype(jnp.float32)
        around = before + behind
        around += jnp.where(y == 0, 0.0, pltpu.roll(field, 1, 1))
        around += jnp.where(y == cells_y - 1, 0.0, pltpu.roll(field, cells_y - 1, 1))
        around += jnp.where(z == 0, 0.0, pltpu.roll(field, 1, 2))
        around += jnp.where(z == cells_z - 1, 0.0, pltpu.roll(field, cells_z - 1, 2))
        force = diagonal[None] * field - around
        weighed = (density[None] * field).astype(jnp.bfloat16).astype(jnp.float32) * field
        out = pl.ds(g * SUB * SUB, SUB * SUB)
        part = None
        for i in range(cells_y // SUB):
            rows_y, lanes = slice(i * SUB, (i + 1) * SUB), slice(i * cells_z, (i + 1) * cells_z)
            stiff[0, out, lanes] = force[:, rows_y].reshape(SUB * SUB, cells_z).astype(jnp.bfloat16)
            flat[out, lanes] = field[:, rows_y].reshape(SUB * SUB, cells_z).astype(jnp.bfloat16)
            part = weighed[:, rows_y] if part is None else part + weighed[:, rows_y]
        acc[modes] += part
        return carry

    lax.fori_loop(0, rows // SUB, group, 0)
    accumulate(total, stiff[0], flat[...])

    @pl.when(layer == last)
    def _():
        gram[...] = same_row_sum(total[...])
        column = jnp.sum(jnp.sum(acc[...], axis=1), axis=1, keepdims=True)
        mass[...] = jnp.broadcast_to(column, (rows, rows)).T[: mass.shape[0]]


def stiff_terms(own, low, high, coefs, masses, order):
    rows, layers, cells_y, cells_z = own.shape
    tall, wide = rows * SUB, cells_y // SUB * cells_z
    block = (rows, 1, cells_y, cells_z)
    cells = (1, cells_y, cells_z)
    return pl.pallas_call(
        stiff_kernel,
        grid=(layers,),
        in_specs=[
            pl.BlockSpec(block, lambda g: (0, g, 0, 0)),
            pl.BlockSpec(block, lambda g: (0, jnp.maximum(g - 1, 0), 0, 0)),
            pl.BlockSpec(block, lambda g: (0, jnp.minimum(g + 1, layers - 1), 0, 0)),
            pl.BlockSpec(block, lambda g: (0, 0, 0, 0)),
            pl.BlockSpec(block, lambda g: (0, 0, 0, 0)),
            pl.BlockSpec(cells, lambda g: (g, 0, 0)),
            pl.BlockSpec(cells, lambda g: (g, 0, 0)),
            pl.BlockSpec(memory_space=pl.ANY),
        ],
        out_specs=[
            pl.BlockSpec((1, tall, wide), lambda g: (g, 0, 0)),
            pl.BlockSpec((rows, rows), lambda g: (0, 0)),
            pl.BlockSpec((2 * SUB, rows), lambda g: (0, 0)),
        ],
        out_shape=[
            jax.ShapeDtypeStruct((layers, tall, wide), jnp.bfloat16),
            jax.ShapeDtypeStruct((rows, rows), jnp.float32),
            jax.ShapeDtypeStruct((2 * SUB, rows), jnp.float32),
        ],
        scratch_shapes=[
            pltpu.VMEM((tall, tall), jnp.float32),
            pltpu.VMEM((tall, wide), jnp.bfloat16),
            pltpu.VMEM((rows, SUB, cells_z), jnp.float32),
        ],
        compiler_params=params(),
        cost_estimate=SMALL,
        name="stiff_terms",
    )(own, own, own, low, high, coefs, masses, order)


def cross_kernel(at, skip, stiff, other, order, gram, total):
    step = pl.program_id(0)

    @pl.when(step == 0)
    def _():
        total[...] = jnp.zeros_like(total)

    accumulate(total, stiff[0], split_rows(other[:, 0]))

    @pl.when(step == pl.num_programs(0) - 1)
    def _():
        gram[...] = same_row_sum(total[...])


def cross_terms(stiff, other, at, skip, layers, order):
    rows, _, cells_y, cells_z = other.shape
    _, tall, wide = stiff.shape
    return pl.pallas_call(
        cross_kernel,
        grid_spec=pltpu.PrefetchScalarGridSpec(
            num_scalar_prefetch=2,
            grid=(layers,),
            in_specs=[
                pl.BlockSpec((1, tall, wide), lambda g, at, skip: (at[0] + g, 0, 0)),
                pl.BlockSpec((rows, 1, cells_y, cells_z), lambda g, at, skip: (0, skip[0] + g, 0, 0)),
                pl.BlockSpec(memory_space=pl.ANY),
            ],
            out_specs=pl.BlockSpec((rows, rows), lambda g, at, skip: (0, 0)),
            scratch_shapes=[pltpu.VMEM((tall, tall), jnp.float32)],
        ),
        out_shape=jax.ShapeDtypeStruct((rows, rows), jnp.float32),
        compiler_params=params(),
        cost_estimate=SMALL,
        name="cross_terms",
    )(at.reshape(1), skip.reshape(1), stiff, other, order)


def cut_kernel(at, whole, *rest):
    out, held, reads, writes = rest[-4:]
    pieces = held.shape[0]
    layers = out.shape[1]
    bounds = [layers * i // pieces for i in range(pieces + 1)]
    ins, outs = [], []
    for i in range(pieces):
        start, size = bounds[i], bounds[i + 1] - bounds[i]
        piece = held.at[i, :, pl.ds(0, size)]
        ins.append(
            pltpu.make_async_copy(whole.at[:, pl.ds(at[0] + start, size)], piece, reads.at[i])
        )
        outs.append(pltpu.make_async_copy(piece, out.at[:, pl.ds(start, size)], writes.at[i]))
    for copy in ins:
        copy.start()
    for i in range(pieces):
        ins[i].wait()
        outs[i].start()
    for copy in outs:
        copy.wait()


def cut(whole, at, count, *orders):
    rows, _, cells_y, cells_z = whole.shape
    pieces = min(4, count)
    longest = -(-count // pieces)
    return pl.pallas_call(
        cut_kernel,
        grid_spec=pltpu.PrefetchScalarGridSpec(
            num_scalar_prefetch=1,
            grid=(1,),
            in_specs=[pl.BlockSpec(memory_space=pl.ANY)] * (1 + len(orders)),
            out_specs=pl.BlockSpec(memory_space=pl.ANY),
            scratch_shapes=[
                pltpu.VMEM((pieces, rows, longest, cells_y, cells_z), whole.dtype),
                pltpu.SemaphoreType.DMA((pieces,)),
                pltpu.SemaphoreType.DMA((pieces,)),
            ],
        ),
        out_shape=jax.ShapeDtypeStruct((rows, count, cells_y, cells_z), whole.dtype),
        compiler_params=params(),
        cost_estimate=SMALL,
        name="cut",
    )(at.reshape(1), whole, *orders)


def cut_middle_kernel(start, whole, out, sem):
    copy = pltpu.make_async_copy(whole.at[:, pl.ds(start, out.shape[1])], out, sem)
    copy.start()
    copy.wait()


def cut_middle(whole, count):
    rows, layers, cells_y, cells_z = whole.shape
    return pl.pallas_call(
        functools.partial(cut_middle_kernel, (layers - count) // 2),
        in_specs=[pl.BlockSpec(memory_space=pl.ANY)],
        out_specs=pl.BlockSpec(memory_space=pl.ANY),
        scratch_shapes=[pltpu.SemaphoreType.DMA],
        out_shape=jax.ShapeDtypeStruct((rows, count, cells_y, cells_z), whole.dtype),
        compiler_params=pltpu.CompilerParams(vmem_limit_bytes=VMEM_BYTES),
        cost_estimate=SMALL,
        name="cut_middle",
    )(whole)


def merge_kernel(blk, whole, theirs, node, root):
    nodes, _, both = whole.shape
    rows = both // 2
    first = blk[0] == 0
    total = None
    for p in range(nodes):
        here = slice(p * rows, (p + 1) * rows)
        gram = whole[p, :rows, :rows]
        cross = whole[p, :rows, rows:] + theirs[:rows, here].T
        scale_gram = 1.0 / jnp.sqrt(whole[p, rows : rows + 1, :rows])
        scale_cross = 1.0 / jnp.sqrt(theirs[rows : rows + 1, here])
        scale = jnp.broadcast_to(scale_gram, (rows, rows)).T
        low, high = jnp.where(first, gram, cross), jnp.where(first, cross, gram)
        scale_low = jnp.where(first, scale_gram, scale_cross)
        scale_high = jnp.where(first, scale_cross, scale_gram)
        node[p, :, :rows] = low
        node[p, :, rows:] = high
        scaled = jnp.concatenate([scale * low * scale_low, scale * high * scale_high], axis=1)
        total = scaled if total is None else total + scaled
    root[...] = total


def merge(whole, theirs, blk):
    nodes, _, both = whole.shape
    rows = both // 2
    return pl.pallas_call(
        merge_kernel,
        grid_spec=pltpu.PrefetchScalarGridSpec(
            num_scalar_prefetch=1,
            grid=(1,),
            in_specs=[
                pl.BlockSpec(whole.shape, lambda g, blk: (0, 0, 0)),
                pl.BlockSpec(theirs.shape, lambda g, blk: (0, 0)),
            ],
            out_specs=[
                pl.BlockSpec((nodes, rows, 2 * rows), lambda g, blk: (0, 0, 0)),
                pl.BlockSpec((rows, 2 * rows), lambda g, blk: (0, 0)),
            ],
        ),
        out_shape=[
            jax.ShapeDtypeStruct((nodes, rows, 2 * rows), jnp.float32),
            jax.ShapeDtypeStruct((rows, 2 * rows), jnp.float32),
        ],
        compiler_params=params(),
        cost_estimate=SMALL,
        name="merge",
    )(blk.astype(jnp.int32).reshape(1), whole, theirs)


def spread_kernel(block, out):
    tall, wide = out.shape
    eigs, modes = block.shape

    def shape_of(rows, cols, dim):
        index = lax.broadcasted_iota(jnp.int32, (rows, cols), dim)
        near = lax.broadcasted_iota(jnp.int32, (rows, cols), 1 - dim)
        return (index // SUB == near).astype(jnp.bfloat16)

    wider = jnp.dot(block[...], shape_of(modes, wide, 1), preferred_element_type=jnp.float32)
    full = jnp.dot(
        shape_of(tall, eigs, 0), wider.astype(jnp.bfloat16), preferred_element_type=jnp.float32
    )
    row = lax.broadcasted_iota(jnp.int32, (tall, wide), 0) % SUB
    col = lax.broadcasted_iota(jnp.int32, (tall, wide), 1) % SUB
    out[...] = jnp.where(row == col, full, 0.0).astype(out.dtype)


def spread_blocks(block):
    eigs, modes = block.shape
    return pl.pallas_call(
        spread_kernel,
        out_shape=jax.ShapeDtypeStruct((eigs * SUB, modes * SUB), block.dtype),
        compiler_params=pltpu.CompilerParams(vmem_limit_bytes=VMEM_BYTES),
        cost_estimate=SMALL,
        name="spread_blocks",
    )(block)


def vector_kernel(at, spread, own, other, *rest):
    out, done = rest[-2:]
    done[...] = jnp.zeros_like(done)
    rows, _, cells_y, cells_z = own.shape
    both = jnp.concatenate([split_rows(own[:, 0]), split_rows(other[:, 0])], axis=0)
    made = jnp.dot(spread[...], both, preferred_element_type=jnp.float32)
    eigs = out.shape[0]
    parts = [
        made[:, i * cells_z : (i + 1) * cells_z].reshape(eigs, SUB, cells_z)
        for i in range(cells_y // SUB)
    ]
    out[:, 0] = jnp.concatenate(parts, axis=1).astype(out.dtype)


def expand(spread, own, other, at, held, *orders):
    rows, layers, cells_y, cells_z = other.shape
    eigs = spread.shape[0] // SUB
    inputs = [at.reshape(1), spread, own, other]
    specs = [
        pl.BlockSpec(spread.shape, lambda g, at: (0, 0)),
        pl.BlockSpec((rows, 1, cells_y, cells_z), lambda g, at: (0, at[0] + g, 0, 0)),
        pl.BlockSpec((rows, 1, cells_y, cells_z), lambda g, at: (0, g, 0, 0)),
    ]
    aliases = {}
    if held is not None:
        aliases = {len(inputs): 0}
        inputs.append(held)
    inputs += orders
    specs += [pl.BlockSpec(memory_space=pl.ANY)] * (len(inputs) - 1 - len(specs))
    return pl.pallas_call(
        vector_kernel,
        grid_spec=pltpu.PrefetchScalarGridSpec(
            num_scalar_prefetch=1,
            grid=(layers,),
            in_specs=specs,
            out_specs=[
                pl.BlockSpec((eigs, 1, cells_y, cells_z), lambda g, at: (0, at[0] + g, 0, 0)),
                pl.BlockSpec((SUB, cells_z), lambda g, at: (0, 0)),
            ],
        ),
        out_shape=[
            jax.ShapeDtypeStruct((eigs,) + own.shape[1:], jnp.bfloat16),
            jax.ShapeDtypeStruct((SUB, cells_z), jnp.float32),
        ],
        input_output_aliases=aliases,
        compiler_params=params(),
        cost_estimate=SMALL,
        name="expand",
    )(*inputs)


def halves(spread):
    middle = spread.shape[1] // 2
    return slice(0, middle), slice(middle, 2 * middle)


def early_kernel(spread, own, made):
    mine, _ = halves(spread)
    for layer in range(own.shape[1]):
        flat = split_rows(own[:, layer])
        made[layer] = jnp.dot(spread[:, mine], flat, preferred_element_type=jnp.float32)


def expand_early(spread, own):
    rows, layers, cells_y, cells_z = own.shape
    inside = pl.BlockSpec(memory_space=pltpu.VMEM)
    shape = (layers, spread.shape[0], cells_y // SUB * cells_z)
    return pl.pallas_call(
        early_kernel,
        in_specs=[inside, inside],
        out_specs=inside,
        out_shape=jax.ShapeDtypeStruct(shape, jnp.float32),
        compiler_params=pltpu.CompilerParams(vmem_limit_bytes=LAST_BYTES),
        cost_estimate=SMALL,
        name="expand_early",
    )(spread, own)


def last_kernel(at, spread, early, other, held, out, made, sem):
    rows, layers, cells_y, cells_z = other.shape
    _, theirs = halves(spread)
    for layer in range(layers):
        flat = split_rows(other[:, layer])
        whole = early[layer] + jnp.dot(spread[:, theirs], flat, preferred_element_type=jnp.float32)
        tiles = [
            whole[:, i * cells_z : (i + 1) * cells_z].reshape(out.shape[0], SUB, cells_z)
            for i in range(cells_y // SUB)
        ]
        made[:, layer] = jnp.concatenate(tiles, axis=1).astype(made.dtype)
    copy = pltpu.make_async_copy(made, out.at[:, pl.ds(at[0], layers)], sem)
    copy.start()
    copy.wait()


def expand_last(spread, early, other, at, held):
    rows, layers, cells_y, cells_z = other.shape
    eigs = spread.shape[0] // SUB
    inside, outside = pl.BlockSpec(memory_space=pltpu.VMEM), pl.BlockSpec(memory_space=pl.ANY)
    return pl.pallas_call(
        last_kernel,
        in_specs=[pl.BlockSpec(memory_space=pltpu.SMEM), inside, inside, inside, outside],
        out_specs=outside,
        out_shape=jax.ShapeDtypeStruct(held.shape, held.dtype),
        scratch_shapes=[
            pltpu.VMEM((eigs, layers, cells_y, cells_z), held.dtype),
            pltpu.SemaphoreType.DMA,
        ],
        input_output_aliases={4: 0},
        compiler_params=pltpu.CompilerParams(vmem_limit_bytes=LAST_BYTES),
        cost_estimate=SMALL,
        name="expand_last",
    )(at.reshape(1), spread, early, other, held)


def shares(total, parts):
    return [total // parts + (i < total % parts) for i in range(parts)]


def swap(x):
    return lax.ppermute(x, "blk", [(0, 1), (1, 0)])


def crossed(x):
    leaves, leaf = lax.axis_size("leaf"), lax.axis_index("leaf")
    places, place = lax.axis_size("dof"), lax.axis_index("dof")
    pairs = [(2 * i + j, 2 * (i ^ (leaves // 2)) + 1 - j) for i in range(leaves) for j in range(2)]
    count = x.shape[0] // (2 * places)
    part = lax.dynamic_slice_in_dim(x, (leaf % 2 * places + place) * count, count, 0)
    part = lax.ppermute(part, ("leaf", "blk"), pairs)
    step = 1
    while step < places:
        part = joined(part, "dof", step)
        step *= 2
    return joined(part, "leaf", 1)


def joined(part, axis, step):
    rest = lax.ppermute(part, axis, [(i, i ^ step) for i in range(lax.axis_size(axis))])
    first = lax.axis_index(axis) // step % 2 == 0
    return jnp.where(first, jnp.concatenate([part, rest], 0), jnp.concatenate([rest, part], 0))


def paired_sum(x, axis):
    size, step = lax.axis_size(axis), 1
    while step < size:
        x = x + lax.ppermute(x, axis, [(i, i ^ step) for i in range(size)])
        step *= 2
    return x


def line_sum(x, axis):
    if lax.axis_size(axis) != 4:
        return lax.psum(x, axis)
    x = x + lax.ppermute(x, axis, [(0, 1), (1, 0), (2, 3), (3, 2)])
    x = x + lax.ppermute(x, axis, [(1, 2), (2, 1)])
    outer = lax.ppermute(x, axis, [(1, 0), (2, 3)])
    place = lax.axis_index(axis)
    return jnp.where((place == 0) | (place == 3), outer, x)


def halved(modes, stiffness, density, eigen_blocks, parent):
    own = modes[0]
    rows, layers = own.shape[:2]
    half = layers // 2
    blk, dof, leaf = lax.axis_index("blk"), lax.axis_index("dof"), lax.axis_index("leaf")
    upper = (blk + dof) % 2

    def spot(offset, count, top):
        forward, back = half - 1 + offset, half + 1 - offset - count
        return jnp.where(top == 1, forward, back).astype(jnp.int32)

    def far_spot(offset, count, top):
        forward, back = half + 1 + offset, half - 1 - offset - count
        return jnp.where(top == 0, forward, back).astype(jnp.int32)

    def send(at, count, *orders):
        return swap(cut(own, at, count, *orders))

    last, middle, reach = half // 16, half // 8, half // 8
    fars = [half - reach - middle - last, middle, last]
    far_at = [reach - 1 + sum(fars[:i]) for i in range(len(fars))]
    nears = shares(half - reach, PARTS)
    near_at = [reach + 1 + sum(nears[:i]) for i in range(len(nears))]

    core = cut_middle(own, 2 * reach)
    met = swap(core)
    near = [send(spot(o, n, 1 - upper), n, core) for o, n in zip(near_at, nears)]
    far = [send(far_spot(far_at[0], fars[0], 1 - upper), fars[0], core)]
    size = lax.axis_size("dof")
    low = lax.ppermute(own[:, -1:], "dof", [(i, i + 1) for i in range(size - 1)])
    high = lax.ppermute(own[:, :1], "dof", [(i + 1, i) for i in range(size - 1)])
    stiff, gram, mass = stiff_terms(own, low, high, stiffness[0], density[0], met)

    mine = lax.dynamic_slice_in_dim(eigen_blocks[0], blk * rows, rows, 0)
    other = lax.dynamic_slice_in_dim(eigen_blocks[0], (1 - blk) * rows, rows, 0)
    spread = spread_blocks(jnp.concatenate([mine, other], axis=0).T)

    across = functools.partial(
        lax.dot_general,
        dimension_numbers=(((1, 2), (1, 2)), ((), ())),
        preferred_element_type=jnp.float32,
    )
    border = across(core[:, reach - 1], met[:, reach]) - across(core[:, reach], met[:, reach - 1])
    cross = jnp.where(upper == 1, 0.5 * border, -0.5 * border)
    within = upper * reach
    vectors, order = expand(spread, own, met, jnp.full_like(upper, half - reach), None, mass)
    cross = cross + cross_terms(stiff, met, half - reach + within, within, reach, order)
    for chunk, offset, count in zip(near, near_at, nears):
        at = spot(offset, count, upper)
        vectors, order = expand(spread, own, chunk, at, vectors)
        cross = cross + cross_terms(stiff, chunk, at, jnp.zeros_like(at), count, order)

    tops, masses = jnp.concatenate([gram, cross], axis=1), jnp.concatenate([mass, mass], axis=1)
    whole = line_sum(jnp.concatenate([tops, masses], axis=0), "dof")
    nodes = lax.axis_size("leaf") // 2
    belongs = (parent[leaf] == jnp.arange(nodes, dtype=jnp.int32)).astype(jnp.float32)
    whole = paired_sum(belongs[:, None, None] * whole[None], "leaf")
    theirs = crossed(jnp.concatenate([whole[p, :, rows:] for p in range(nodes)], axis=1))
    far += [send(far_spot(o, n, 1 - upper), n, whole) for o, n in zip(far_at[1:], fars[1:])]

    node_stiffness, root_stiffness = merge(whole, theirs, blk)
    places = [far_spot(o, n, upper) for o, n in zip(far_at, fars)]
    order = (root_stiffness,)
    for chunk, at in zip(far[:-1], places[:-1]):
        vectors, _ = expand(spread, own, chunk, at, vectors, *order)
        order = ()
    early = expand_early(spread, cut(own, places[-1], last, whole))
    vectors = expand_last(spread, early, far[-1], places[-1], vectors)
    return (node_stiffness, root_stiffness, vectors[None])


def extended(x, sides, width):
    for axis, dim in sides:
        size, length = (lax.axis_size(axis), x.shape[dim])
        up = [(i, (i + 1) % size) for i in range(size - 1)]
        down = [(j, i) for i, j in up]
        last = lax.slice_in_dim(x, length - width, length, axis=dim)
        leading = lax.slice_in_dim(x, 0, width, axis=dim)
        before = lax.ppermute(last, axis, up)
        after = lax.ppermute(leading, axis, down)
        x = jnp.concatenate([before, x, after], axis=dim)
    return x


def neighbours(padded):
    inner = padded[:, 1:-1]
    sides = jnp.pad(inner, ((0, 0), (0, 0), (1, 1), (1, 1)))
    total = padded[:, 2:] + padded[:, :-2]
    total = total + sides[:, :, 2:, 1:-1] + sides[:, :, :-2, 1:-1]
    total = total + sides[:, :, 1:-1, 2:] + sides[:, :, 1:-1, :-2]
    return total


def gathered(modes, stiffness, density, eigen_blocks, parent):
    own = modes[0]
    rows, cells_x, cells_y, cells_z = own.shape
    cells = cells_x * cells_y * cells_z
    total_modes = rows * lax.axis_size("blk")
    padded = extended(own, (("dof", 1),), 1).astype(jnp.float32)
    field = padded[:, 1:-1]
    stiff = ((6.0 + stiffness[0]) * field - neighbours(padded)).astype(jnp.bfloat16)
    stiff_flat = stiff.reshape(rows, cells)
    own_flat = own.reshape(rows, cells)
    mass_flat = density[0].reshape(cells)
    weighed_own = (mass_flat[None, :] * own_flat.astype(jnp.float32)).astype(jnp.bfloat16)
    diag_own = jnp.einsum("rc,rc->r", weighed_own, own_flat, preferred_element_type=jnp.float32)
    diagonal = lax.all_gather(diag_own, "blk", axis=0, tiled=True)
    blocks = eigen_blocks[0]
    eig_rows = blocks.shape[1]
    piece = lax.all_gather(own_flat, "blk", axis=0, tiled=True)
    columns = lax.dot_general(
        stiff_flat, piece, (((1,), (1,)), ((), ())), preferred_element_type=jnp.float32
    )
    reduced = columns
    vectors = lax.dot_general(
        blocks, piece, (((0,), (0,)), ((), ())), preferred_element_type=jnp.float32
    )
    reduced, vectors = (reduced, vectors)
    vector_flat = vectors.astype(jnp.bfloat16)
    leaf_vectors = vector_flat.reshape(1, eig_rows, cells_x, cells_y, cells_z)
    leaves = lax.axis_size("leaf")
    nodes = leaves // 2
    node_ids = jnp.arange(nodes, dtype=jnp.int32)
    halves = lax.axis_size("dof")
    gathered_rows, gathered_diag = (
        lax.all_gather(reduced[None], ("leaf", "dof"), axis=0, tiled=True),
        lax.all_gather(diagonal[None], ("leaf", "dof"), axis=0, tiled=True),
    )
    leaf_rows = jnp.sum(gathered_rows.reshape(leaves, halves, rows, total_modes), axis=1)
    leaf_diag = jnp.sum(gathered_diag.reshape(leaves, halves, total_modes), axis=1)
    onehot = (parent[:, None] == node_ids[None, :]).astype(jnp.float32)
    node_stiffness = jnp.einsum("lp,lij->pij", onehot, leaf_rows, precision=lax.Precision.HIGHEST)
    node_mass = jnp.einsum("lp,li->pi", onehot, leaf_diag, precision=lax.Precision.HIGHEST)
    scale = 1.0 / jnp.sqrt(node_mass)
    scale_own = lax.dynamic_slice_in_dim(scale, lax.axis_index("blk") * rows, rows, 1)
    root_stiffness = jnp.sum(scale_own[:, :, None] * node_stiffness * scale[:, None, :], axis=0)
    return (node_stiffness, root_stiffness, leaf_vectors)


def body(modes, *others):
    leaves = lax.axis_size("leaf")
    paired = leaves >= 4 and leaves & (leaves - 1) == 0
    layers, cells_y = modes.shape[2:4]
    fits = layers % 2 == 0 and layers >= 32 and cells_y % SUB == 0 and modes.shape[1] % SUB == 0
    if lax.axis_size("blk") == 2 and paired and fits:
        return halved(modes, *others)
    return gathered(modes, *others)


def solution(mesh):
    in_specs = (
        P("leaf", "blk", "dof", None, None),
        P("leaf", "dof", None, None),
        P("leaf", "dof", None, None),
        P("leaf", None, "blk"),
        P(),
    )
    out_specs = (P(None, "blk", None), P("blk", None), P("leaf", "blk", "dof", None, None))
    return jax.shard_map(body, mesh=mesh, in_specs=in_specs, out_specs=out_specs, check_vma=False)
```

```python
import functools
import jax
import jax.numpy as jnp
from jax import lax
from jax.experimental import pallas as pl
from jax.experimental.pallas import tpu as pltpu
from jax.sharding import PartitionSpec as P

SUB = 8
VMEM_BYTES = 48 * 1024 * 1024
LAST_BYTES = 16 * 1024 * 1024
PARTS = 5
SMALL = pl.CostEstimate(flops=1024, bytes_accessed=1024, transcendentals=0)


def params():
    return pltpu.CompilerParams(
        dimension_semantics=("arbitrary",), vmem_limit_bytes=VMEM_BYTES
    )


def split_rows(x):
    wide = x.astype(jnp.float32)
    rows, cells_y, cells_z = wide.shape
    parts = [
        wide[:, i * SUB : (i + 1) * SUB].reshape(rows * SUB, cells_z).astype(jnp.bfloat16)
        for i in range(cells_y // SUB)
    ]
    return jnp.concatenate(parts, axis=1)


def accumulate(total, left, right):
    total[...] += lax.dot_general(
        left, right, (((1,), (1,)), ((), ())), preferred_element_type=jnp.float32
    )


def same_row_sum(total):
    tall, wide = total.shape
    row = lax.broadcasted_iota(jnp.int32, (tall, wide), 0) % SUB
    col = lax.broadcasted_iota(jnp.int32, (tall, wide), 1) % SUB
    kept = jnp.where(row == col, total, 0.0).reshape(tall // SUB, SUB, wide)
    folded = jnp.sum(kept, axis=1)
    group = lax.broadcasted_iota(jnp.int32, (wide, wide // SUB), 0) // SUB
    pick = (group == lax.broadcasted_iota(jnp.int32, (wide, wide // SUB), 1)).astype(jnp.float32)
    return jnp.dot(folded, pick, precision=lax.Precision.HIGHEST, preferred_element_type=jnp.float32)


def stiff_kernel(own, prev, after, low, high, coefs, masses, order, stiff, gram, mass, total, flat, acc):
    layer, last = pl.program_id(0), pl.num_programs(0) - 1
    rows, _, cells_y, cells_z = own.shape

    @pl.when(layer == 0)
    def _():
        total[...] = jnp.zeros_like(total)
        acc[...] = jnp.zeros_like(acc)

    y = lax.broadcasted_iota(jnp.int32, (SUB, cells_y, cells_z), 1)
    z = lax.broadcasted_iota(jnp.int32, (SUB, cells_y, cells_z), 2)
    diagonal = 6.0 + coefs[0]
    density = masses[0]

    def group(g, carry):
        modes = pl.ds(g * SUB, SUB)
        field = own[modes, 0].astype(jnp.float32)
        before = jnp.where(layer == 0, low[modes, 0], prev[modes, 0]).astype(jnp.float32)
        behind = jnp.where(layer == last, high[modes, 0], after[modes, 0]).astype(jnp.float32)
        around = before + behind
        around += jnp.where(y == 0, 0.0, pltpu.roll(field, 1, 1))
        around += jnp.where(y == cells_y - 1, 0.0, pltpu.roll(field, cells_y - 1, 1))
        around += jnp.where(z == 0, 0.0, pltpu.roll(field, 1, 2))
        around += jnp.where(z == cells_z - 1, 0.0, pltpu.roll(field, cells_z - 1, 2))
        force = diagonal[None] * field - around
        weighed = (density[None] * field).astype(jnp.bfloat16).astype(jnp.float32) * field
        out = pl.ds(g * SUB * SUB, SUB * SUB)
        part = None
        for i in range(cells_y // SUB):
            rows_y, lanes = slice(i * SUB, (i + 1) * SUB), slice(i * cells_z, (i + 1) * cells_z)
            stiff[0, out, lanes] = force[:, rows_y].reshape(SUB * SUB, cells_z).astype(jnp.bfloat16)
            flat[out, lanes] = field[:, rows_y].reshape(SUB * SUB, cells_z).astype(jnp.bfloat16)
            part = weighed[:, rows_y] if part is None else part + weighed[:, rows_y]
        acc[modes] += part
        return carry

    lax.fori_loop(0, rows // SUB, group, 0)
    accumulate(total, stiff[0], flat[...])

    @pl.when(layer == last)
    def _():
        gram[...] = same_row_sum(total[...])
        column = jnp.sum(jnp.sum(acc[...], axis=1), axis=1, keepdims=True)
        mass[...] = jnp.broadcast_to(column, (rows, rows)).T[: mass.shape[0]]


def stiff_terms(own, low, high, coefs, masses, order):
    rows, layers, cells_y, cells_z = own.shape
    tall, wide = rows * SUB, cells_y // SUB * cells_z
    block = (rows, 1, cells_y, cells_z)
    cells = (1, cells_y, cells_z)
    return pl.pallas_call(
        stiff_kernel,
        grid=(layers,),
        in_specs=[
            pl.BlockSpec(block, lambda g: (0, g, 0, 0)),
            pl.BlockSpec(block, lambda g: (0, jnp.maximum(g - 1, 0), 0, 0)),
            pl.BlockSpec(block, lambda g: (0, jnp.minimum(g + 1, layers - 1), 0, 0)),
            pl.BlockSpec(block, lambda g: (0, 0, 0, 0)),
            pl.BlockSpec(block, lambda g: (0, 0, 0, 0)),
            pl.BlockSpec(cells, lambda g: (g, 0, 0)),
            pl.BlockSpec(cells, lambda g: (g, 0, 0)),
            pl.BlockSpec(memory_space=pl.ANY),
        ],
        out_specs=[
            pl.BlockSpec((1, tall, wide), lambda g: (g, 0, 0)),
            pl.BlockSpec((rows, rows), lambda g: (0, 0)),
            pl.BlockSpec((2 * SUB, rows), lambda g: (0, 0)),
        ],
        out_shape=[
            jax.ShapeDtypeStruct((layers, tall, wide), jnp.bfloat16),
            jax.ShapeDtypeStruct((rows, rows), jnp.float32),
            jax.ShapeDtypeStruct((2 * SUB, rows), jnp.float32),
        ],
        scratch_shapes=[
            pltpu.VMEM((tall, tall), jnp.float32),
            pltpu.VMEM((tall, wide), jnp.bfloat16),
            pltpu.VMEM((rows, SUB, cells_z), jnp.float32),
        ],
        compiler_params=params(),
        cost_estimate=SMALL,
        name="stiff_terms",
    )(own, own, own, low, high, coefs, masses, order)


def cross_kernel(at, skip, stiff, other, order, gram, total):
    step = pl.program_id(0)

    @pl.when(step == 0)
    def _():
        total[...] = jnp.zeros_like(total)

    accumulate(total, stiff[0], split_rows(other[:, 0]))

    @pl.when(step == pl.num_programs(0) - 1)
    def _():
        gram[...] = same_row_sum(total[...])


def cross_terms(stiff, other, at, skip, layers, order):
    rows, _, cells_y, cells_z = other.shape
    _, tall, wide = stiff.shape
    return pl.pallas_call(
        cross_kernel,
        grid_spec=pltpu.PrefetchScalarGridSpec(
            num_scalar_prefetch=2,
            grid=(layers,),
            in_specs=[
                pl.BlockSpec((1, tall, wide), lambda g, at, skip: (at[0] + g, 0, 0)),
                pl.BlockSpec((rows, 1, cells_y, cells_z), lambda g, at, skip: (0, skip[0] + g, 0, 0)),
                pl.BlockSpec(memory_space=pl.ANY),
            ],
            out_specs=pl.BlockSpec((rows, rows), lambda g, at, skip: (0, 0)),
            scratch_shapes=[pltpu.VMEM((tall, tall), jnp.float32)],
        ),
        out_shape=jax.ShapeDtypeStruct((rows, rows), jnp.float32),
        compiler_params=params(),
        cost_estimate=SMALL,
        name="cross_terms",
    )(at.reshape(1), skip.reshape(1), stiff, other, order)


def cut_kernel(at, whole, *rest):
    out, held, reads, writes = rest[-4:]
    pieces = held.shape[0]
    layers = out.shape[1]
    bounds = [layers * i // pieces for i in range(pieces + 1)]
    ins, outs = [], []
    for i in range(pieces):
        start, size = bounds[i], bounds[i + 1] - bounds[i]
        piece = held.at[i, :, pl.ds(0, size)]
        ins.append(
            pltpu.make_async_copy(whole.at[:, pl.ds(at[0] + start, size)], piece, reads.at[i])
        )
        outs.append(pltpu.make_async_copy(piece, out.at[:, pl.ds(start, size)], writes.at[i]))
    for copy in ins:
        copy.start()
    for i in range(pieces):
        ins[i].wait()
        outs[i].start()
    for copy in outs:
        copy.wait()


def cut(whole, at, count, *orders):
    rows, _, cells_y, cells_z = whole.shape
    pieces = min(4, count)
    longest = -(-count // pieces)
    return pl.pallas_call(
        cut_kernel,
        grid_spec=pltpu.PrefetchScalarGridSpec(
            num_scalar_prefetch=1,
            grid=(1,),
            in_specs=[pl.BlockSpec(memory_space=pl.ANY)] * (1 + len(orders)),
            out_specs=pl.BlockSpec(memory_space=pl.ANY),
            scratch_shapes=[
                pltpu.VMEM((pieces, rows, longest, cells_y, cells_z), whole.dtype),
                pltpu.SemaphoreType.DMA((pieces,)),
                pltpu.SemaphoreType.DMA((pieces,)),
            ],
        ),
        out_shape=jax.ShapeDtypeStruct((rows, count, cells_y, cells_z), whole.dtype),
        compiler_params=params(),
        cost_estimate=SMALL,
        name="cut",
    )(at.reshape(1), whole, *orders)


def cut_middle_kernel(start, whole, out, held, reads, writes):
    layers = out.shape[1]
    ins, outs = [], []
    for i in range(layers):
        piece = held.at[:, pl.ds(i, 1)]
        ins.append(pltpu.make_async_copy(whole.at[:, pl.ds(start + i, 1)], piece, reads.at[i]))
        outs.append(pltpu.make_async_copy(piece, out.at[:, pl.ds(i, 1)], writes.at[i]))
    for copy in ins:
        copy.start()
    for i in range(layers):
        ins[i].wait()
        outs[i].start()
    for copy in outs:
        copy.wait()


def cut_middle(whole, count):
    rows, layers, cells_y, cells_z = whole.shape
    shape = (rows, count, cells_y, cells_z)
    return pl.pallas_call(
        functools.partial(cut_middle_kernel, (layers - count) // 2),
        in_specs=[pl.BlockSpec(memory_space=pl.ANY)],
        out_specs=pl.BlockSpec(memory_space=pl.ANY),
        scratch_shapes=[
            pltpu.VMEM(shape, whole.dtype),
            pltpu.SemaphoreType.DMA((count,)),
            pltpu.SemaphoreType.DMA((count,)),
        ],
        out_shape=jax.ShapeDtypeStruct(shape, whole.dtype),
        compiler_params=pltpu.CompilerParams(vmem_limit_bytes=VMEM_BYTES),
        cost_estimate=SMALL,
        name="cut_middle",
    )(whole)


def merge_kernel(blk, whole, theirs, node, root):
    nodes, _, both = whole.shape
    rows = both // 2
    first = blk[0] == 0
    total = None
    for p in range(nodes):
        here = slice(p * rows, (p + 1) * rows)
        gram = whole[p, :rows, :rows]
        cross = whole[p, :rows, rows:] + theirs[:rows, here].T
        scale_gram = 1.0 / jnp.sqrt(whole[p, rows : rows + 1, :rows])
        scale_cross = 1.0 / jnp.sqrt(theirs[rows : rows + 1, here])
        scale = jnp.broadcast_to(scale_gram, (rows, rows)).T
        low, high = jnp.where(first, gram, cross), jnp.where(first, cross, gram)
        scale_low = jnp.where(first, scale_gram, scale_cross)
        scale_high = jnp.where(first, scale_cross, scale_gram)
        node[p, :, :rows] = low
        node[p, :, rows:] = high
        scaled = jnp.concatenate([scale * low * scale_low, scale * high * scale_high], axis=1)
        total = scaled if total is None else total + scaled
    root[...] = total


def merge(whole, theirs, blk):
    nodes, _, both = whole.shape
    rows = both // 2
    return pl.pallas_call(
        merge_kernel,
        grid_spec=pltpu.PrefetchScalarGridSpec(
            num_scalar_prefetch=1,
            grid=(1,),
            in_specs=[
                pl.BlockSpec(whole.shape, lambda g, blk: (0, 0, 0)),
                pl.BlockSpec(theirs.shape, lambda g, blk: (0, 0)),
            ],
            out_specs=[
                pl.BlockSpec((nodes, rows, 2 * rows), lambda g, blk: (0, 0, 0)),
                pl.BlockSpec((rows, 2 * rows), lambda g, blk: (0, 0)),
            ],
        ),
        out_shape=[
            jax.ShapeDtypeStruct((nodes, rows, 2 * rows), jnp.float32),
            jax.ShapeDtypeStruct((rows, 2 * rows), jnp.float32),
        ],
        compiler_params=params(),
        cost_estimate=SMALL,
        name="merge",
    )(blk.astype(jnp.int32).reshape(1), whole, theirs)


def spread_kernel(block, out):
    tall, wide = out.shape
    eigs, modes = block.shape

    def shape_of(rows, cols, dim):
        index = lax.broadcasted_iota(jnp.int32, (rows, cols), dim)
        near = lax.broadcasted_iota(jnp.int32, (rows, cols), 1 - dim)
        return (index // SUB == near).astype(jnp.bfloat16)

    wider = jnp.dot(block[...], shape_of(modes, wide, 1), preferred_element_type=jnp.float32)
    full = jnp.dot(
        shape_of(tall, eigs, 0), wider.astype(jnp.bfloat16), preferred_element_type=jnp.float32
    )
    row = lax.broadcasted_iota(jnp.int32, (tall, wide), 0) % SUB
    col = lax.broadcasted_iota(jnp.int32, (tall, wide), 1) % SUB
    out[...] = jnp.where(row == col, full, 0.0).astype(out.dtype)


def spread_blocks(block):
    eigs, modes = block.shape
    return pl.pallas_call(
        spread_kernel,
        out_shape=jax.ShapeDtypeStruct((eigs * SUB, modes * SUB), block.dtype),
        compiler_params=pltpu.CompilerParams(vmem_limit_bytes=VMEM_BYTES),
        cost_estimate=SMALL,
        name="spread_blocks",
    )(block)


def vector_kernel(at, spread, own, other, *rest):
    out, done = rest[-2:]
    done[...] = jnp.zeros_like(done)
    rows, _, cells_y, cells_z = own.shape
    both = jnp.concatenate([split_rows(own[:, 0]), split_rows(other[:, 0])], axis=0)
    made = jnp.dot(spread[...], both, preferred_element_type=jnp.float32)
    eigs = out.shape[0]
    parts = [
        made[:, i * cells_z : (i + 1) * cells_z].reshape(eigs, SUB, cells_z)
        for i in range(cells_y // SUB)
    ]
    out[:, 0] = jnp.concatenate(parts, axis=1).astype(out.dtype)


def expand(spread, own, other, at, held, *orders):
    rows, layers, cells_y, cells_z = other.shape
    eigs = spread.shape[0] // SUB
    inputs = [at.reshape(1), spread, own, other]
    specs = [
        pl.BlockSpec(spread.shape, lambda g, at: (0, 0)),
        pl.BlockSpec((rows, 1, cells_y, cells_z), lambda g, at: (0, at[0] + g, 0, 0)),
        pl.BlockSpec((rows, 1, cells_y, cells_z), lambda g, at: (0, g, 0, 0)),
    ]
    aliases = {}
    if held is not None:
        aliases = {len(inputs): 0}
        inputs.append(held)
    inputs += orders
    specs += [pl.BlockSpec(memory_space=pl.ANY)] * (len(inputs) - 1 - len(specs))
    return pl.pallas_call(
        vector_kernel,
        grid_spec=pltpu.PrefetchScalarGridSpec(
            num_scalar_prefetch=1,
            grid=(layers,),
            in_specs=specs,
            out_specs=[
                pl.BlockSpec((eigs, 1, cells_y, cells_z), lambda g, at: (0, at[0] + g, 0, 0)),
                pl.BlockSpec((SUB, cells_z), lambda g, at: (0, 0)),
            ],
        ),
        out_shape=[
            jax.ShapeDtypeStruct((eigs,) + own.shape[1:], jnp.bfloat16),
            jax.ShapeDtypeStruct((SUB, cells_z), jnp.float32),
        ],
        input_output_aliases=aliases,
        compiler_params=params(),
        cost_estimate=SMALL,
        name="expand",
    )(*inputs)


def halves(spread):
    middle = spread.shape[1] // 2
    return slice(0, middle), slice(middle, 2 * middle)


def early_kernel(spread, own, made):
    mine, _ = halves(spread)
    for layer in range(own.shape[1]):
        flat = split_rows(own[:, layer])
        made[layer] = jnp.dot(spread[:, mine], flat, preferred_element_type=jnp.float32)


def expand_early(spread, own):
    rows, layers, cells_y, cells_z = own.shape
    inside = pl.BlockSpec(memory_space=pltpu.VMEM)
    shape = (layers, spread.shape[0], cells_y // SUB * cells_z)
    return pl.pallas_call(
        early_kernel,
        in_specs=[inside, inside],
        out_specs=inside,
        out_shape=jax.ShapeDtypeStruct(shape, jnp.float32),
        compiler_params=pltpu.CompilerParams(vmem_limit_bytes=LAST_BYTES),
        cost_estimate=SMALL,
        name="expand_early",
    )(spread, own)


def last_kernel(at, spread, early, other, held, out, made, sem):
    rows, layers, cells_y, cells_z = other.shape
    _, theirs = halves(spread)
    for layer in range(layers):
        flat = split_rows(other[:, layer])
        whole = early[layer] + jnp.dot(spread[:, theirs], flat, preferred_element_type=jnp.float32)
        tiles = [
            whole[:, i * cells_z : (i + 1) * cells_z].reshape(out.shape[0], SUB, cells_z)
            for i in range(cells_y // SUB)
        ]
        made[:, layer] = jnp.concatenate(tiles, axis=1).astype(made.dtype)
    copy = pltpu.make_async_copy(made, out.at[:, pl.ds(at[0], layers)], sem)
    copy.start()
    copy.wait()


def expand_last(spread, early, other, at, held):
    rows, layers, cells_y, cells_z = other.shape
    eigs = spread.shape[0] // SUB
    inside, outside = pl.BlockSpec(memory_space=pltpu.VMEM), pl.BlockSpec(memory_space=pl.ANY)
    return pl.pallas_call(
        last_kernel,
        in_specs=[pl.BlockSpec(memory_space=pltpu.SMEM), inside, inside, inside, outside],
        out_specs=outside,
        out_shape=jax.ShapeDtypeStruct(held.shape, held.dtype),
        scratch_shapes=[
            pltpu.VMEM((eigs, layers, cells_y, cells_z), held.dtype),
            pltpu.SemaphoreType.DMA,
        ],
        input_output_aliases={4: 0},
        compiler_params=pltpu.CompilerParams(vmem_limit_bytes=LAST_BYTES),
        cost_estimate=SMALL,
        name="expand_last",
    )(at.reshape(1), spread, early, other, held)


def shares(total, parts):
    return [total // parts + (i < total % parts) for i in range(parts)]


def swap(x):
    return lax.ppermute(x, "blk", [(0, 1), (1, 0)])


def crossed(x):
    leaves, leaf = lax.axis_size("leaf"), lax.axis_index("leaf")
    places, place = lax.axis_size("dof"), lax.axis_index("dof")
    pairs = [(2 * i + j, 2 * (i ^ (leaves // 2)) + 1 - j) for i in range(leaves) for j in range(2)]
    count = x.shape[0] // (2 * places)
    part = lax.dynamic_slice_in_dim(x, (leaf % 2 * places + place) * count, count, 0)
    part = lax.ppermute(part, ("leaf", "blk"), pairs)
    step = 1
    while step < places:
        part = joined(part, "dof", step)
        step *= 2
    return joined(part, "leaf", 1)


def joined(part, axis, step):
    rest = lax.ppermute(part, axis, [(i, i ^ step) for i in range(lax.axis_size(axis))])
    first = lax.axis_index(axis) // step % 2 == 0
    return jnp.where(first, jnp.concatenate([part, rest], 0), jnp.concatenate([rest, part], 0))


def paired_sum(x, axis):
    size, step = lax.axis_size(axis), 1
    while step < size:
        x = x + lax.ppermute(x, axis, [(i, i ^ step) for i in range(size)])
        step *= 2
    return x


def line_sum(x, axis):
    if lax.axis_size(axis) != 4:
        return lax.psum(x, axis)
    x = x + lax.ppermute(x, axis, [(0, 1), (1, 0), (2, 3), (3, 2)])
    x = x + lax.ppermute(x, axis, [(1, 2), (2, 1)])
    outer = lax.ppermute(x, axis, [(1, 0), (2, 3)])
    place = lax.axis_index(axis)
    return jnp.where((place == 0) | (place == 3), outer, x)


def halved(modes, stiffness, density, eigen_blocks, parent):
    own = modes[0]
    rows, layers = own.shape[:2]
    half = layers // 2
    blk, dof, leaf = lax.axis_index("blk"), lax.axis_index("dof"), lax.axis_index("leaf")
    upper = (blk + dof) % 2

    def spot(offset, count, top):
        forward, back = half - 1 + offset, half + 1 - offset - count
        return jnp.where(top == 1, forward, back).astype(jnp.int32)

    def far_spot(offset, count, top):
        forward, back = half + 1 + offset, half - 1 - offset - count
        return jnp.where(top == 0, forward, back).astype(jnp.int32)

    def send(at, count, *orders):
        return swap(cut(own, at, count, *orders))

    last, middle, reach = half // 16, half // 8, half // 8
    fars = [half - reach - middle - last, middle, last]
    far_at = [reach - 1 + sum(fars[:i]) for i in range(len(fars))]
    nears = shares(half - reach, PARTS)
    near_at = [reach + 1 + sum(nears[:i]) for i in range(len(nears))]

    core = cut_middle(own, 2 * reach)
    met = swap(core)
    near = [send(spot(o, n, 1 - upper), n, core) for o, n in zip(near_at, nears)]
    far = [send(far_spot(far_at[0], fars[0], 1 - upper), fars[0], core)]
    size = lax.axis_size("dof")
    low = lax.ppermute(own[:, -1:], "dof", [(i, i + 1) for i in range(size - 1)])
    high = lax.ppermute(own[:, :1], "dof", [(i + 1, i) for i in range(size - 1)])
    stiff, gram, mass = stiff_terms(own, low, high, stiffness[0], density[0], met)

    mine = lax.dynamic_slice_in_dim(eigen_blocks[0], blk * rows, rows, 0)
    other = lax.dynamic_slice_in_dim(eigen_blocks[0], (1 - blk) * rows, rows, 0)
    spread = spread_blocks(jnp.concatenate([mine, other], axis=0).T)

    across = functools.partial(
        lax.dot_general,
        dimension_numbers=(((1, 2), (1, 2)), ((), ())),
        preferred_element_type=jnp.float32,
    )
    border = across(core[:, reach - 1], met[:, reach]) - across(core[:, reach], met[:, reach - 1])
    cross = jnp.where(upper == 1, 0.5 * border, -0.5 * border)
    within = upper * reach
    vectors, order = expand(spread, own, met, jnp.full_like(upper, half - reach), None, mass)
    cross = cross + cross_terms(stiff, met, half - reach + within, within, reach, order)
    for chunk, offset, count in zip(near, near_at, nears):
        at = spot(offset, count, upper)
        vectors, order = expand(spread, own, chunk, at, vectors)
        cross = cross + cross_terms(stiff, chunk, at, jnp.zeros_like(at), count, order)

    tops, masses = jnp.concatenate([gram, cross], axis=1), jnp.concatenate([mass, mass], axis=1)
    whole = line_sum(jnp.concatenate([tops, masses], axis=0), "dof")
    nodes = lax.axis_size("leaf") // 2
    belongs = (parent[leaf] == jnp.arange(nodes, dtype=jnp.int32)).astype(jnp.float32)
    whole = paired_sum(belongs[:, None, None] * whole[None], "leaf")
    theirs = crossed(jnp.concatenate([whole[p, :, rows:] for p in range(nodes)], axis=1))
    far += [send(far_spot(o, n, 1 - upper), n, whole) for o, n in zip(far_at[1:], fars[1:])]

    node_stiffness, root_stiffness = merge(whole, theirs, blk)
    places = [far_spot(o, n, upper) for o, n in zip(far_at, fars)]
    order = (root_stiffness,)
    for chunk, at in zip(far[:-1], places[:-1]):
        vectors, _ = expand(spread, own, chunk, at, vectors, *order)
        order = ()
    early = expand_early(spread, cut(own, places[-1], last, whole))
    vectors = expand_last(spread, early, far[-1], places[-1], vectors)
    return (node_stiffness, root_stiffness, vectors[None])


def extended(x, sides, width):
    for axis, dim in sides:
        size, length = (lax.axis_size(axis), x.shape[dim])
        up = [(i, (i + 1) % size) for i in range(size - 1)]
        down = [(j, i) for i, j in up]
        last = lax.slice_in_dim(x, length - width, length, axis=dim)
        leading = lax.slice_in_dim(x, 0, width, axis=dim)
        before = lax.ppermute(last, axis, up)
        after = lax.ppermute(leading, axis, down)
        x = jnp.concatenate([before, x, after], axis=dim)
    return x


def neighbours(padded):
    inner = padded[:, 1:-1]
    sides = jnp.pad(inner, ((0, 0), (0, 0), (1, 1), (1, 1)))
    total = padded[:, 2:] + padded[:, :-2]
    total = total + sides[:, :, 2:, 1:-1] + sides[:, :, :-2, 1:-1]
    total = total + sides[:, :, 1:-1, 2:] + sides[:, :, 1:-1, :-2]
    return total


def gathered(modes, stiffness, density, eigen_blocks, parent):
    own = modes[0]
    rows, cells_x, cells_y, cells_z = own.shape
    cells = cells_x * cells_y * cells_z
    total_modes = rows * lax.axis_size("blk")
    padded = extended(own, (("dof", 1),), 1).astype(jnp.float32)
    field = padded[:, 1:-1]
    stiff = ((6.0 + stiffness[0]) * field - neighbours(padded)).astype(jnp.bfloat16)
    stiff_flat = stiff.reshape(rows, cells)
    own_flat = own.reshape(rows, cells)
    mass_flat = density[0].reshape(cells)
    weighed_own = (mass_flat[None, :] * own_flat.astype(jnp.float32)).astype(jnp.bfloat16)
    diag_own = jnp.einsum("rc,rc->r", weighed_own, own_flat, preferred_element_type=jnp.float32)
    diagonal = lax.all_gather(diag_own, "blk", axis=0, tiled=True)
    blocks = eigen_blocks[0]
    eig_rows = blocks.shape[1]
    piece = lax.all_gather(own_flat, "blk", axis=0, tiled=True)
    columns = lax.dot_general(
        stiff_flat, piece, (((1,), (1,)), ((), ())), preferred_element_type=jnp.float32
    )
    reduced = columns
    vectors = lax.dot_general(
        blocks, piece, (((0,), (0,)), ((), ())), preferred_element_type=jnp.float32
    )
    reduced, vectors = (reduced, vectors)
    vector_flat = vectors.astype(jnp.bfloat16)
    leaf_vectors = vector_flat.reshape(1, eig_rows, cells_x, cells_y, cells_z)
    leaves = lax.axis_size("leaf")
    nodes = leaves // 2
    node_ids = jnp.arange(nodes, dtype=jnp.int32)
    halves = lax.axis_size("dof")
    gathered_rows, gathered_diag = (
        lax.all_gather(reduced[None], ("leaf", "dof"), axis=0, tiled=True),
        lax.all_gather(diagonal[None], ("leaf", "dof"), axis=0, tiled=True),
    )
    leaf_rows = jnp.sum(gathered_rows.reshape(leaves, halves, rows, total_modes), axis=1)
    leaf_diag = jnp.sum(gathered_diag.reshape(leaves, halves, total_modes), axis=1)
    onehot = (parent[:, None] == node_ids[None, :]).astype(jnp.float32)
    node_stiffness = jnp.einsum("lp,lij->pij", onehot, leaf_rows, precision=lax.Precision.HIGHEST)
    node_mass = jnp.einsum("lp,li->pi", onehot, leaf_diag, precision=lax.Precision.HIGHEST)
    scale = 1.0 / jnp.sqrt(node_mass)
    scale_own = lax.dynamic_slice_in_dim(scale, lax.axis_index("blk") * rows, rows, 1)
    root_stiffness = jnp.sum(scale_own[:, :, None] * node_stiffness * scale[:, None, :], axis=0)
    return (node_stiffness, root_stiffness, leaf_vectors)


def body(modes, *others):
    leaves = lax.axis_size("leaf")
    paired = leaves >= 4 and leaves & (leaves - 1) == 0
    layers, cells_y = modes.shape[2:4]
    fits = layers % 2 == 0 and layers >= 32 and cells_y % SUB == 0 and modes.shape[1] % SUB == 0
    if lax.axis_size("blk") == 2 and paired and fits:
        return halved(modes, *others)
    return gathered(modes, *others)


def solution(mesh):
    in_specs = (
        P("leaf", "blk", "dof", None, None),
        P("leaf", "dof", None, None),
        P("leaf", "dof", None, None),
        P("leaf", None, "blk"),
        P(),
    )
    out_specs = (P(None, "blk", None), P("blk", None), P("leaf", "blk", "dof", None, None))
    return jax.shard_map(body, mesh=mesh, in_specs=in_specs, out_specs=out_specs, check_vma=False)
```

```python
import functools
import jax
import jax.numpy as jnp
from jax import lax
from jax.experimental import pallas as pl
from jax.experimental.pallas import tpu as pltpu
from jax.sharding import PartitionSpec as P

SUB = 8
VMEM_BYTES = 48 * 1024 * 1024
LAST_BYTES = 16 * 1024 * 1024
PARTS = 4
SMALL = pl.CostEstimate(flops=1024, bytes_accessed=1024, transcendentals=0)


def params():
    return pltpu.CompilerParams(
        dimension_semantics=("arbitrary",), vmem_limit_bytes=VMEM_BYTES
    )


def split_rows(x):
    wide = x.astype(jnp.float32)
    rows, cells_y, cells_z = wide.shape
    parts = [
        wide[:, i * SUB : (i + 1) * SUB].reshape(rows * SUB, cells_z).astype(jnp.bfloat16)
        for i in range(cells_y // SUB)
    ]
    return jnp.concatenate(parts, axis=1)


def accumulate(total, left, right):
    total[...] += lax.dot_general(
        left, right, (((1,), (1,)), ((), ())), preferred_element_type=jnp.float32
    )


def same_row_sum(total):
    tall, wide = total.shape
    row = lax.broadcasted_iota(jnp.int32, (tall, wide), 0) % SUB
    col = lax.broadcasted_iota(jnp.int32, (tall, wide), 1) % SUB
    kept = jnp.where(row == col, total, 0.0).reshape(tall // SUB, SUB, wide)
    folded = jnp.sum(kept, axis=1)
    group = lax.broadcasted_iota(jnp.int32, (wide, wide // SUB), 0) // SUB
    pick = (group == lax.broadcasted_iota(jnp.int32, (wide, wide // SUB), 1)).astype(jnp.float32)
    return jnp.dot(folded, pick, precision=lax.Precision.HIGHEST, preferred_element_type=jnp.float32)


def stiff_kernel(own, prev, after, low, high, coefs, masses, order, stiff, gram, mass, total, flat, acc):
    layer, last = pl.program_id(0), pl.num_programs(0) - 1
    rows, _, cells_y, cells_z = own.shape

    @pl.when(layer == 0)
    def _():
        total[...] = jnp.zeros_like(total)
        acc[...] = jnp.zeros_like(acc)

    y = lax.broadcasted_iota(jnp.int32, (SUB, cells_y, cells_z), 1)
    z = lax.broadcasted_iota(jnp.int32, (SUB, cells_y, cells_z), 2)
    diagonal = 6.0 + coefs[0]
    density = masses[0]

    def group(g, carry):
        modes = pl.ds(g * SUB, SUB)
        field = own[modes, 0].astype(jnp.float32)
        before = jnp.where(layer == 0, low[modes, 0], prev[modes, 0]).astype(jnp.float32)
        behind = jnp.where(layer == last, high[modes, 0], after[modes, 0]).astype(jnp.float32)
        around = before + behind
        around += jnp.where(y == 0, 0.0, pltpu.roll(field, 1, 1))
        around += jnp.where(y == cells_y - 1, 0.0, pltpu.roll(field, cells_y - 1, 1))
        around += jnp.where(z == 0, 0.0, pltpu.roll(field, 1, 2))
        around += jnp.where(z == cells_z - 1, 0.0, pltpu.roll(field, cells_z - 1, 2))
        force = diagonal[None] * field - around
        weighed = (density[None] * field).astype(jnp.bfloat16).astype(jnp.float32) * field
        out = pl.ds(g * SUB * SUB, SUB * SUB)
        part = None
        for i in range(cells_y // SUB):
            rows_y, lanes = slice(i * SUB, (i + 1) * SUB), slice(i * cells_z, (i + 1) * cells_z)
            stiff[0, out, lanes] = force[:, rows_y].reshape(SUB * SUB, cells_z).astype(jnp.bfloat16)
            flat[out, lanes] = field[:, rows_y].reshape(SUB * SUB, cells_z).astype(jnp.bfloat16)
            part = weighed[:, rows_y] if part is None else part + weighed[:, rows_y]
        acc[modes] += part
        return carry

    lax.fori_loop(0, rows // SUB, group, 0)
    accumulate(total, stiff[0], flat[...])

    @pl.when(layer == last)
    def _():
        gram[...] = same_row_sum(total[...])
        column = jnp.sum(jnp.sum(acc[...], axis=1), axis=1, keepdims=True)
        mass[...] = jnp.broadcast_to(column, (rows, rows)).T[: mass.shape[0]]


def stiff_terms(own, low, high, coefs, masses, order):
    rows, layers, cells_y, cells_z = own.shape
    tall, wide = rows * SUB, cells_y // SUB * cells_z
    block = (rows, 1, cells_y, cells_z)
    cells = (1, cells_y, cells_z)
    return pl.pallas_call(
        stiff_kernel,
        grid=(layers,),
        in_specs=[
            pl.BlockSpec(block, lambda g: (0, g, 0, 0)),
            pl.BlockSpec(block, lambda g: (0, jnp.maximum(g - 1, 0), 0, 0)),
            pl.BlockSpec(block, lambda g: (0, jnp.minimum(g + 1, layers - 1), 0, 0)),
            pl.BlockSpec(block, lambda g: (0, 0, 0, 0)),
            pl.BlockSpec(block, lambda g: (0, 0, 0, 0)),
            pl.BlockSpec(cells, lambda g: (g, 0, 0)),
            pl.BlockSpec(cells, lambda g: (g, 0, 0)),
            pl.BlockSpec(memory_space=pl.ANY),
        ],
        out_specs=[
            pl.BlockSpec((1, tall, wide), lambda g: (g, 0, 0)),
            pl.BlockSpec((rows, rows), lambda g: (0, 0)),
            pl.BlockSpec((2 * SUB, rows), lambda g: (0, 0)),
        ],
        out_shape=[
            jax.ShapeDtypeStruct((layers, tall, wide), jnp.bfloat16),
            jax.ShapeDtypeStruct((rows, rows), jnp.float32),
            jax.ShapeDtypeStruct((2 * SUB, rows), jnp.float32),
        ],
        scratch_shapes=[
            pltpu.VMEM((tall, tall), jnp.float32),
            pltpu.VMEM((tall, wide), jnp.bfloat16),
            pltpu.VMEM((rows, SUB, cells_z), jnp.float32),
        ],
        compiler_params=params(),
        cost_estimate=SMALL,
        name="stiff_terms",
    )(own, own, own, low, high, coefs, masses, order)


def cross_kernel(at, skip, stiff, other, order, gram, total):
    step = pl.program_id(0)

    @pl.when(step == 0)
    def _():
        total[...] = jnp.zeros_like(total)

    accumulate(total, stiff[0], split_rows(other[:, 0]))

    @pl.when(step == pl.num_programs(0) - 1)
    def _():
        gram[...] = same_row_sum(total[...])


def cross_terms(stiff, other, at, skip, layers, order):
    rows, _, cells_y, cells_z = other.shape
    _, tall, wide = stiff.shape
    return pl.pallas_call(
        cross_kernel,
        grid_spec=pltpu.PrefetchScalarGridSpec(
            num_scalar_prefetch=2,
            grid=(layers,),
            in_specs=[
                pl.BlockSpec((1, tall, wide), lambda g, at, skip: (at[0] + g, 0, 0)),
                pl.BlockSpec((rows, 1, cells_y, cells_z), lambda g, at, skip: (0, skip[0] + g, 0, 0)),
                pl.BlockSpec(memory_space=pl.ANY),
            ],
            out_specs=pl.BlockSpec((rows, rows), lambda g, at, skip: (0, 0)),
            scratch_shapes=[pltpu.VMEM((tall, tall), jnp.float32)],
        ),
        out_shape=jax.ShapeDtypeStruct((rows, rows), jnp.float32),
        compiler_params=params(),
        cost_estimate=SMALL,
        name="cross_terms",
    )(at.reshape(1), skip.reshape(1), stiff, other, order)


def cut_kernel(at, whole, *rest):
    out, held, reads, writes = rest[-4:]
    pieces = held.shape[0]
    layers = out.shape[1]
    bounds = [layers * i // pieces for i in range(pieces + 1)]
    ins, outs = [], []
    for i in range(pieces):
        start, size = bounds[i], bounds[i + 1] - bounds[i]
        piece = held.at[i, :, pl.ds(0, size)]
        ins.append(
            pltpu.make_async_copy(whole.at[:, pl.ds(at[0] + start, size)], piece, reads.at[i])
        )
        outs.append(pltpu.make_async_copy(piece, out.at[:, pl.ds(start, size)], writes.at[i]))
    for copy in ins:
        copy.start()
    for i in range(pieces):
        ins[i].wait()
        outs[i].start()
    for copy in outs:
        copy.wait()


def cut(whole, at, count, *orders):
    rows, _, cells_y, cells_z = whole.shape
    pieces = min(4, count)
    longest = -(-count // pieces)
    return pl.pallas_call(
        cut_kernel,
        grid_spec=pltpu.PrefetchScalarGridSpec(
            num_scalar_prefetch=1,
            grid=(1,),
            in_specs=[pl.BlockSpec(memory_space=pl.ANY)] * (1 + len(orders)),
            out_specs=pl.BlockSpec(memory_space=pl.ANY),
            scratch_shapes=[
                pltpu.VMEM((pieces, rows, longest, cells_y, cells_z), whole.dtype),
                pltpu.SemaphoreType.DMA((pieces,)),
                pltpu.SemaphoreType.DMA((pieces,)),
            ],
        ),
        out_shape=jax.ShapeDtypeStruct((rows, count, cells_y, cells_z), whole.dtype),
        compiler_params=params(),
        cost_estimate=SMALL,
        name="cut",
    )(at.reshape(1), whole, *orders)


def cut_middle_kernel(start, whole, out, held, reads, writes):
    layers = out.shape[1]
    ins, outs = [], []
    for i in range(layers):
        piece = held.at[:, pl.ds(i, 1)]
        ins.append(pltpu.make_async_copy(whole.at[:, pl.ds(start + i, 1)], piece, reads.at[i]))
        outs.append(pltpu.make_async_copy(piece, out.at[:, pl.ds(i, 1)], writes.at[i]))
    for copy in ins:
        copy.start()
    for i in range(layers):
        ins[i].wait()
        outs[i].start()
    for copy in outs:
        copy.wait()


def cut_middle(whole, count):
    rows, layers, cells_y, cells_z = whole.shape
    shape = (rows, count, cells_y, cells_z)
    return pl.pallas_call(
        functools.partial(cut_middle_kernel, (layers - count) // 2),
        in_specs=[pl.BlockSpec(memory_space=pl.ANY)],
        out_specs=pl.BlockSpec(memory_space=pl.ANY),
        scratch_shapes=[
            pltpu.VMEM(shape, whole.dtype),
            pltpu.SemaphoreType.DMA((count,)),
            pltpu.SemaphoreType.DMA((count,)),
        ],
        out_shape=jax.ShapeDtypeStruct(shape, whole.dtype),
        compiler_params=pltpu.CompilerParams(vmem_limit_bytes=VMEM_BYTES),
        cost_estimate=SMALL,
        name="cut_middle",
    )(whole)


def merge_kernel(blk, whole, theirs, node, root):
    nodes, _, both = whole.shape
    rows = both // 2
    first = blk[0] == 0
    total = None
    for p in range(nodes):
        here = slice(p * rows, (p + 1) * rows)
        gram = whole[p, :rows, :rows]
        cross = whole[p, :rows, rows:] + theirs[:rows, here].T
        scale_gram = 1.0 / jnp.sqrt(whole[p, rows : rows + 1, :rows])
        scale_cross = 1.0 / jnp.sqrt(theirs[rows : rows + 1, here])
        scale = jnp.broadcast_to(scale_gram, (rows, rows)).T
        low, high = jnp.where(first, gram, cross), jnp.where(first, cross, gram)
        scale_low = jnp.where(first, scale_gram, scale_cross)
        scale_high = jnp.where(first, scale_cross, scale_gram)
        node[p, :, :rows] = low
        node[p, :, rows:] = high
        scaled = jnp.concatenate([scale * low * scale_low, scale * high * scale_high], axis=1)
        total = scaled if total is None else total + scaled
    root[...] = total


def merge(whole, theirs, blk):
    nodes, _, both = whole.shape
    rows = both // 2
    return pl.pallas_call(
        merge_kernel,
        grid_spec=pltpu.PrefetchScalarGridSpec(
            num_scalar_prefetch=1,
            grid=(1,),
            in_specs=[
                pl.BlockSpec(whole.shape, lambda g, blk: (0, 0, 0)),
                pl.BlockSpec(theirs.shape, lambda g, blk: (0, 0)),
            ],
            out_specs=[
                pl.BlockSpec((nodes, rows, 2 * rows), lambda g, blk: (0, 0, 0)),
                pl.BlockSpec((rows, 2 * rows), lambda g, blk: (0, 0)),
            ],
        ),
        out_shape=[
            jax.ShapeDtypeStruct((nodes, rows, 2 * rows), jnp.float32),
            jax.ShapeDtypeStruct((rows, 2 * rows), jnp.float32),
        ],
        compiler_params=params(),
        cost_estimate=SMALL,
        name="merge",
    )(blk.astype(jnp.int32).reshape(1), whole, theirs)


def spread_kernel(block, out):
    tall, wide = out.shape
    eigs, modes = block.shape

    def shape_of(rows, cols, dim):
        index = lax.broadcasted_iota(jnp.int32, (rows, cols), dim)
        near = lax.broadcasted_iota(jnp.int32, (rows, cols), 1 - dim)
        return (index // SUB == near).astype(jnp.bfloat16)

    wider = jnp.dot(block[...], shape_of(modes, wide, 1), preferred_element_type=jnp.float32)
    full = jnp.dot(
        shape_of(tall, eigs, 0), wider.astype(jnp.bfloat16), preferred_element_type=jnp.float32
    )
    row = lax.broadcasted_iota(jnp.int32, (tall, wide), 0) % SUB
    col = lax.broadcasted_iota(jnp.int32, (tall, wide), 1) % SUB
    out[...] = jnp.where(row == col, full, 0.0).astype(out.dtype)


def spread_blocks(block):
    eigs, modes = block.shape
    return pl.pallas_call(
        spread_kernel,
        out_shape=jax.ShapeDtypeStruct((eigs * SUB, modes * SUB), block.dtype),
        compiler_params=pltpu.CompilerParams(vmem_limit_bytes=VMEM_BYTES),
        cost_estimate=SMALL,
        name="spread_blocks",
    )(block)


def vector_kernel(at, spread, own, other, *rest):
    out, done = rest[-2:]
    done[...] = jnp.zeros_like(done)
    rows, _, cells_y, cells_z = own.shape
    both = jnp.concatenate([split_rows(own[:, 0]), split_rows(other[:, 0])], axis=0)
    made = jnp.dot(spread[...], both, preferred_element_type=jnp.float32)
    eigs = out.shape[0]
    parts = [
        made[:, i * cells_z : (i + 1) * cells_z].reshape(eigs, SUB, cells_z)
        for i in range(cells_y // SUB)
    ]
    out[:, 0] = jnp.concatenate(parts, axis=1).astype(out.dtype)


def expand(spread, own, other, at, held, *orders):
    rows, layers, cells_y, cells_z = other.shape
    eigs = spread.shape[0] // SUB
    inputs = [at.reshape(1), spread, own, other]
    specs = [
        pl.BlockSpec(spread.shape, lambda g, at: (0, 0)),
        pl.BlockSpec((rows, 1, cells_y, cells_z), lambda g, at: (0, at[0] + g, 0, 0)),
        pl.BlockSpec((rows, 1, cells_y, cells_z), lambda g, at: (0, g, 0, 0)),
    ]
    aliases = {}
    if held is not None:
        aliases = {len(inputs): 0}
        inputs.append(held)
    inputs += orders
    specs += [pl.BlockSpec(memory_space=pl.ANY)] * (len(inputs) - 1 - len(specs))
    return pl.pallas_call(
        vector_kernel,
        grid_spec=pltpu.PrefetchScalarGridSpec(
            num_scalar_prefetch=1,
            grid=(layers,),
            in_specs=specs,
            out_specs=[
                pl.BlockSpec((eigs, 1, cells_y, cells_z), lambda g, at: (0, at[0] + g, 0, 0)),
                pl.BlockSpec((SUB, cells_z), lambda g, at: (0, 0)),
            ],
        ),
        out_shape=[
            jax.ShapeDtypeStruct((eigs,) + own.shape[1:], jnp.bfloat16),
            jax.ShapeDtypeStruct((SUB, cells_z), jnp.float32),
        ],
        input_output_aliases=aliases,
        compiler_params=params(),
        cost_estimate=SMALL,
        name="expand",
    )(*inputs)


def halves(spread):
    middle = spread.shape[1] // 2
    return slice(0, middle), slice(middle, 2 * middle)


def early_kernel(spread, own, made):
    mine, _ = halves(spread)
    for layer in range(own.shape[1]):
        flat = split_rows(own[:, layer])
        made[layer] = jnp.dot(spread[:, mine], flat, preferred_element_type=jnp.float32)


def expand_early(spread, own):
    rows, layers, cells_y, cells_z = own.shape
    inside = pl.BlockSpec(memory_space=pltpu.VMEM)
    shape = (layers, spread.shape[0], cells_y // SUB * cells_z)
    return pl.pallas_call(
        early_kernel,
        in_specs=[inside, inside],
        out_specs=inside,
        out_shape=jax.ShapeDtypeStruct(shape, jnp.float32),
        compiler_params=pltpu.CompilerParams(vmem_limit_bytes=LAST_BYTES),
        cost_estimate=SMALL,
        name="expand_early",
    )(spread, own)


def last_kernel(at, spread, early, other, held, out, made, sem):
    rows, layers, cells_y, cells_z = other.shape
    _, theirs = halves(spread)
    for layer in range(layers):
        flat = split_rows(other[:, layer])
        whole = early[layer] + jnp.dot(spread[:, theirs], flat, preferred_element_type=jnp.float32)
        tiles = [
            whole[:, i * cells_z : (i + 1) * cells_z].reshape(out.shape[0], SUB, cells_z)
            for i in range(cells_y // SUB)
        ]
        made[:, layer] = jnp.concatenate(tiles, axis=1).astype(made.dtype)
    copy = pltpu.make_async_copy(made, out.at[:, pl.ds(at[0], layers)], sem)
    copy.start()
    copy.wait()


def expand_last(spread, early, other, at, held):
    rows, layers, cells_y, cells_z = other.shape
    eigs = spread.shape[0] // SUB
    inside, outside = pl.BlockSpec(memory_space=pltpu.VMEM), pl.BlockSpec(memory_space=pl.ANY)
    return pl.pallas_call(
        last_kernel,
        in_specs=[pl.BlockSpec(memory_space=pltpu.SMEM), inside, inside, inside, outside],
        out_specs=outside,
        out_shape=jax.ShapeDtypeStruct(held.shape, held.dtype),
        scratch_shapes=[
            pltpu.VMEM((eigs, layers, cells_y, cells_z), held.dtype),
            pltpu.SemaphoreType.DMA,
        ],
        input_output_aliases={4: 0},
        compiler_params=pltpu.CompilerParams(vmem_limit_bytes=LAST_BYTES),
        cost_estimate=SMALL,
        name="expand_last",
    )(at.reshape(1), spread, early, other, held)


def shares(total, parts):
    return [total // parts + (i < total % parts) for i in range(parts)]


def swap(x):
    return lax.ppermute(x, "blk", [(0, 1), (1, 0)])


def crossed(x):
    leaves, leaf = lax.axis_size("leaf"), lax.axis_index("leaf")
    places, place = lax.axis_size("dof"), lax.axis_index("dof")
    pairs = [(2 * i + j, 2 * (i ^ (leaves // 2)) + 1 - j) for i in range(leaves) for j in range(2)]
    count = x.shape[0] // (2 * places)
    part = lax.dynamic_slice_in_dim(x, (leaf % 2 * places + place) * count, count, 0)
    part = lax.ppermute(part, ("leaf", "blk"), pairs)
    step = 1
    while step < places:
        part = joined(part, "dof", step)
        step *= 2
    return joined(part, "leaf", 1)


def joined(part, axis, step):
    rest = lax.ppermute(part, axis, [(i, i ^ step) for i in range(lax.axis_size(axis))])
    first = lax.axis_index(axis) // step % 2 == 0
    return jnp.where(first, jnp.concatenate([part, rest], 0), jnp.concatenate([rest, part], 0))


def paired_sum(x, axis):
    size, step = lax.axis_size(axis), 1
    while step < size:
        x = x + lax.ppermute(x, axis, [(i, i ^ step) for i in range(size)])
        step *= 2
    return x


def line_sum(x, axis):
    if lax.axis_size(axis) != 4:
        return lax.psum(x, axis)
    x = x + lax.ppermute(x, axis, [(0, 1), (1, 0), (2, 3), (3, 2)])
    x = x + lax.ppermute(x, axis, [(1, 2), (2, 1)])
    outer = lax.ppermute(x, axis, [(1, 0), (2, 3)])
    place = lax.axis_index(axis)
    return jnp.where((place == 0) | (place == 3), outer, x)


def halved(modes, stiffness, density, eigen_blocks, parent):
    own = modes[0]
    rows, layers = own.shape[:2]
    half = layers // 2
    blk, dof, leaf = lax.axis_index("blk"), lax.axis_index("dof"), lax.axis_index("leaf")
    upper = (blk + dof) % 2

    def spot(offset, count, top):
        forward, back = half - 1 + offset, half + 1 - offset - count
        return jnp.where(top == 1, forward, back).astype(jnp.int32)

    def far_spot(offset, count, top):
        forward, back = half + 1 + offset, half - 1 - offset - count
        return jnp.where(top == 0, forward, back).astype(jnp.int32)

    def send(at, count, *orders):
        return swap(cut(own, at, count, *orders))

    last, middle, reach = half // 16, half // 8, half // 8
    fars = [half - reach - middle - last, middle, last]
    far_at = [reach - 1 + sum(fars[:i]) for i in range(len(fars))]
    nears = shares(half - reach, PARTS)
    near_at = [reach + 1 + sum(nears[:i]) for i in range(len(nears))]

    core = cut_middle(own, 2 * reach)
    met = swap(core)
    near = [send(spot(o, n, 1 - upper), n, core) for o, n in zip(near_at, nears)]
    far = [send(far_spot(far_at[0], fars[0], 1 - upper), fars[0], core)]
    size = lax.axis_size("dof")
    low = lax.ppermute(own[:, -1:], "dof", [(i, i + 1) for i in range(size - 1)])
    high = lax.ppermute(own[:, :1], "dof", [(i + 1, i) for i in range(size - 1)])
    stiff, gram, mass = stiff_terms(own, low, high, stiffness[0], density[0], met)

    mine = lax.dynamic_slice_in_dim(eigen_blocks[0], blk * rows, rows, 0)
    other = lax.dynamic_slice_in_dim(eigen_blocks[0], (1 - blk) * rows, rows, 0)
    spread = spread_blocks(jnp.concatenate([mine, other], axis=0).T)

    across = functools.partial(
        lax.dot_general,
        dimension_numbers=(((1, 2), (1, 2)), ((), ())),
        preferred_element_type=jnp.float32,
    )
    border = across(core[:, reach - 1], met[:, reach]) - across(core[:, reach], met[:, reach - 1])
    cross = jnp.where(upper == 1, 0.5 * border, -0.5 * border)
    within = upper * reach
    vectors, order = expand(spread, own, met, jnp.full_like(upper, half - reach), None, mass)
    cross = cross + cross_terms(stiff, met, half - reach + within, within, reach, order)
    for chunk, offset, count in zip(near, near_at, nears):
        at = spot(offset, count, upper)
        vectors, order = expand(spread, own, chunk, at, vectors)
        cross = cross + cross_terms(stiff, chunk, at, jnp.zeros_like(at), count, order)

    tops, masses = jnp.concatenate([gram, cross], axis=1), jnp.concatenate([mass, mass], axis=1)
    whole = line_sum(jnp.concatenate([tops, masses], axis=0), "dof")
    nodes = lax.axis_size("leaf") // 2
    belongs = (parent[leaf] == jnp.arange(nodes, dtype=jnp.int32)).astype(jnp.float32)
    whole = paired_sum(belongs[:, None, None] * whole[None], "leaf")
    theirs = crossed(jnp.concatenate([whole[p, :, rows:] for p in range(nodes)], axis=1))
    far += [send(far_spot(o, n, 1 - upper), n, whole) for o, n in zip(far_at[1:], fars[1:])]

    node_stiffness, root_stiffness = merge(whole, theirs, blk)
    places = [far_spot(o, n, upper) for o, n in zip(far_at, fars)]
    order = (root_stiffness,)
    for chunk, at in zip(far[:-1], places[:-1]):
        vectors, _ = expand(spread, own, chunk, at, vectors, *order)
        order = ()
    early = expand_early(spread, cut(own, places[-1], last, whole))
    vectors = expand_last(spread, early, far[-1], places[-1], vectors)
    return (node_stiffness, root_stiffness, vectors[None])


def extended(x, sides, width):
    for axis, dim in sides:
        size, length = (lax.axis_size(axis), x.shape[dim])
        up = [(i, (i + 1) % size) for i in range(size - 1)]
        down = [(j, i) for i, j in up]
        last = lax.slice_in_dim(x, length - width, length, axis=dim)
        leading = lax.slice_in_dim(x, 0, width, axis=dim)
        before = lax.ppermute(last, axis, up)
        after = lax.ppermute(leading, axis, down)
        x = jnp.concatenate([before, x, after], axis=dim)
    return x


def neighbours(padded):
    inner = padded[:, 1:-1]
    sides = jnp.pad(inner, ((0, 0), (0, 0), (1, 1), (1, 1)))
    total = padded[:, 2:] + padded[:, :-2]
    total = total + sides[:, :, 2:, 1:-1] + sides[:, :, :-2, 1:-1]
    total = total + sides[:, :, 1:-1, 2:] + sides[:, :, 1:-1, :-2]
    return total


def gathered(modes, stiffness, density, eigen_blocks, parent):
    own = modes[0]
    rows, cells_x, cells_y, cells_z = own.shape
    cells = cells_x * cells_y * cells_z
    total_modes = rows * lax.axis_size("blk")
    padded = extended(own, (("dof", 1),), 1).astype(jnp.float32)
    field = padded[:, 1:-1]
    stiff = ((6.0 + stiffness[0]) * field - neighbours(padded)).astype(jnp.bfloat16)
    stiff_flat = stiff.reshape(rows, cells)
    own_flat = own.reshape(rows, cells)
    mass_flat = density[0].reshape(cells)
    weighed_own = (mass_flat[None, :] * own_flat.astype(jnp.float32)).astype(jnp.bfloat16)
    diag_own = jnp.einsum("rc,rc->r", weighed_own, own_flat, preferred_element_type=jnp.float32)
    diagonal = lax.all_gather(diag_own, "blk", axis=0, tiled=True)
    blocks = eigen_blocks[0]
    eig_rows = blocks.shape[1]
    piece = lax.all_gather(own_flat, "blk", axis=0, tiled=True)
    columns = lax.dot_general(
        stiff_flat, piece, (((1,), (1,)), ((), ())), preferred_element_type=jnp.float32
    )
    reduced = columns
    vectors = lax.dot_general(
        blocks, piece, (((0,), (0,)), ((), ())), preferred_element_type=jnp.float32
    )
    reduced, vectors = (reduced, vectors)
    vector_flat = vectors.astype(jnp.bfloat16)
    leaf_vectors = vector_flat.reshape(1, eig_rows, cells_x, cells_y, cells_z)
    leaves = lax.axis_size("leaf")
    nodes = leaves // 2
    node_ids = jnp.arange(nodes, dtype=jnp.int32)
    halves = lax.axis_size("dof")
    gathered_rows, gathered_diag = (
        lax.all_gather(reduced[None], ("leaf", "dof"), axis=0, tiled=True),
        lax.all_gather(diagonal[None], ("leaf", "dof"), axis=0, tiled=True),
    )
    leaf_rows = jnp.sum(gathered_rows.reshape(leaves, halves, rows, total_modes), axis=1)
    leaf_diag = jnp.sum(gathered_diag.reshape(leaves, halves, total_modes), axis=1)
    onehot = (parent[:, None] == node_ids[None, :]).astype(jnp.float32)
    node_stiffness = jnp.einsum("lp,lij->pij", onehot, leaf_rows, precision=lax.Precision.HIGHEST)
    node_mass = jnp.einsum("lp,li->pi", onehot, leaf_diag, precision=lax.Precision.HIGHEST)
    scale = 1.0 / jnp.sqrt(node_mass)
    scale_own = lax.dynamic_slice_in_dim(scale, lax.axis_index("blk") * rows, rows, 1)
    root_stiffness = jnp.sum(scale_own[:, :, None] * node_stiffness * scale[:, None, :], axis=0)
    return (node_stiffness, root_stiffness, leaf_vectors)


def body(modes, *others):
    leaves = lax.axis_size("leaf")
    paired = leaves >= 4 and leaves & (leaves - 1) == 0
    layers, cells_y = modes.shape[2:4]
    fits = layers % 2 == 0 and layers >= 32 and cells_y % SUB == 0 and modes.shape[1] % SUB == 0
    if lax.axis_size("blk") == 2 and paired and fits:
        return halved(modes, *others)
    return gathered(modes, *others)


def solution(mesh):
    in_specs = (
        P("leaf", "blk", "dof", None, None),
        P("leaf", "dof", None, None),
        P("leaf", "dof", None, None),
        P("leaf", None, "blk"),
        P(),
    )
    out_specs = (P(None, "blk", None), P("blk", None), P("leaf", "blk", "dof", None, None))
    return jax.shard_map(body, mesh=mesh, in_specs=in_specs, out_specs=out_specs, check_vma=False)
```
